32 devices in a mesh: ctx: 8 (over y, x, core), tp: 4 (over z).
Axes of the slice: x: 2, y: 2, z: 4, core: 2. Of those that a mesh axis runs over, the one named last changes fastest.
Arguments:
- hyena_inputs: bfloat16 [3, 1024, 4096], P(None, 'ctx', 'tp'), may hold values from -6 to 6
- filters: float32 [128, 4096], P('tp'), may hold values from -1.25 to 1.25
- skip_bias: float32 [4096], P('tp'), may hold values from -4 to 4
- queries: bfloat16 [1024, 4096], P('ctx', 'tp'), may hold values from -8 to 8
- keys_values: bfloat16 [2, 1024, 4096], P(None, 'ctx', 'tp'), may hold values from -8 to 8
- doc_start: int32 [1024], P('ctx'), may hold values from 0 to 1023, as said below
Outputs:
- hyena_out: bfloat16 [1024, 4096], P('ctx', 'tp')
- attention_out: bfloat16 [1024, 4096], P('ctx', 'tp')
- log_totals: float32 [32, 1024], P('tp', 'ctx')
The draws below stay inside these ranges and needn't reach their ends.
Inputs may be any that keep to these rules, and one draw needn't show every extreme that they name: doc_start[t] <= t; doc_start is non-decreasing, equal within a document and equal to t at a document's first base; no document is longer than 896 bases and one has exactly 896; the last base forms a document of its own.
All inputs are finite; a program needn't handle non-finite values.
Results may differ from the reference program's by a relative error of at most 0.009.
Values may be sent and summed in bfloat16 or wider, within the bound.
No kernel may reach another device: no remote copies, remote signals or barrier semaphores. Data moves between devices by JAX's collectives and lax.ppermute only.
A program may use at most 128 MiB of HBM per device.

```python
import math
import jax
import jax.numpy as jnp
from jax import lax

C = 4096
AH = 32
HD = 128
FLEN = 128
TOK_DEV = 128
HOPS = 7
DOC_MAX = 896
TOKENS = 1024


def draw_queries(key, part):
    key = jax.random.fold_in(key, 11)
    drawn = jnp.clip(jax.random.normal(key, (TOKENS, AH * HD), jnp.float32), -6.0, 6.0)
    return drawn.astype(jnp.bfloat16)


def draw_keys_values(key, part):
    key = jax.random.fold_in(key, 13)
    first_key, second_key = jax.random.split(key)
    key_rows = jnp.clip(jax.random.normal(first_key, (TOKENS, AH * HD), jnp.float32), -6.0, 6.0)
    value_rows = jnp.clip(jax.random.normal(second_key, (TOKENS, AH * HD), jnp.float32), -6.0, 6.0)
    return jnp.stack([key_rows, value_rows]).astype(jnp.bfloat16)


def draw_doc_start(key, part):
    key = jax.random.fold_in(key, 17)
    keys = jax.random.split(key, 4)
    places = jnp.arange(TOKENS, dtype=jnp.int32)
    block_count = TOKENS // TOK_DEV
    region_block = jax.random.randint(keys[0], (), 0, block_count - HOPS, dtype=jnp.int32)
    region_offset = jax.random.randint(keys[1], (), TOK_DEV // 4, 3 * TOK_DEV // 4 + 1, dtype=jnp.int32)
    region_start = region_block * TOK_DEV + region_offset
    region_end = region_start + DOC_MAX

    def chain_starts(subkey, anchor):
        lengths = jax.random.randint(subkey, (TOKENS,), 1, DOC_MAX + 1, dtype=jnp.int32)
        starts = jnp.cumsum(lengths).astype(jnp.int32) - lengths
        relative = jnp.maximum(places - anchor, 0)
        which = jnp.searchsorted(starts, relative, side='right').astype(jnp.int32) - 1
        return anchor + starts[which]
    earlier = chain_starts(keys[2], jnp.int32(0))
    later = chain_starts(keys[3], region_end)
    result = jnp.where(places < region_start, earlier, jnp.where(places < region_end, region_start, later))
    result = jnp.where(places == TOKENS - 1, places, result)
    return result.astype(jnp.int32)


def block_scale(key, extent, cuts, least, largest):
    factor_of, own = 1.0, jax.random.fold_in(key, 6)
    for position, shards_of in cuts:
        heights = jnp.exp(jax.random.uniform(jax.random.fold_in(own, position), (shards_of,), jnp.float32, least / len(cuts), largest / len(cuts)))
        factor_of = factor_of * jnp.repeat(heights, extent[position] // shards_of).reshape([-1 if axis == position else 1 for axis in range(len(extent))])
    return factor_of


def noise(key, shape, spread, limit, pieces=(), held_as=jnp.bfloat16):
    array = spread * jax.random.normal(key, shape, jnp.float32)
    if pieces:
        array = array * block_scale(key, shape, pieces, -0.22, 0.18)
    return jnp.clip(array, -limit, limit).astype(held_as)


def setup_inputs(seed: int = 0) -> dict:
    key_list = jax.random.split(jax.random.key(seed), 7)
    return {
        "hyena_inputs": noise(key_list[0], (3, TOKENS, C), 1.0, 6.0, ((1, 8), (2, 4))),
        "filters": noise(key_list[1], (FLEN, C), 0.088, 1.25, ((0, 4),), jnp.float32),
        "skip_bias": noise(key_list[2], (C,), 1.0, 4.0, ((0, 4),), jnp.float32),
        "queries": draw_queries(jax.random.fold_in(key_list[6], 71), 0),
        "keys_values": draw_keys_values(jax.random.fold_in(key_list[6], 71), 0),
        "doc_start": draw_doc_start(jax.random.fold_in(key_list[6], 71), 0),
    }


def reference(hyena_inputs, filters, skip_bias, queries, keys_values, doc_start):
    hyena_query = hyena_inputs[0].astype(jnp.float32)
    kv_product = (hyena_inputs[1].astype(jnp.float32) * hyena_inputs[2].astype(jnp.float32)).astype(jnp.bfloat16)
    kv_product = lax.optimization_barrier(kv_product)
    product = kv_product.astype(jnp.float32)
    block_count = TOKENS // TOK_DEV
    padded = jnp.concatenate([jnp.zeros((FLEN - 1, C), jnp.float32), product], axis=0)

    def convolve_block(block_index):
        begin_row = (block_index * TOK_DEV).astype(jnp.int32)
        window = lax.dynamic_slice_in_dim(padded, begin_row, TOK_DEV + FLEN - 1, 0)
        places = begin_row + jnp.arange(TOK_DEV, dtype=jnp.int32)
        starts = lax.dynamic_slice_in_dim(doc_start, begin_row, TOK_DEV, 0)

        def add_tap(tap_index, running):
            shifted = lax.dynamic_slice_in_dim(window, (FLEN - 1 - tap_index).astype(jnp.int32), TOK_DEV, 0)
            weight = lax.dynamic_slice_in_dim(filters, tap_index, 1, 0)
            allowed = (places - tap_index >= starts)[:, None]
            return running + jnp.where(allowed, shifted * weight, 0.0)
        return lax.fori_loop(jnp.int32(0), jnp.int32(FLEN), add_tap, jnp.zeros((TOK_DEV, C), jnp.float32))
    convolved = lax.map(convolve_block, jnp.arange(block_count, dtype=jnp.int32)).reshape(TOKENS, C)
    hyena_out = (hyena_query * (skip_bias[None, :] * product + convolved)).astype(jnp.bfloat16)
    query_heads = queries.astype(jnp.float32).reshape(TOKENS, AH, HD)
    key_heads = keys_values[0].astype(jnp.float32).reshape(TOKENS, AH, HD)
    value_heads = keys_values[1].astype(jnp.float32).reshape(TOKENS, AH, HD)
    reach_rows = HOPS * TOK_DEV
    key_padded = jnp.concatenate([jnp.zeros((reach_rows, AH, HD), jnp.float32), key_heads], axis=0)
    value_padded = jnp.concatenate([jnp.zeros((reach_rows, AH, HD), jnp.float32), value_heads], axis=0)
    score_scale = 1.0 / math.sqrt(HD)

    def attend(block_index):
        begin_row = (block_index * TOK_DEV).astype(jnp.int32)
        query_rows = lax.dynamic_slice_in_dim(query_heads, begin_row, TOK_DEV, 0)
        key_rows = lax.dynamic_slice_in_dim(key_padded, begin_row, reach_rows + TOK_DEV, 0)
        value_rows = lax.dynamic_slice_in_dim(value_padded, begin_row, reach_rows + TOK_DEV, 0)
        places = begin_row + jnp.arange(TOK_DEV, dtype=jnp.int32)
        key_places = begin_row - reach_rows + jnp.arange(reach_rows + TOK_DEV, dtype=jnp.int32)
        starts = lax.dynamic_slice_in_dim(doc_start, begin_row, TOK_DEV, 0)
        allowed = (key_places[None, :] >= starts[:, None]) & (key_places[None, :] <= places[:, None])
        scores = jnp.einsum('thd,khd->htk', query_rows, key_rows) * score_scale
        scores = jnp.where(allowed[None], scores, -jnp.inf)
        row_top = lax.optimization_barrier(jnp.max(scores, axis=2))
        weights = jnp.exp(scores - row_top[:, :, None])
        denominator = lax.optimization_barrier(jnp.sum(weights, axis=2))
        rounded = lax.optimization_barrier(weights.astype(jnp.bfloat16)).astype(jnp.float32)
        mixed = jnp.einsum('htk,khd->thd', rounded, value_rows) / denominator.T[:, :, None]
        return (mixed.astype(jnp.bfloat16), row_top + jnp.log(denominator))
    outputs, totals = lax.map(attend, jnp.arange(block_count, dtype=jnp.int32))
    attention_out = outputs.reshape(TOKENS, AH * HD)
    log_totals = totals.transpose(1, 0, 2).reshape(AH, TOKENS)
    return (hyena_out, attention_out, log_totals)
```

```python
import functools
import math

import jax
import jax.numpy as jnp
import numpy as np
from jax import lax
from jax.experimental import pallas as pl
from jax.experimental.pallas import tpu as pltpu
from jax.sharding import PartitionSpec as P

HD = 128
FLEN = 128
DIGIT = 256
NOTE_ROWS = 16
MASKED = -1e30
VMEM_LIMIT = 16 * 1024 * 1024


def vmem():
    return pl.BlockSpec(memory_space=pltpu.VMEM)


def hbm():
    return pl.BlockSpec(memory_space=pltpu.HBM)


def call(kernel, out_shape, args, flops, nbytes, scratch=(), specs=None):
    return pl.pallas_call(
        kernel,
        out_shape=out_shape,
        in_specs=specs or [vmem() for _ in args],
        out_specs=jax.tree.map(lambda _: vmem(), out_shape),
        scratch_shapes=list(scratch),
        compiler_params=pltpu.CompilerParams(vmem_limit_bytes=VMEM_LIMIT),
        cost_estimate=pl.CostEstimate(flops=flops, bytes_accessed=nbytes, transcendentals=0),
    )(*args)


def crossed(array, axis, bits):
    return lax.ppermute(array, axis, [(i, i ^ bits) for i in range(lax.axis_size(axis))])


def place(heads):
    index = lax.axis_index("ctx")
    member = lax.rem(index, heads)
    return index // heads, member // 2, lax.rem(member, 2)


def pack_heads(heads, extra, queries_ref, keys_values_ref, starts_ref, *refs):
    extras, refs = refs[:extra], refs[extra:]
    *outs, held_ref, start_sem, extra_sem, sem = refs
    outs, brought = outs[:-extra], outs[-extra:]
    rows = queries_ref.shape[0]
    _, pair, _ = place(heads)
    first = pltpu.make_async_copy(starts_ref, held_ref, start_sem)
    first.start()
    copies = []
    for step, out in enumerate(outs):
        columns = pl.ds(pl.multiple_of((pair ^ step) * (2 * HD), 2 * HD), 2 * HD)
        for part, source in enumerate(
            (queries_ref, keys_values_ref.at[0], keys_values_ref.at[1])
        ):
            copies.append(
                pltpu.make_async_copy(
                    source.at[:, columns], out.at[pl.ds(part * rows, rows)], sem.at[step, part]
                )
            )
    for index, (source, out) in enumerate(zip(extras, brought)):
        copies.append(pltpu.make_async_copy(source, out, extra_sem.at[index]))
    for copy in copies:
        copy.start()
    first.wait()
    starts = held_ref[...]
    high = (starts // DIGIT).astype(jnp.float32)
    low = (starts % DIGIT).astype(jnp.float32)
    line = lax.broadcasted_iota(jnp.int32, (NOTE_ROWS, rows), 0)
    note = jnp.where(line == 0, high, jnp.where(line == 1, low, 0.0)).astype(jnp.bfloat16)
    for out in outs:
        out[3 * rows :, :HD] = note
        out[3 * rows :, HD:] = note
    for copy in copies:
        copy.wait()


def split(matrix):
    high = matrix.astype(jnp.bfloat16)
    low = (matrix - high.astype(jnp.float32)).astype(jnp.bfloat16)
    return jnp.concatenate([high, low], axis=1)


def pack_hyena(
    hyena_ref, filters_ref, ahead_ref, wide_back_ref,
    product_ref, own_ref, far_ref, near_ref, early_ref, late_ref, back_ref,
):
    product_ref[...] = (hyena_ref[1].astype(jnp.float32) * hyena_ref[2].astype(jnp.float32)).astype(
        jnp.bfloat16
    )
    width = own_ref.shape[1]
    panel = lax.axis_index("tp")
    parity = lax.rem(lax.axis_index("ctx"), 2)

    def taps(target):
        columns = pl.ds(pl.multiple_of(target * width, width), width)
        return filters_ref[:, columns].astype(jnp.bfloat16)

    own_ref[...] = taps(panel)
    far_ref[...] = taps(panel ^ (2 + parity))
    near_ref[...] = taps(panel ^ 1)
    rows = product_ref.shape[0]
    early_ref[...] = split(ahead_ref[:, :rows])
    late_ref[...] = split(ahead_ref[:, rows:])
    back_ref[...] = wide_back_ref[...].astype(jnp.bfloat16)


def columns_of(ref, rows, index):
    return ref[rows, index * 2 * HD : (index + 1) * 2 * HD]


def sort_heads(heads, *refs):
    count = heads // 2
    far_ref, near_ref, product_ref, query_ref, side_ref = refs[-5:]
    rows = (refs[0].shape[0] - NOTE_ROWS) // 3
    _, pair, _ = place(heads)
    for step in range(count):
        source = pair ^ step
        query_ref[source, :rows] = refs[step][:rows]
        query_ref[source, rows:] = refs[step][3 * rows :]
        side_ref[2 * source] = refs[step][rows : 2 * rows]
        side_ref[2 * source + 1] = refs[step][2 * rows : 3 * rows]
    height, width = far_ref.shape
    parts = width // (2 * HD)
    for part in range(parts):
        line = slice(part * height, (part + 1) * height)
        side_ref[heads, line] = columns_of(far_ref, slice(None), part)
        side_ref[heads + 1, line] = columns_of(near_ref, slice(None), part)
        side_ref[heads + 2 + part] = columns_of(product_ref, slice(None), part)


UNIT = 2


def key_set(ref, blocks, head, origin, parity, own):
    columns = slice(head * HD, (head + 1) * HD)
    rows = ref.shape[1]
    key = jnp.concatenate([ref[2 * block, :, columns] for block in range(blocks)], axis=0)
    value = jnp.concatenate([ref[2 * block + 1, :, columns] for block in range(blocks)], axis=0)
    firsts = [((2 * block + parity) * rows + origin, block >= own) for block in range(blocks)]
    return key, value, firsts


def masked_scores(sets, query, start, own):
    blocks = []
    for key, _, firsts in sets:
        scores = lax.dot_general(
            key, query, (((1,), (1,)), ((), ())), preferred_element_type=jnp.float32
        )
        rows = key.shape[0] // len(firsts)
        line = lax.broadcasted_iota(jnp.int32, (rows, query.shape[0]), 0)
        for index, (first, causal) in enumerate(firsts):
            allowed = line >= start - first
            if causal:
                allowed &= line <= own - first
            blocks.append(jnp.where(allowed, scores[index * rows : (index + 1) * rows], MASKED))
    return blocks


def highest(blocks):
    return jnp.max(functools.reduce(jnp.maximum, blocks), axis=0, keepdims=True)


def weigh(sets, blocks, top):
    weights = [jnp.exp2((block - top) * FACTOR) for block in blocks]
    total = jnp.sum(functools.reduce(jnp.add, weights), axis=0, keepdims=True)
    value = jnp.concatenate([one[1] for one in sets], axis=0)
    rounded = jnp.concatenate([each.astype(jnp.bfloat16) for each in weights], axis=0)
    return total, dot(value.T, rounded)


def unit_rows(heads, query_ref, head, begin):
    rows = query_ref.shape[1] - NOTE_ROWS
    group, _, parity = place(heads)
    query = query_ref[begin : begin + UNIT, :rows, head * HD : (head + 1) * HD]
    starts = []
    for block in range(begin, begin + UNIT):
        note = query_ref[block, rows:, :HD].astype(jnp.float32)
        starts.append(note[0:1] * float(DIGIT) + note[1:2])
    start = jnp.concatenate(starts, axis=1).astype(jnp.int32) - group * (heads * rows)
    line = lax.broadcasted_iota(jnp.int32, (1, UNIT * rows), 1)
    own = line // rows * rows + line + (2 * begin + parity) * rows
    return query.reshape(UNIT * rows, HD), start, own


FACTOR = math.log2(math.e) / math.sqrt(HD)


def attend_first(heads, query_ref, key_value_ref, top_ref, total_ref, mixed_ref):
    rows = query_ref.shape[1] - NOTE_ROWS
    _, _, parity = place(heads)
    for head in range(2):
        for unit in range(heads // 2 // UNIT):
            begin = unit * UNIT
            query, start, own = unit_rows(heads, query_ref, head, begin)
            sets = [key_set(key_value_ref, begin + UNIT, head, 0, parity, begin)]
            blocks = masked_scores(sets, query, start, own)
            top = highest(blocks)
            top_ref[head, unit] = top
            total_ref[head, unit], mixed_ref[head, unit] = weigh(sets, blocks, top)


def attend_second(heads, *refs):
    count = heads // 2
    query_ref, top_ref, total_ref, mixed_ref, other_ref, *more = refs[: -count - 1]
    outs, held_ref = refs[-count - 1 : -1], refs[-1]
    rows = query_ref.shape[1] - NOTE_ROWS
    _, pair, parity = place(heads)
    for head in range(2):
        columns = slice(head * HD, (head + 1) * HD)
        for unit in range(count // UNIT):
            begin = unit * UNIT
            query, start, own = unit_rows(heads, query_ref, head, begin)
            sets = [key_set(other_ref, begin + UNIT, head, 0, 1 - parity, begin)]
            for ref, side in zip(more, (parity, 1 - parity)):
                sets.append(key_set(ref, count, head, -heads * rows, side, count))
            blocks = masked_scores(sets, query, start, own)
            before = top_ref[head, unit]
            top = jnp.maximum(before, highest(blocks))
            scale = jnp.exp2((before - top) * FACTOR)
            total, mixed = weigh(sets, blocks, top)
            total = total_ref[head, unit] * scale + total
            mixed = mixed_ref[head, unit] * scale + mixed
            mixed = (mixed / total).T.astype(jnp.bfloat16)
            logs = top * (1.0 / math.sqrt(HD)) + jnp.log(total)
            high = logs.astype(jnp.bfloat16).astype(jnp.float32)
            middle = (logs - high).astype(jnp.bfloat16).astype(jnp.float32)
            low = logs - high - middle
            line = lax.broadcasted_iota(jnp.int32, (NOTE_ROWS, UNIT * rows), 0)
            note = jnp.where(
                line == 0, high, jnp.where(line == 1, middle, jnp.where(line == 2, low, 0.0))
            ).astype(jnp.bfloat16)
            for index in range(UNIT):
                span = slice(index * rows, (index + 1) * rows)
                held_ref[begin + index, :rows, columns] = mixed[span]
                held_ref[begin + index, rows:, columns] = note[:, span]
    for step, out in enumerate(outs):
        out[...] = held_ref[pair ^ step]


def unpack_heads(heads, *refs):
    *sources, out_ref, logs_ref = refs
    rows = out_ref.shape[0]
    _, pair, _ = place(heads)
    for step, source in enumerate(sources):
        owner = pair ^ step
        out_ref[:, pl.ds(pl.multiple_of(owner * (2 * HD), 2 * HD), 2 * HD)] = source[:rows]
        note = source[rows:].astype(jnp.float32)
        logs = note[0:1] + note[1:2] + note[2:3]
        for head in range(2):
            logs_ref[pl.ds(owner * 2 + head, 1), :] = logs[:, head * HD : (head + 1) * HD]


def dot(left, right):
    return jnp.dot(left, right, preferred_element_type=jnp.float32)


def twice(array):
    return jnp.concatenate([array, array], axis=0)


def document_starts(starts_ref, rows):
    return jnp.maximum(starts_ref[...] - lax.axis_index("ctx") * rows, -rows)


def filtered(spectrum, filter_ref, back_ref):
    half = spectrum.shape[0] // 2
    even, odd = spectrum[:half], spectrum[half:]
    tap_even, tap_odd = filter_ref[:half], filter_ref[half:]
    real = (even * tap_even - odd * tap_odd).astype(jnp.bfloat16)
    imag = (even * tap_odd + odd * tap_even).astype(jnp.bfloat16)
    return dot(back_ref[...], jnp.concatenate([real, imag], axis=0))


def convolve(
    heads, other_ref, mine_ref, before_ref, own_taps_ref, starts_ref, product_ref, gate_ref, skip_ref,
    early_ref, late_ref, back_ref, out_ref, taps_ref, halo_ref, filter_ref, sum_ref,
):
    rows = product_ref.shape[0]
    height, width = own_taps_ref.shape
    panel = lax.axis_index("tp")
    even = lax.rem(lax.axis_index("ctx"), 2) == 0
    everything = slice(None)

    def store(step, part, value):
        line = pl.ds(pl.multiple_of((panel ^ step) * height, height), height)
        taps_ref[line, part * 2 * HD : (part + 1) * 2 * HD] = value

    for part in range(width // (2 * HD)):
        line = slice(part * height, (part + 1) * height)
        mine_far, other_far = mine_ref[heads, line], other_ref[heads, line]
        store(0, part, columns_of(own_taps_ref, everything, part))
        store(1, part, jnp.where(even, mine_ref[heads + 1, line], other_ref[heads + 1, line]))
        store(2, part, jnp.where(even, mine_far, other_far))
        store(3, part, jnp.where(even, other_far, mine_far))
        halo_ref[:, part * 2 * HD : (part + 1) * 2 * HD] = jnp.where(
            even, columns_of(before_ref, everything, part), other_ref[heads + 2 + part]
        )
    filter_ref[...] = dot(early_ref[...], twice(taps_ref[...]))
    starts = document_starts(starts_ref, rows)
    line = lax.broadcasted_iota(jnp.int32, (rows, 1), 0)
    zero = jnp.zeros((), jnp.bfloat16)

    begin = jnp.min(starts)
    past = jnp.where(line - rows >= begin, halo_ref[...], zero)
    here = jnp.where(line >= begin, product_ref[...], zero)
    spectrum = dot(early_ref[...], twice(past)) + dot(late_ref[...], twice(here))
    sum_ref[...] = filtered(spectrum, filter_ref, back_ref)

    def one_document(begin):
        here = jnp.where(line >= begin, product_ref[...], zero)
        result = filtered(dot(late_ref[...], twice(here)), filter_ref, back_ref)
        sum_ref[...] = jnp.where(line >= begin, result, sum_ref[...])
        return jnp.min(jnp.where(starts > begin, starts, rows))

    second = jnp.min(jnp.where(starts > begin, starts, rows))
    lax.while_loop(lambda begin: begin < rows, one_document, second)
    out_ref[...] = (
        gate_ref[0].astype(jnp.float32)
        * (skip_ref[...] * product_ref[...].astype(jnp.float32) + sum_ref[...])
    ).astype(jnp.bfloat16)


def twiddles(rows):
    window = 2 * rows
    order = np.arange(rows)[:, None] * 2 + 1
    angle = np.pi * ((order * np.arange(window)[None, :]) % (2 * window)) / window
    ahead = np.concatenate([np.cos(angle), -np.sin(angle)], axis=0)
    back = ahead.T[rows:] / rows
    return jnp.asarray(ahead, jnp.float32), jnp.asarray(back, jnp.float32)


def taps_pairs(peers, panels):
    assert panels == 4
    far, near = [], []
    for peer in range(peers):
        for panel in range(panels):
            here = peer * panels + panel
            far.append((here, peer * panels + (panel ^ (2 + peer % 2))))
            if peer % 2 == 0:
                near.append((here, peer * panels + (panel ^ 1)))
    return far, near


def local(hyena_inputs, filters, skip_bias, queries, keys_values, doc_start):
    rows = queries.shape[0]
    channels = hyena_inputs.shape[2]
    heads = queries.shape[1] // HD
    count = heads // 2
    peers = lax.axis_size("ctx")
    bf16, f32 = jnp.bfloat16, jnp.float32
    shape = jax.ShapeDtypeStruct
    starts = doc_start.reshape(1, rows)

    extras = (filters, *twiddles(rows))
    *packed, near_filters, ahead, back = call(
        functools.partial(pack_heads, heads, len(extras)),
        (shape((3 * rows + NOTE_ROWS, 2 * HD), bf16),) * count
        + tuple(shape(x.shape, x.dtype) for x in extras),
        [
            pltpu.with_memory_space_constraint(x, pltpu.HBM)
            for x in (queries, keys_values, starts, *extras)
        ],
        0,
        4 * queries.size * 3,
        scratch=(
            pltpu.VMEM((1, rows), jnp.int32),
            pltpu.SemaphoreType.DMA,
            pltpu.SemaphoreType.DMA((len(extras),)),
            pltpu.SemaphoreType.DMA((count, 3)),
        ),
        specs=[hbm()] * (3 + len(extras)),
    )
    arrived = [packed[0]] + [None] * (count - 1)
    for step in reversed(range(1, count)):
        arrived[step] = crossed(packed[step], "ctx", 2 * step)
    product, own_taps, far_taps, near_taps, early, late, back = call(
        pack_hyena,
        (shape((rows, channels), bf16),)
        + (shape((filters.shape[0], channels), bf16),) * 3
        + (shape((2 * rows, 2 * rows), bf16),) * 2
        + (shape((rows, 2 * rows), bf16),),
        (hyena_inputs, near_filters, ahead, back),
        0,
        4 * queries.size * 3,
    )
    axes = ("ctx", "tp")
    far_pairs, near_pairs = taps_pairs(peers, lax.axis_size("tp"))
    far_taps = lax.ppermute(far_taps, axes, far_pairs)
    near_taps = lax.ppermute(near_taps, axes, near_pairs)
    before = lax.ppermute(product, "ctx", [(i, i + 1) for i in range(1, peers - 1, 2)])
    query, key_value = call(
        functools.partial(sort_heads, heads),
        (
            shape((count, rows + NOTE_ROWS, 2 * HD), bf16),
            shape((heads + 2 + channels // (2 * HD), rows, 2 * HD), bf16),
        ),
        (*arrived, far_taps, near_taps, product),
        0,
        4 * queries.size * 3,
    )
    other = crossed(key_value, "ctx", 1)
    units = count // UNIT
    partial = call(
        functools.partial(attend_first, heads),
        (
            shape((2, units, 1, UNIT * rows), f32),
            shape((2, units, 1, UNIT * rows), f32),
            shape((2, units, HD, UNIT * rows), f32),
        ),
        (query, key_value),
        2 * (heads * rows) ** 2 * HD,
        4 * queries.size * 4,
    )
    operands = [query, *partial, other]
    if peers > heads:
        pairs = [(i, i + heads) for i in range(peers - heads)]
        operands += [lax.ppermute(each, "ctx", pairs) for each in (key_value, other)]
    mixed = call(
        functools.partial(attend_second, heads),
        (shape((rows + NOTE_ROWS, 2 * HD), bf16),) * count,
        operands,
        2 * (heads * rows) ** 2 * HD,
        4 * queries.size * 4,
        scratch=(pltpu.VMEM((count, rows + NOTE_ROWS, 2 * HD), bf16),),
    )
    returned = [mixed[0]] + [None] * (count - 1)
    for step in reversed(range(1, count)):
        returned[step] = crossed(mixed[step], "ctx", 2 * step)
    hyena_out = call(
        functools.partial(convolve, heads),
        shape((rows, channels), bf16),
        (
            other, key_value, before, own_taps, starts, product, hyena_inputs,
            skip_bias.reshape(1, channels), early, late, back,
        ),
        2 * 4 * 256 * 256 * channels,
        4 * queries.size * 4,
        scratch=(
            pltpu.VMEM((FLEN, channels), bf16),
            pltpu.VMEM((rows, channels), bf16),
            pltpu.VMEM((2 * rows, channels), f32),
            pltpu.VMEM((rows, channels), f32),
        ),
    )
    attention_out, log_totals = call(
        functools.partial(unpack_heads, heads),
        (shape((rows, heads * HD), bf16), shape((heads, rows), f32)),
        returned,
        0,
        4 * queries.size,
    )
    return (hyena_out, attention_out, log_totals)


def solution(mesh):
    in_specs = (
        P(None, "ctx", "tp"),
        P("tp", None),
        P("tp"),
        P("ctx", "tp"),
        P(None, "ctx", "tp"),
        P("ctx"),
    )
    out_specs = (P("ctx", "tp"), P("ctx", "tp"), P("tp", "ctx"))
    return jax.shard_map(local, mesh=mesh, in_specs=in_specs, out_specs=out_specs, check_vma=False)
```

```python
import functools
import math

import jax
import jax.numpy as jnp
import numpy as np
from jax import lax
from jax.experimental import pallas as pl
from jax.experimental.pallas import tpu as pltpu
from jax.sharding import PartitionSpec as P

HD = 128
FLEN = 128
DIGIT = 256
NOTE_ROWS = 16
MASKED = -1e30
VMEM_LIMIT = 16 * 1024 * 1024


def vmem():
    return pl.BlockSpec(memory_space=pltpu.VMEM)


def hbm():
    return pl.BlockSpec(memory_space=pltpu.HBM)


def call(kernel, out_shape, args, flops, nbytes, scratch=(), specs=None):
    return pl.pallas_call(
        kernel,
        out_shape=out_shape,
        in_specs=specs or [vmem() for _ in args],
        out_specs=jax.tree.map(lambda _: vmem(), out_shape),
        scratch_shapes=list(scratch),
        compiler_params=pltpu.CompilerParams(vmem_limit_bytes=VMEM_LIMIT),
        cost_estimate=pl.CostEstimate(flops=flops, bytes_accessed=nbytes, transcendentals=0),
    )(*args)


def crossed(array, axis, bits):
    return lax.ppermute(array, axis, [(i, i ^ bits) for i in range(lax.axis_size(axis))])


def place(heads):
    index = lax.axis_index("ctx")
    member = lax.rem(index, heads)
    return index // heads, member // 2, lax.rem(member, 2)


def pack_heads(heads, queries_ref, keys_values_ref, starts_ref, *refs):
    *outs, held_ref, start_sem, sem = refs
    rows = queries_ref.shape[0]
    _, pair, _ = place(heads)
    first = pltpu.make_async_copy(starts_ref, held_ref, start_sem)
    first.start()
    copies = []
    for step, out in enumerate(outs):
        columns = pl.ds(pl.multiple_of((pair ^ step) * (2 * HD), 2 * HD), 2 * HD)
        for part, source in enumerate(
            (queries_ref, keys_values_ref.at[0], keys_values_ref.at[1])
        ):
            copies.append(
                pltpu.make_async_copy(
                    source.at[:, columns], out.at[pl.ds(part * rows, rows)], sem.at[step, part]
                )
            )
    for copy in copies:
        copy.start()
    first.wait()
    starts = held_ref[...]
    high = (starts // DIGIT).astype(jnp.float32)
    low = (starts % DIGIT).astype(jnp.float32)
    line = lax.broadcasted_iota(jnp.int32, (NOTE_ROWS, rows), 0)
    note = jnp.where(line == 0, high, jnp.where(line == 1, low, 0.0)).astype(jnp.bfloat16)
    for out in outs:
        out[3 * rows :, :HD] = note
        out[3 * rows :, HD:] = note
    for copy in copies:
        copy.wait()


def split(matrix):
    high = matrix.astype(jnp.bfloat16)
    low = (matrix - high.astype(jnp.float32)).astype(jnp.bfloat16)
    return jnp.concatenate([high, low], axis=1)


def pack_hyena(
    hyena_ref, filters_ref, ahead_ref, back_ref, starts_ref, skip_ref,
    product_ref, own_ref, far_ref, near_ref, early_ref, late_ref, back_out, starts_out, skip_out,
    taps_ref, ahead_held, back_held, sem,
):
    width = own_ref.shape[1]
    panel = lax.axis_index("tp")
    parity = lax.rem(lax.axis_index("ctx"), 2)
    targets = (panel, panel ^ (3 - parity), panel ^ 1)
    pairs = [(ahead_ref, ahead_held), (back_ref, back_held)]
    pairs += [(starts_ref, starts_out), (skip_ref, skip_out)]
    for index, target in enumerate(targets):
        columns = pl.ds(pl.multiple_of(target * width, width), width)
        pairs.append((filters_ref.at[:, columns], taps_ref.at[index]))
    copies = [
        pltpu.make_async_copy(source, out, sem.at[index])
        for index, (source, out) in enumerate(pairs)
    ]
    for copy in copies:
        copy.start()
    product_ref[...] = (hyena_ref[1].astype(jnp.float32) * hyena_ref[2].astype(jnp.float32)).astype(
        jnp.bfloat16
    )
    for copy in copies:
        copy.wait()
    for index, out in enumerate((own_ref, far_ref, near_ref)):
        out[...] = taps_ref[index].astype(jnp.bfloat16)
    rows = product_ref.shape[0]
    early_ref[...] = split(ahead_held[:, :rows])
    late_ref[...] = split(ahead_held[:, rows:])
    back_out[...] = back_held[...].astype(jnp.bfloat16)


def columns_of(ref, rows, index):
    return ref[rows, index * 2 * HD : (index + 1) * 2 * HD]


def sort_heads(heads, *refs):
    count = heads // 2
    far_ref, near_ref, product_ref, query_ref, side_ref = refs[-5:]
    rows = (refs[0].shape[0] - NOTE_ROWS) // 3
    _, pair, _ = place(heads)
    for step in range(count):
        source = pair ^ step
        query_ref[source, :rows] = refs[step][:rows]
        query_ref[source, rows:] = refs[step][3 * rows :]
        side_ref[2 * source] = refs[step][rows : 2 * rows]
        side_ref[2 * source + 1] = refs[step][2 * rows : 3 * rows]
    height, width = far_ref.shape
    parts = width // (2 * HD)
    for part in range(parts):
        line = slice(part * height, (part + 1) * height)
        side_ref[heads, line] = columns_of(far_ref, slice(None), part)
        side_ref[heads + 1, line] = columns_of(near_ref, slice(None), part)
        side_ref[heads + 2 + part] = columns_of(product_ref, slice(None), part)


UNIT = 2


def key_set(ref, blocks, head, origin, parity, causal):
    columns = slice(head * HD, (head + 1) * HD)
    rows = ref.shape[1]
    key = jnp.concatenate([ref[2 * block, :, columns] for block in range(blocks)], axis=0)
    value = jnp.concatenate([ref[2 * block + 1, :, columns] for block in range(blocks)], axis=0)
    return key, value, [(2 * block + parity) * rows + origin for block in range(blocks)], causal


def masked_scores(sets, query, start, own, begin):
    held = [[] for _ in range(UNIT)]
    for key, _, firsts, causal in sets:
        scores = lax.dot_general(
            key, query, (((1,), (1,)), ((), ())), preferred_element_type=jnp.float32
        )
        rows = key.shape[0] // len(firsts)
        line = lax.broadcasted_iota(jnp.int32, (rows, rows), 0)
        for block, first in enumerate(firsts):
            for index in range(UNIT):
                if causal and block > begin + index:
                    held[index].append(None)
                    continue
                lanes = slice(index * rows, (index + 1) * rows)
                allowed = line >= start[:, lanes] - first
                if causal and block == begin + index:
                    allowed &= line <= own[:, lanes] - first
                part = scores[block * rows : (block + 1) * rows, lanes]
                held[index].append(jnp.where(allowed, part, MASKED))
    return held


def highest(held):
    tops = [functools.reduce(jnp.maximum, [x for x in parts if x is not None]) for parts in held]
    return jnp.concatenate([jnp.max(top, axis=0, keepdims=True) for top in tops], axis=1)


def weigh(held, top):
    totals, rounded = [], []
    for index, parts in enumerate(held):
        rows = next(x for x in parts if x is not None).shape[1]
        here = top[:, index * rows : (index + 1) * rows]
        weights = [None if x is None else jnp.exp2((x - here) * FACTOR) for x in parts]
        total = functools.reduce(jnp.add, [x for x in weights if x is not None])
        totals.append(jnp.sum(total, axis=0, keepdims=True))
        rounded.append(
            [
                jnp.zeros((rows, rows), jnp.bfloat16) if x is None else x.astype(jnp.bfloat16)
                for x in weights
            ]
        )
    lines = [jnp.concatenate(line, axis=1) for line in zip(*rounded)]
    return jnp.concatenate(totals, axis=1), jnp.concatenate(lines, axis=0)


def mix(sets, rounded):
    return dot(jnp.concatenate([one[1] for one in sets], axis=0).T, rounded)


def unit_rows(heads, query_ref, begin):
    rows = query_ref.shape[1] - NOTE_ROWS
    group, _, parity = place(heads)
    starts = []
    for block in range(begin, begin + UNIT):
        note = query_ref[block, rows:, :HD].astype(jnp.float32)
        starts.append(note[0:1] * float(DIGIT) + note[1:2])
    start = jnp.concatenate(starts, axis=1).astype(jnp.int32) - group * (heads * rows)
    line = lax.broadcasted_iota(jnp.int32, (1, UNIT * rows), 1)
    own = line // rows * rows + line + (2 * begin + parity) * rows
    return start, own


def unit_queries(query_ref, head, begin):
    rows = query_ref.shape[1] - NOTE_ROWS
    blocks = range(begin, begin + UNIT)
    columns = slice(head * HD, (head + 1) * HD)
    return jnp.concatenate([query_ref[block, :rows, columns] for block in blocks], axis=0)


FACTOR = math.log2(math.e) / math.sqrt(HD)


def attend_first(heads, query_ref, key_value_ref, top_ref, total_ref, mixed_ref):
    _, _, parity = place(heads)
    for unit in range(heads // 2 // UNIT):
        begin = unit * UNIT
        start, own = unit_rows(heads, query_ref, begin)
        sets = [[key_set(key_value_ref, begin + UNIT, head, 0, parity, True)] for head in range(2)]
        held = [
            masked_scores(sets[head], unit_queries(query_ref, head, begin), start, own, begin)
            for head in range(2)
        ]
        tops = [highest(each) for each in held]
        weights = [weigh(each, top) for each, top in zip(held, tops)]
        for head, (total, rounded) in enumerate(weights):
            top_ref[head, unit] = tops[head]
            total_ref[head, unit] = total
            mixed_ref[head, unit] = mix(sets[head], rounded)


def attend_second(heads, mine, *refs):
    count = heads // 2
    query_ref, top_ref, total_ref, mixed_ref, other_ref, *more = refs[: -UNIT - 1]
    outs, held_ref = refs[-UNIT - 1 : -1], refs[-1]
    more = more[: len(more) // 2 * 2]
    rows = query_ref.shape[1] - NOTE_ROWS
    _, pair, parity = place(heads)
    here = pair // UNIT

    def one_unit(unit):
        begin = unit * UNIT
        start, own = unit_rows(heads, query_ref, begin)
        sets, held, tops = [], [], []
        for head in range(2):
            sets.append([key_set(other_ref, begin + UNIT, head, 0, 1 - parity, True)])
            for ref, side in zip(more, (parity, 1 - parity)):
                sets[head].append(key_set(ref, count, head, -heads * rows, side, False))
            query = unit_queries(query_ref, head, begin)
            held.append(masked_scores(sets[head], query, start, own, begin))
        for head in range(2):
            tops.append(jnp.maximum(top_ref[head, unit], highest(held[head])))
        weights = [weigh(each, top) for each, top in zip(held, tops)]
        for head, (total, rounded) in enumerate(weights):
            columns = slice(head * HD, (head + 1) * HD)
            top = tops[head]
            scale = jnp.exp2((top_ref[head, unit] - top) * FACTOR)
            total = total_ref[head, unit] * scale + total
            mixed = mixed_ref[head, unit] * scale + mix(sets[head], rounded)
            mixed = (mixed * (1.0 / total)).astype(jnp.bfloat16).T
            logs = top * (1.0 / math.sqrt(HD)) + jnp.log(total)
            high = logs.astype(jnp.bfloat16).astype(jnp.float32)
            middle = (logs - high).astype(jnp.bfloat16).astype(jnp.float32)
            low = logs - high - middle
            line = lax.broadcasted_iota(jnp.int32, (NOTE_ROWS, UNIT * rows), 0)
            note = jnp.where(
                line == 0, high, jnp.where(line == 1, middle, jnp.where(line == 2, low, 0.0))
            ).astype(jnp.bfloat16)
            for index in range(UNIT):
                span = slice(index * rows, (index + 1) * rows)
                held_ref[index, :rows, columns] = mixed[span]
                held_ref[index, rows:, columns] = note[:, span]

    for unit in range(count // UNIT):

        @pl.when((here == unit) if mine else (here != unit))
        def _():
            one_unit(unit)

    for step, out in enumerate(outs):
        out[...] = held_ref[lax.rem(pair, UNIT) ^ step]


def unpack_heads(heads, steps, *refs):
    *sources, out_ref, logs_ref = refs
    rows = out_ref.shape[0]
    _, pair, _ = place(heads)
    for step, source in zip(steps, sources):
        owner = pair ^ step
        out_ref[:, pl.ds(pl.multiple_of(owner * (2 * HD), 2 * HD), 2 * HD)] = source[:rows]
        note = source[rows:].astype(jnp.float32)
        logs = note[0:1] + note[1:2] + note[2:3]
        for head in range(2):
            logs_ref[pl.ds(owner * 2 + head, 1), :] = logs[:, head * HD : (head + 1) * HD]


def dot(left, right):
    return jnp.dot(left, right, preferred_element_type=jnp.float32)


def twice(array):
    return jnp.concatenate([array, array], axis=0)


def document_starts(starts_ref, rows):
    return jnp.maximum(starts_ref[...] - lax.axis_index("ctx") * rows, -rows)


def filtered(spectrum, filter_ref, back_ref):
    half = spectrum.shape[0] // 2
    even, odd = spectrum[:half], spectrum[half:]
    tap_even, tap_odd = filter_ref[:half], filter_ref[half:]
    real = (even * tap_even - odd * tap_odd).astype(jnp.bfloat16)
    imag = (even * tap_odd + odd * tap_even).astype(jnp.bfloat16)
    return dot(back_ref[...], jnp.concatenate([real, imag], axis=0))


def convolve(
    heads, other_ref, mine_ref, before_ref, own_taps_ref, starts_ref, product_ref, gate_ref, skip_ref,
    early_ref, late_ref, back_ref, out_ref, taps_ref, halo_ref, filter_ref, sum_ref,
):
    rows = product_ref.shape[0]
    height, width = own_taps_ref.shape
    panel = lax.axis_index("tp")
    even = lax.rem(lax.axis_index("ctx"), 2) == 0
    everything = slice(None)

    def store(step, part, value):
        line = pl.ds(pl.multiple_of((panel ^ step) * height, height), height)
        taps_ref[line, part * 2 * HD : (part + 1) * 2 * HD] = value

    for part in range(width // (2 * HD)):
        line = slice(part * height, (part + 1) * height)
        mine_far, other_far = mine_ref[heads, line], other_ref[heads, line]
        store(0, part, columns_of(own_taps_ref, everything, part))
        store(1, part, jnp.where(even, other_ref[heads + 1, line], mine_ref[heads + 1, line]))
        store(2, part, jnp.where(even, other_far, mine_far))
        store(3, part, jnp.where(even, mine_far, other_far))
        halo_ref[:, part * 2 * HD : (part + 1) * 2 * HD] = jnp.where(
            even, columns_of(before_ref, everything, part), other_ref[heads + 2 + part]
        )
    filter_ref[...] = dot(early_ref[...], twice(taps_ref[...]))
    starts = document_starts(starts_ref, rows)
    line = lax.broadcasted_iota(jnp.int32, (rows, 1), 0)
    zero = jnp.zeros((), jnp.bfloat16)

    begin = jnp.min(starts)
    past = jnp.where(line - rows >= begin, halo_ref[...], zero)
    here = jnp.where(line >= begin, product_ref[...], zero)
    spectrum = dot(early_ref[...], twice(past)) + dot(late_ref[...], twice(here))
    sum_ref[...] = filtered(spectrum, filter_ref, back_ref)

    def one_document(begin):
        here = jnp.where(line >= begin, product_ref[...], zero)
        result = filtered(dot(late_ref[...], twice(here)), filter_ref, back_ref)
        sum_ref[...] = jnp.where(line >= begin, result, sum_ref[...])
        return jnp.min(jnp.where(starts > begin, starts, rows))

    second = jnp.min(jnp.where(starts > begin, starts, rows))
    lax.while_loop(lambda begin: begin < rows, one_document, second)
    out_ref[...] = (
        gate_ref[0].astype(jnp.float32)
        * (skip_ref[...] * product_ref[...].astype(jnp.float32) + sum_ref[...])
    ).astype(jnp.bfloat16)


def twiddles(rows):
    window = 2 * rows
    order = np.arange(rows)[:, None] * 2 + 1
    angle = np.pi * ((order * np.arange(window)[None, :]) % (2 * window)) / window
    ahead = np.concatenate([np.cos(angle), -np.sin(angle)], axis=0)
    back = ahead.T[rows:] / rows
    return jnp.asarray(ahead, jnp.float32), jnp.asarray(back, jnp.float32)


def taps_pairs(peers, panels):
    assert panels == 4
    far, near = [], []
    for peer in range(peers):
        for panel in range(panels):
            here = peer * panels + panel
            far.append((here, peer * panels + (panel ^ (3 - peer % 2))))
            if peer % 2 == 1:
                near.append((here, peer * panels + (panel ^ 1)))
    return far, near


def local(hyena_inputs, filters, skip_bias, queries, keys_values, doc_start):
    rows = queries.shape[0]
    channels = hyena_inputs.shape[2]
    heads = queries.shape[1] // HD
    count = heads // 2
    peers = lax.axis_size("ctx")
    bf16, f32 = jnp.bfloat16, jnp.float32
    shape = jax.ShapeDtypeStruct
    starts = doc_start.reshape(1, rows)

    packed = call(
        functools.partial(pack_heads, heads),
        (shape((3 * rows + NOTE_ROWS, 2 * HD), bf16),) * count,
        [pltpu.with_memory_space_constraint(x, pltpu.HBM) for x in (queries, keys_values, starts)],
        0,
        4 * queries.size * 3,
        scratch=(
            pltpu.VMEM((1, rows), jnp.int32),
            pltpu.SemaphoreType.DMA,
            pltpu.SemaphoreType.DMA((count, 3)),
        ),
        specs=[hbm()] * 3,
    )
    arrived = [packed[0]] + [None] * (count - 1)
    for step in reversed(range(1, count)):
        arrived[step] = crossed(packed[step], "ctx", 2 * step)
    height = filters.shape[0]
    ahead, back = twiddles(rows)
    near_hbm = [
        pltpu.with_memory_space_constraint(x, pltpu.HBM)
        for x in (filters, ahead, back, starts, skip_bias.reshape(1, channels))
    ]
    product, own_taps, far_taps, near_taps, early, late, back, near_starts, skip = call(
        pack_hyena,
        (shape((rows, channels), bf16),)
        + (shape((height, channels), bf16),) * 3
        + (shape((2 * rows, 2 * rows), bf16),) * 2
        + (shape((rows, 2 * rows), bf16),)
        + (shape((1, rows), jnp.int32), shape((1, channels), f32)),
        (hyena_inputs, *near_hbm),
        0,
        4 * queries.size * 3,
        scratch=(
            pltpu.VMEM((3, height, channels), f32),
            pltpu.VMEM((2 * rows, 2 * rows), f32),
            pltpu.VMEM((rows, 2 * rows), f32),
            pltpu.SemaphoreType.DMA((7,)),
        ),
        specs=[vmem()] + [hbm()] * 5,
    )
    axes = ("ctx", "tp")
    far_pairs, near_pairs = taps_pairs(peers, lax.axis_size("tp"))
    far_taps = lax.ppermute(far_taps, axes, far_pairs)
    near_taps = lax.ppermute(near_taps, axes, near_pairs)
    before = lax.ppermute(product, "ctx", [(i, i + 1) for i in range(1, peers - 1, 2)])
    query, key_value = call(
        functools.partial(sort_heads, heads),
        (
            shape((count, rows + NOTE_ROWS, 2 * HD), bf16),
            shape((heads + 2 + channels // (2 * HD), rows, 2 * HD), bf16),
        ),
        (*arrived, far_taps, near_taps, product),
        0,
        4 * queries.size * 3,
    )
    other = crossed(key_value, "ctx", 1)
    units = count // UNIT
    partial = call(
        functools.partial(attend_first, heads),
        (
            shape((2, units, 1, UNIT * rows), f32),
            shape((2, units, 1, UNIT * rows), f32),
            shape((2, units, HD, UNIT * rows), f32),
        ),
        (query, key_value),
        2 * (heads * rows) ** 2 * HD,
        4 * queries.size * 4,
    )
    operands = [query, *partial, other]
    if peers > heads:
        pairs = [(i, i + heads) for i in range(peers - heads)]
        operands += [lax.ppermute(each, "ctx", pairs) for each in (key_value, other)]
    assert count == 2 * UNIT
    message = shape((rows + NOTE_ROWS, 2 * HD), bf16)

    def second(mine, *more):
        return call(
            functools.partial(attend_second, heads, mine),
            (message,) * UNIT,
            (*operands, *more),
            (heads * rows) ** 2 * HD,
            4 * queries.size * 4,
            scratch=(pltpu.VMEM((UNIT, rows + NOTE_ROWS, 2 * HD), bf16),),
        )

    theirs = second(False)
    own = second(True, theirs[0])
    returned = [own[0], crossed(theirs[0], "ctx", 4), crossed(theirs[1], "ctx", 6)]
    returned.append(crossed(own[1], "ctx", 2))
    hyena_out = call(
        functools.partial(convolve, heads),
        shape((rows, channels), bf16),
        (
            other, key_value, before, own_taps, near_starts, product, hyena_inputs,
            skip, early, late, back,
        ),
        2 * 4 * 256 * 256 * channels,
        4 * queries.size * 4,
        scratch=(
            pltpu.VMEM((FLEN, channels), bf16),
            pltpu.VMEM((rows, channels), bf16),
            pltpu.VMEM((2 * rows, channels), f32),
            pltpu.VMEM((rows, channels), f32),
        ),
    )
    attention_out, log_totals = call(
        functools.partial(unpack_heads, heads, (0, 2, 3, 1)),
        (shape((rows, heads * HD), bf16), shape((heads, rows), f32)),
        returned,
        0,
        4 * queries.size,
    )
    return (hyena_out, attention_out, log_totals)


def solution(mesh):
    in_specs = (
        P(None, "ctx", "tp"),
        P("tp", None),
        P("tp"),
        P("ctx", "tp"),
        P(None, "ctx", "tp"),
        P("ctx"),
    )
    out_specs = (P("ctx", "tp"), P("ctx", "tp"), P("tp", "ctx"))
    return jax.shard_map(local, mesh=mesh, in_specs=in_specs, out_specs=out_specs, check_vma=False)
```

```python
import functools
import math

import jax
import jax.numpy as jnp
import numpy as np
from jax import lax
from jax.experimental import pallas as pl
from jax.experimental.pallas import tpu as pltpu
from jax.sharding import PartitionSpec as P

HD = 128
FLEN = 128
DIGIT = 256
NOTE_ROWS = 16
MASKED = -1e30
VMEM_LIMIT = 16 * 1024 * 1024


def vmem():
    return pl.BlockSpec(memory_space=pltpu.VMEM)


def hbm():
    return pl.BlockSpec(memory_space=pltpu.HBM)


def call(kernel, out_shape, args, flops, nbytes, scratch=(), specs=None):
    return pl.pallas_call(
        kernel,
        out_shape=out_shape,
        in_specs=specs or [vmem() for _ in args],
        out_specs=jax.tree.map(lambda _: vmem(), out_shape),
        scratch_shapes=list(scratch),
        compiler_params=pltpu.CompilerParams(vmem_limit_bytes=VMEM_LIMIT),
        cost_estimate=pl.CostEstimate(flops=flops, bytes_accessed=nbytes, transcendentals=0),
    )(*args)


def crossed(array, axis, bits):
    return lax.ppermute(array, axis, [(i, i ^ bits) for i in range(lax.axis_size(axis))])


def place(heads):
    index = lax.axis_index("ctx")
    member = lax.rem(index, heads)
    return index // heads, member // 2, lax.rem(member, 2)


def pack_heads(heads, queries_ref, keys_values_ref, starts_ref, filters_ref, *refs):
    *outs, taps_ref, held_ref, start_sem, taps_sem, sem = refs
    rows = queries_ref.shape[0]
    _, pair, _ = place(heads)
    first = pltpu.make_async_copy(starts_ref, held_ref, start_sem)
    first.start()
    copies = []
    for step, out in enumerate(outs):
        columns = pl.ds(pl.multiple_of((pair ^ step) * (2 * HD), 2 * HD), 2 * HD)
        for part, source in enumerate(
            (queries_ref, keys_values_ref.at[0], keys_values_ref.at[1])
        ):
            copies.append(
                pltpu.make_async_copy(
                    source.at[:, columns], out.at[pl.ds(part * rows, rows)], sem.at[step, part]
                )
            )
    width = taps_ref.shape[2]
    panel = lax.axis_index("tp")
    for index, target in enumerate((panel, panel ^ (3 - lax.rem(lax.axis_index("ctx"), 2)), panel ^ 1)):
        columns = pl.ds(pl.multiple_of(target * width, width), width)
        copies.append(
            pltpu.make_async_copy(
                filters_ref.at[:, columns], taps_ref.at[index], taps_sem.at[index]
            )
        )
    for copy in copies:
        copy.start()
    first.wait()
    starts = held_ref[...]
    high = (starts // DIGIT).astype(jnp.float32)
    low = (starts % DIGIT).astype(jnp.float32)
    line = lax.broadcasted_iota(jnp.int32, (NOTE_ROWS, rows), 0)
    note = jnp.where(line == 0, high, jnp.where(line == 1, low, 0.0)).astype(jnp.bfloat16)
    for out in outs:
        out[3 * rows :, :HD] = note
        out[3 * rows :, HD:] = note
    for copy in copies:
        copy.wait()


def split(matrix):
    high = matrix.astype(jnp.bfloat16)
    low = (matrix - high.astype(jnp.float32)).astype(jnp.bfloat16)
    return jnp.concatenate([high, low], axis=1)


def pack_hyena(hyena_ref, taps_ref, product_ref, own_ref, far_ref, mixed_ref):
    product_ref[...] = (hyena_ref[1].astype(jnp.float32) * hyena_ref[2].astype(jnp.float32)).astype(
        jnp.bfloat16
    )
    own_ref[...] = taps_ref[0].astype(jnp.bfloat16)
    far_ref[...] = taps_ref[1].astype(jnp.bfloat16)
    height, width = own_ref.shape
    whole = mixed_ref.shape[1]
    mixed_ref[...] = product_ref[:, :whole]

    @pl.when(lax.rem(lax.axis_index("ctx"), 2) == 1)
    def _():
        near = taps_ref[2].astype(jnp.bfloat16)
        mixed_ref[:height] = near[:, :whole]
        mixed_ref[height : 2 * height, : width - whole] = near[:, whole:]


def prepare(
    ahead_ref, back_ref, starts_ref, skip_ref, early_ref, late_ref, back_out, starts_out, skip_out,
    ahead_held, back_held, sem,
):
    pairs = (
        (ahead_ref, ahead_held), (back_ref, back_held), (starts_ref, starts_out), (skip_ref, skip_out)
    )
    copies = [
        pltpu.make_async_copy(source, out, sem.at[index])
        for index, (source, out) in enumerate(pairs)
    ]
    for copy in copies:
        copy.start()
    for copy in copies:
        copy.wait()
    rows = back_out.shape[0]
    early_ref[...] = split(ahead_held[:, :rows])
    late_ref[...] = split(ahead_held[:, rows:])
    back_out[...] = back_held[...].astype(jnp.bfloat16)


def columns_of(ref, rows, index):
    return ref[rows, index * 2 * HD : (index + 1) * 2 * HD]


def near_strip(came_ref, height, part):
    parts = came_ref.shape[1] // (2 * HD)
    line = part // parts
    return columns_of(came_ref, slice(line * height, (line + 1) * height), part % parts)


def sort_heads(heads, *refs):
    count = heads // 2
    far_ref, came_ref, product_ref = refs[count : count + 3]
    query_ref, side_ref = refs[-2:]
    rows = (refs[0].shape[0] - NOTE_ROWS) // 3
    _, pair, _ = place(heads)
    for step in range(count):
        source = pair ^ step
        query_ref[source, :rows] = refs[step][:rows]
        query_ref[source, rows:] = refs[step][3 * rows :]
        side_ref[2 * source] = refs[step][rows : 2 * rows]
        side_ref[2 * source + 1] = refs[step][2 * rows : 3 * rows]
    height, width = far_ref.shape
    parts = width // (2 * HD)
    for part in range(parts):
        line = slice(part * height, (part + 1) * height)
        side_ref[heads, line] = columns_of(far_ref, slice(None), part)
        side_ref[heads + 1, line] = near_strip(came_ref, height, part)
    side_ref[heads + 2] = columns_of(product_ref, slice(None), parts - 1)


UNIT = 2


def key_set(ref, blocks, head, origin, parity, causal):
    columns = slice(head * HD, (head + 1) * HD)
    rows = ref.shape[1]
    key = jnp.concatenate([ref[2 * block, :, columns] for block in range(blocks)], axis=0)
    value = jnp.concatenate([ref[2 * block + 1, :, columns] for block in range(blocks)], axis=0)
    return key, value, [(2 * block + parity) * rows + origin for block in range(blocks)], causal


def masked_scores(sets, query, start, own, begin):
    held = [[] for _ in range(UNIT)]
    for key, _, firsts, causal in sets:
        scores = lax.dot_general(
            key, query, (((1,), (1,)), ((), ())), preferred_element_type=jnp.float32
        )
        rows = key.shape[0] // len(firsts)
        line = lax.broadcasted_iota(jnp.int32, (rows, rows), 0)
        for block, first in enumerate(firsts):
            for index in range(UNIT):
                if causal and block > begin + index:
                    held[index].append(None)
                    continue
                lanes = slice(index * rows, (index + 1) * rows)
                allowed = line >= start[:, lanes] - first
                if causal and block == begin + index:
                    allowed &= line <= own[:, lanes] - first
                part = scores[block * rows : (block + 1) * rows, lanes]
                held[index].append(jnp.where(allowed, part, MASKED))
    return held


def highest(held):
    tops = [functools.reduce(jnp.maximum, [x for x in parts if x is not None]) for parts in held]
    return jnp.concatenate([jnp.max(top, axis=0, keepdims=True) for top in tops], axis=1)


def weigh(held, top):
    totals, rounded = [], []
    for index, parts in enumerate(held):
        rows = next(x for x in parts if x is not None).shape[1]
        here = top[:, index * rows : (index + 1) * rows]
        weights = [None if x is None else jnp.exp2((x - here) * FACTOR) for x in parts]
        total = functools.reduce(jnp.add, [x for x in weights if x is not None])
        totals.append(jnp.sum(total, axis=0, keepdims=True))
        rounded.append(
            [
                jnp.zeros((rows, rows), jnp.bfloat16) if x is None else x.astype(jnp.bfloat16)
                for x in weights
            ]
        )
    lines = [jnp.concatenate(line, axis=1) for line in zip(*rounded)]
    return jnp.concatenate(totals, axis=1), jnp.concatenate(lines, axis=0)


def mix(sets, rounded):
    return dot(jnp.concatenate([one[1] for one in sets], axis=0).T, rounded)


def unit_rows(heads, query_ref, begin):
    rows = query_ref.shape[1] - NOTE_ROWS
    group, _, parity = place(heads)
    starts = []
    for block in range(begin, begin + UNIT):
        note = query_ref[block, rows:, :HD].astype(jnp.float32)
        starts.append(note[0:1] * float(DIGIT) + note[1:2])
    start = jnp.concatenate(starts, axis=1).astype(jnp.int32) - group * (heads * rows)
    line = lax.broadcasted_iota(jnp.int32, (1, UNIT * rows), 1)
    own = line // rows * rows + line + (2 * begin + parity) * rows
    return start, own


def unit_queries(query_ref, head, begin):
    rows = query_ref.shape[1] - NOTE_ROWS
    blocks = range(begin, begin + UNIT)
    columns = slice(head * HD, (head + 1) * HD)
    return jnp.concatenate([query_ref[block, :rows, columns] for block in blocks], axis=0)


FACTOR = math.log2(math.e) / math.sqrt(HD)


def attend_first(heads, query_ref, key_value_ref, top_ref, total_ref, mixed_ref):
    _, _, parity = place(heads)
    for unit in range(heads // 2 // UNIT):
        begin = unit * UNIT
        start, own = unit_rows(heads, query_ref, begin)
        sets = [[key_set(key_value_ref, begin + UNIT, head, 0, parity, True)] for head in range(2)]
        held = [
            masked_scores(sets[head], unit_queries(query_ref, head, begin), start, own, begin)
            for head in range(2)
        ]
        tops = [highest(each) for each in held]
        weights = [weigh(each, top) for each, top in zip(held, tops)]
        for head, (total, rounded) in enumerate(weights):
            top_ref[head, unit] = tops[head]
            total_ref[head, unit] = total
            mixed_ref[head, unit] = mix(sets[head], rounded)


def attend_second(heads, mine, *refs):
    count = heads // 2
    query_ref, top_ref, total_ref, mixed_ref, other_ref, *more = refs[: -UNIT - 1]
    outs, held_ref = refs[-UNIT - 1 : -1], refs[-1]
    more = more[: len(more) // 2 * 2]
    rows = query_ref.shape[1] - NOTE_ROWS
    _, pair, parity = place(heads)
    here = pair // UNIT

    def one_unit(unit):
        begin = unit * UNIT
        start, own = unit_rows(heads, query_ref, begin)
        sets, held, tops = [], [], []
        for head in range(2):
            sets.append([key_set(other_ref, begin + UNIT, head, 0, 1 - parity, True)])
            for ref, side in zip(more, (parity, 1 - parity)):
                sets[head].append(key_set(ref, count, head, -heads * rows, side, False))
            query = unit_queries(query_ref, head, begin)
            held.append(masked_scores(sets[head], query, start, own, begin))
        for head in range(2):
            tops.append(jnp.maximum(top_ref[head, unit], highest(held[head])))
        weights = [weigh(each, top) for each, top in zip(held, tops)]
        for head, (total, rounded) in enumerate(weights):
            columns = slice(head * HD, (head + 1) * HD)
            top = tops[head]
            scale = jnp.exp2((top_ref[head, unit] - top) * FACTOR)
            total = total_ref[head, unit] * scale + total
            mixed = mixed_ref[head, unit] * scale + mix(sets[head], rounded)
            mixed = (mixed * (1.0 / total)).astype(jnp.bfloat16).T
            logs = top * (1.0 / math.sqrt(HD)) + jnp.log(total)
            high = logs.astype(jnp.bfloat16).astype(jnp.float32)
            middle = (logs - high).astype(jnp.bfloat16).astype(jnp.float32)
            low = logs - high - middle
            line = lax.broadcasted_iota(jnp.int32, (NOTE_ROWS, UNIT * rows), 0)
            note = jnp.where(
                line == 0, high, jnp.where(line == 1, middle, jnp.where(line == 2, low, 0.0))
            ).astype(jnp.bfloat16)
            for index in range(UNIT):
                span = slice(index * rows, (index + 1) * rows)
                held_ref[index, :rows, columns] = mixed[span]
                held_ref[index, rows:, columns] = note[:, span]

    for unit in range(count // UNIT):

        @pl.when((here == unit) if mine else (here != unit))
        def _():
            one_unit(unit)

    for step, out in enumerate(outs):
        out[...] = held_ref[lax.rem(pair, UNIT) ^ step]


def unpack_heads(heads, steps, *refs):
    *sources, out_ref, logs_ref = refs
    rows = out_ref.shape[0]
    _, pair, _ = place(heads)
    for step, source in zip(steps, sources):
        owner = pair ^ step
        out_ref[:, pl.ds(pl.multiple_of(owner * (2 * HD), 2 * HD), 2 * HD)] = source[:rows]
        note = source[rows:].astype(jnp.float32)
        logs = note[0:1] + note[1:2] + note[2:3]
        for head in range(2):
            logs_ref[pl.ds(owner * 2 + head, 1), :] = logs[:, head * HD : (head + 1) * HD]


def dot(left, right):
    return jnp.dot(left, right, preferred_element_type=jnp.float32)


def twice(array):
    return jnp.concatenate([array, array], axis=0)


def document_starts(starts_ref, rows):
    return jnp.maximum(starts_ref[...] - lax.axis_index("ctx") * rows, -rows)


def filtered(spectrum, filter_ref, back_ref):
    half = spectrum.shape[0] // 2
    even, odd = spectrum[:half], spectrum[half:]
    tap_even, tap_odd = filter_ref[:half], filter_ref[half:]
    real = (even * tap_even - odd * tap_odd).astype(jnp.bfloat16)
    imag = (even * tap_odd + odd * tap_even).astype(jnp.bfloat16)
    return dot(back_ref[...], jnp.concatenate([real, imag], axis=0))


def convolve(
    heads, other_ref, mine_ref, came_ref, before_ref, own_taps_ref, starts_ref, product_ref, gate_ref, skip_ref,
    early_ref, late_ref, back_ref, out_ref, taps_ref, halo_ref, filter_ref, sum_ref,
):
    rows = product_ref.shape[0]
    height, width = own_taps_ref.shape
    panel = lax.axis_index("tp")
    even = lax.rem(lax.axis_index("ctx"), 2) == 0
    everything = slice(None)

    def store(step, part, value):
        line = pl.ds(pl.multiple_of((panel ^ step) * height, height), height)
        taps_ref[line, part * 2 * HD : (part + 1) * 2 * HD] = value

    parts = width // (2 * HD)
    for part in range(parts):
        line = slice(part * height, (part + 1) * height)
        mine_far, other_far = mine_ref[heads, line], other_ref[heads, line]
        store(0, part, columns_of(own_taps_ref, everything, part))
        store(1, part, jnp.where(even, near_strip(came_ref, height, part), other_ref[heads + 1, line]))
        store(2, part, jnp.where(even, other_far, mine_far))
        store(3, part, jnp.where(even, mine_far, other_far))
        halo_ref[:, part * 2 * HD : (part + 1) * 2 * HD] = jnp.where(
            even,
            columns_of(before_ref, everything, part),
            other_ref[heads + 2] if part == parts - 1 else columns_of(came_ref, everything, part),
        )
    filter_ref[...] = dot(early_ref[...], twice(taps_ref[...]))
    starts = document_starts(starts_ref, rows)
    line = lax.broadcasted_iota(jnp.int32, (rows, 1), 0)
    zero = jnp.zeros((), jnp.bfloat16)

    begin = jnp.min(starts)
    past = jnp.where(line - rows >= begin, halo_ref[...], zero)
    here = jnp.where(line >= begin, product_ref[...], zero)
    spectrum = dot(early_ref[...], twice(past)) + dot(late_ref[...], twice(here))
    sum_ref[...] = filtered(spectrum, filter_ref, back_ref)

    def one_document(begin):
        here = jnp.where(line >= begin, product_ref[...], zero)
        result = filtered(dot(late_ref[...], twice(here)), filter_ref, back_ref)
        sum_ref[...] = jnp.where(line >= begin, result, sum_ref[...])
        return jnp.min(jnp.where(starts > begin, starts, rows))

    second = jnp.min(jnp.where(starts > begin, starts, rows))
    lax.while_loop(lambda begin: begin < rows, one_document, second)
    out_ref[...] = (
        gate_ref[0].astype(jnp.float32)
        * (skip_ref[...] * product_ref[...].astype(jnp.float32) + sum_ref[...])
    ).astype(jnp.bfloat16)


def twiddles(rows):
    window = 2 * rows
    order = np.arange(rows)[:, None] * 2 + 1
    angle = np.pi * ((order * np.arange(window)[None, :]) % (2 * window)) / window
    ahead = np.concatenate([np.cos(angle), -np.sin(angle)], axis=0)
    back = ahead.T[rows:] / rows
    return jnp.asarray(ahead, jnp.float32), jnp.asarray(back, jnp.float32)


def side_pairs(peers, panels):
    assert panels == 4
    far, mixed = [], []
    for peer in range(peers):
        for panel in range(panels):
            here = peer * panels + panel
            far.append((here, peer * panels + (panel ^ (3 - peer % 2))))
            if peer % 2 == 0:
                mixed.append((here, here + panels))
            else:
                mixed.append((here, (peer - 1) * panels + (panel ^ 1)))
    return far, mixed


def local(hyena_inputs, filters, skip_bias, queries, keys_values, doc_start):
    rows = queries.shape[0]
    channels = hyena_inputs.shape[2]
    heads = queries.shape[1] // HD
    count = heads // 2
    peers = lax.axis_size("ctx")
    bf16, f32 = jnp.bfloat16, jnp.float32
    shape = jax.ShapeDtypeStruct
    starts = doc_start.reshape(1, rows)

    height = filters.shape[0]

    def pinned(*arrays):
        return [pltpu.with_memory_space_constraint(x, pltpu.HBM) for x in arrays]

    *packed, wide_taps = call(
        functools.partial(pack_heads, heads),
        (shape((3 * rows + NOTE_ROWS, 2 * HD), bf16),) * count + (shape((3, height, channels), f32),),
        pinned(queries, keys_values, starts, filters),
        0,
        4 * queries.size * 3,
        scratch=(
            pltpu.VMEM((1, rows), jnp.int32),
            pltpu.SemaphoreType.DMA,
            pltpu.SemaphoreType.DMA((3,)),
            pltpu.SemaphoreType.DMA((count, 3)),
        ),
        specs=[hbm()] * 4,
    )
    arrived = [packed[0]] + [crossed(packed[step], "ctx", 2 * step) for step in range(1, count)]
    product, own_taps, far_taps, mixed_rows = call(
        pack_hyena,
        (shape((rows, channels), bf16),)
        + (shape((height, channels), bf16),) * 2
        + (shape((rows, channels - 2 * HD), bf16),),
        (hyena_inputs, wide_taps),
        0,
        4 * queries.size * 3,
    )
    axes = ("ctx", "tp")
    far_pairs, mixed_pairs = side_pairs(peers, lax.axis_size("tp"))
    far_taps = lax.ppermute(far_taps, axes, far_pairs)
    came = lax.ppermute(mixed_rows, axes, mixed_pairs)
    before = lax.ppermute(product, "ctx", [(i, i + 1) for i in range(1, peers - 1, 2)])
    ahead, back = twiddles(rows)
    early, late, back, near_starts, skip = call(
        prepare,
        (shape((2 * rows, 2 * rows), bf16),) * 2
        + (shape((rows, 2 * rows), bf16), shape((1, rows), jnp.int32), shape((1, channels), f32)),
        pinned(ahead, back, starts, skip_bias.reshape(1, channels)),
        0,
        4 * queries.size,
        scratch=(
            pltpu.VMEM((2 * rows, 2 * rows), f32),
            pltpu.VMEM((rows, 2 * rows), f32),
            pltpu.SemaphoreType.DMA((4,)),
        ),
        specs=[hbm()] * 4,
    )

    query, key_value = call(
        functools.partial(sort_heads, heads),
        (
            shape((count, rows + NOTE_ROWS, 2 * HD), bf16),
            shape((heads + 3, rows, 2 * HD), bf16),
        ),
        (*arrived, far_taps, came, product, skip),
        0,
        4 * queries.size * 3,
    )
    other = crossed(key_value, "ctx", 1)
    units = count // UNIT
    partial = call(
        functools.partial(attend_first, heads),
        (
            shape((2, units, 1, UNIT * rows), f32),
            shape((2, units, 1, UNIT * rows), f32),
            shape((2, units, HD, UNIT * rows), f32),
        ),
        (query, key_value),
        2 * (heads * rows) ** 2 * HD,
        4 * queries.size * 4,
    )
    operands = [query, *partial, other]
    if peers > heads:
        pairs = [(i, i + heads) for i in range(peers - heads)]
        operands += [lax.ppermute(each, "ctx", pairs) for each in (key_value, other)]
    assert count == 2 * UNIT
    message = shape((rows + NOTE_ROWS, 2 * HD), bf16)

    def second(mine, *more):
        return call(
            functools.partial(attend_second, heads, mine),
            (message,) * UNIT,
            (*operands, *more),
            (heads * rows) ** 2 * HD,
            4 * queries.size * 4,
            scratch=(pltpu.VMEM((UNIT, rows + NOTE_ROWS, 2 * HD), bf16),),
        )

    theirs = second(False)
    own = second(True, theirs[0])
    returned = [own[0], crossed(theirs[0], "ctx", 4), crossed(theirs[1], "ctx", 6)]
    returned.append(crossed(own[1], "ctx", 2))
    hyena_out = call(
        functools.partial(convolve, heads),
        shape((rows, channels), bf16),
        (
            other, key_value, came, before, own_taps, near_starts, product, hyena_inputs,
            skip, early, late, back,
        ),
        2 * 4 * 256 * 256 * channels,
        4 * queries.size * 4,
        scratch=(
            pltpu.VMEM((FLEN, channels), bf16),
            pltpu.VMEM((rows, channels), bf16),
            pltpu.VMEM((2 * rows, channels), f32),
            pltpu.VMEM((rows, channels), f32),
        ),
    )
    attention_out, log_totals = call(
        functools.partial(unpack_heads, heads, (0, 2, 3, 1)),
        (shape((rows, heads * HD), bf16), shape((heads, rows), f32)),
        returned,
        0,
        4 * queries.size,
    )
    return (hyena_out, attention_out, log_totals)


def solution(mesh):
    in_specs = (
        P(None, "ctx", "tp"),
        P("tp", None),
        P("tp"),
        P("ctx", "tp"),
        P(None, "ctx", "tp"),
        P("ctx"),
    )
    out_specs = (P("ctx", "tp"), P("ctx", "tp"), P("tp", "ctx"))
    return jax.shard_map(local, mesh=mesh, in_specs=in_specs, out_specs=out_specs, check_vma=False)
```

```python
import functools
import math

import jax
import jax.numpy as jnp
import numpy as np
from jax import lax
from jax.experimental import pallas as pl
from jax.experimental.pallas import tpu as pltpu
from jax.sharding import PartitionSpec as P

HD = 128
FLEN = 128
DIGIT = 256
NOTE_ROWS = 16
MASKED = -1e30
VMEM_LIMIT = 16 * 1024 * 1024


def vmem():
    return pl.BlockSpec(memory_space=pltpu.VMEM)


def hbm():
    return pl.BlockSpec(memory_space=pltpu.HBM)


def call(kernel, out_shape, args, flops, nbytes, scratch=(), specs=None):
    return pl.pallas_call(
        kernel,
        out_shape=out_shape,
        in_specs=specs or [vmem() for _ in args],
        out_specs=jax.tree.map(lambda _: vmem(), out_shape),
        scratch_shapes=list(scratch),
        compiler_params=pltpu.CompilerParams(vmem_limit_bytes=VMEM_LIMIT),
        cost_estimate=pl.CostEstimate(flops=flops, bytes_accessed=nbytes, transcendentals=0),
    )(*args)


def crossed(array, axis, bits):
    return lax.ppermute(array, axis, [(i, i ^ bits) for i in range(lax.axis_size(axis))])


def place(heads):
    index = lax.axis_index("ctx")
    member = lax.rem(index, heads)
    return index // heads, member // 2, lax.rem(member, 2)


def pack_heads(heads, queries_ref, keys_values_ref, starts_ref, filters_ref, *refs):
    *outs, taps_ref, held_ref, start_sem, taps_sem, sem = refs
    rows = queries_ref.shape[0]
    _, pair, _ = place(heads)
    first = pltpu.make_async_copy(starts_ref, held_ref, start_sem)
    first.start()
    copies = []
    for step, out in enumerate(outs):
        columns = pl.ds(pl.multiple_of((pair ^ step) * (2 * HD), 2 * HD), 2 * HD)
        for part, source in enumerate(
            (queries_ref, keys_values_ref.at[0], keys_values_ref.at[1])
        ):
            copies.append(
                pltpu.make_async_copy(
                    source.at[:, columns], out.at[pl.ds(part * rows, rows)], sem.at[step, part]
                )
            )
    width = taps_ref.shape[2]
    panel = lax.axis_index("tp")
    for index, target in enumerate((panel, panel ^ (3 - lax.rem(lax.axis_index("ctx"), 2)), panel ^ 1)):
        columns = pl.ds(pl.multiple_of(target * width, width), width)
        copies.append(
            pltpu.make_async_copy(
                filters_ref.at[:, columns], taps_ref.at[index], taps_sem.at[index]
            )
        )
    for copy in copies:
        copy.start()
    first.wait()
    starts = held_ref[...]
    high = (starts // DIGIT).astype(jnp.float32)
    low = (starts % DIGIT).astype(jnp.float32)
    line = lax.broadcasted_iota(jnp.int32, (NOTE_ROWS, rows), 0)
    note = jnp.where(line == 0, high, jnp.where(line == 1, low, 0.0)).astype(jnp.bfloat16)
    for out in outs:
        out[3 * rows :, :HD] = note
        out[3 * rows :, HD:] = note
    for copy in copies:
        copy.wait()


def split(matrix):
    high = matrix.astype(jnp.bfloat16)
    low = (matrix - high.astype(jnp.float32)).astype(jnp.bfloat16)
    return jnp.concatenate([high, low], axis=1)


def pack_hyena(hyena_ref, taps_ref, product_ref, own_ref, far_ref, mixed_ref):
    product_ref[...] = (hyena_ref[1].astype(jnp.float32) * hyena_ref[2].astype(jnp.float32)).astype(
        jnp.bfloat16
    )
    own_ref[...] = taps_ref[0].astype(jnp.bfloat16)
    far_ref[...] = taps_ref[1].astype(jnp.bfloat16)
    height, width = own_ref.shape
    whole = mixed_ref.shape[1]
    mixed_ref[...] = product_ref[:, :whole]

    @pl.when(lax.rem(lax.axis_index("ctx"), 2) == 1)
    def _():
        near = taps_ref[2].astype(jnp.bfloat16)
        mixed_ref[:height] = near[:, :whole]
        mixed_ref[height : 2 * height, : width - whole] = near[:, whole:]


def prepare(
    ahead_ref, back_ref, starts_ref, skip_ref, early_ref, late_ref, back_out, starts_out, skip_out,
    ahead_held, back_held, sem,
):
    pairs = (
        (ahead_ref, ahead_held), (back_ref, back_held), (starts_ref, starts_out), (skip_ref, skip_out)
    )
    copies = [
        pltpu.make_async_copy(source, out, sem.at[index])
        for index, (source, out) in enumerate(pairs)
    ]
    for copy in copies:
        copy.start()
    for copy in copies:
        copy.wait()
    rows = back_out.shape[0]
    early_ref[...] = split(ahead_held[:, :rows])
    late_ref[...] = split(ahead_held[:, rows:])
    back_out[...] = back_held[...].astype(jnp.bfloat16)


def columns_of(ref, rows, index):
    return ref[rows, index * 2 * HD : (index + 1) * 2 * HD]


def near_strip(came_ref, height, part):
    parts = came_ref.shape[1] // (2 * HD)
    line = part // parts
    return columns_of(came_ref, slice(line * height, (line + 1) * height), part % parts)


def sort_heads(heads, *refs):
    count = heads // 2
    far_ref, came_ref, product_ref = refs[count : count + 3]
    query_ref, side_ref = refs[-2:]
    rows = (refs[0].shape[0] - NOTE_ROWS) // 3
    _, pair, _ = place(heads)
    for step in range(count):
        source = pair ^ step
        query_ref[source, :rows] = refs[step][:rows]
        query_ref[source, rows:] = refs[step][3 * rows :]
        side_ref[2 * source] = refs[step][rows : 2 * rows]
        side_ref[2 * source + 1] = refs[step][2 * rows : 3 * rows]
    height, width = far_ref.shape
    parts = width // (2 * HD)
    for part in range(parts):
        line = slice(part * height, (part + 1) * height)
        side_ref[heads, line] = columns_of(far_ref, slice(None), part)
        side_ref[heads + 1, line] = near_strip(came_ref, height, part)
    side_ref[heads + 2] = columns_of(product_ref, slice(None), parts - 1)


UNIT = 2


def key_set(ref, blocks, head, origin, parity, causal):
    columns = slice(head * HD, (head + 1) * HD)
    rows = ref.shape[1]
    key = jnp.concatenate([ref[2 * block, :, columns] for block in range(blocks)], axis=0)
    value = jnp.concatenate([ref[2 * block + 1, :, columns] for block in range(blocks)], axis=0)
    return key, value, [(2 * block + parity) * rows + origin for block in range(blocks)], causal


def masked_scores(sets, query, start, own, begin):
    held = [[] for _ in range(UNIT)]
    for key, _, firsts, causal in sets:
        scores = lax.dot_general(
            key, query, (((1,), (1,)), ((), ())), preferred_element_type=jnp.float32
        )
        rows = key.shape[0] // len(firsts)
        line = lax.broadcasted_iota(jnp.int32, (rows, rows), 0)
        for block, first in enumerate(firsts):
            for index in range(UNIT):
                if causal and block > begin + index:
                    held[index].append(None)
                    continue
                lanes = slice(index * rows, (index + 1) * rows)
                allowed = line >= start[:, lanes] - first
                if causal and block == begin + index:
                    allowed &= line <= own[:, lanes] - first
                part = scores[block * rows : (block + 1) * rows, lanes]
                held[index].append(jnp.where(allowed, part, MASKED))
    return held


def highest(held):
    tops = [functools.reduce(jnp.maximum, [x for x in parts if x is not None]) for parts in held]
    return jnp.concatenate([jnp.max(top, axis=0, keepdims=True) for top in tops], axis=1)


def weigh(held, top):
    totals, rounded = [], []
    for index, parts in enumerate(held):
        rows = next(x for x in parts if x is not None).shape[1]
        here = top[:, index * rows : (index + 1) * rows]
        weights = [None if x is None else jnp.exp2((x - here) * FACTOR) for x in parts]
        total = functools.reduce(jnp.add, [x for x in weights if x is not None])
        totals.append(jnp.sum(total, axis=0, keepdims=True))
        rounded.append(
            [
                jnp.zeros((rows, rows), jnp.bfloat16) if x is None else x.astype(jnp.bfloat16)
                for x in weights
            ]
        )
    lines = [jnp.concatenate(line, axis=1) for line in zip(*rounded)]
    return jnp.concatenate(totals, axis=1), jnp.concatenate(lines, axis=0)


def mix(sets, rounded):
    return dot(jnp.concatenate([one[1] for one in sets], axis=0).T, rounded)


def unit_rows(heads, query_ref, begin):
    rows = query_ref.shape[1] - NOTE_ROWS
    group, _, parity = place(heads)
    starts = []
    for block in range(begin, begin + UNIT):
        note = query_ref[block, rows:, :HD].astype(jnp.float32)
        starts.append(note[0:1] * float(DIGIT) + note[1:2])
    start = jnp.concatenate(starts, axis=1).astype(jnp.int32) - group * (heads * rows)
    line = lax.broadcasted_iota(jnp.int32, (1, UNIT * rows), 1)
    own = line // rows * rows + line + (2 * begin + parity) * rows
    return start, own


def unit_queries(query_ref, head, begin):
    rows = query_ref.shape[1] - NOTE_ROWS
    blocks = range(begin, begin + UNIT)
    columns = slice(head * HD, (head + 1) * HD)
    return jnp.concatenate([query_ref[block, :rows, columns] for block in blocks], axis=0)


FACTOR = math.log2(math.e) / math.sqrt(HD)


def attend_first(heads, query_ref, key_value_ref, top_ref, total_ref, mixed_ref):
    _, _, parity = place(heads)
    for unit in range(heads // 2 // UNIT):
        begin = unit * UNIT
        start, own = unit_rows(heads, query_ref, begin)
        sets = [[key_set(key_value_ref, begin + UNIT, head, 0, parity, True)] for head in range(2)]
        held = [
            masked_scores(sets[head], unit_queries(query_ref, head, begin), start, own, begin)
            for head in range(2)
        ]
        tops = [highest(each) for each in held]
        weights = [weigh(each, top) for each, top in zip(held, tops)]
        for head, (total, rounded) in enumerate(weights):
            top_ref[head, unit] = tops[head]
            total_ref[head, unit] = total
            mixed_ref[head, unit] = mix(sets[head], rounded)


def attend_second(heads, mine, *refs):
    count = heads // 2
    query_ref, top_ref, total_ref, mixed_ref, other_ref, *more = refs[: -UNIT - 1]
    outs, held_ref = refs[-UNIT - 1 : -1], refs[-1]
    more = more[: len(more) // 2 * 2]
    rows = query_ref.shape[1] - NOTE_ROWS
    _, pair, parity = place(heads)
    here = pair // UNIT

    def one_unit(unit):
        begin = unit * UNIT
        start, own = unit_rows(heads, query_ref, begin)
        sets, held, tops = [], [], []
        for head in range(2):
            sets.append([key_set(other_ref, begin + UNIT, head, 0, 1 - parity, True)])
            for ref, side in zip(more, (parity, 1 - parity)):
                sets[head].append(key_set(ref, count, head, -heads * rows, side, False))
            query = unit_queries(query_ref, head, begin)
            held.append(masked_scores(sets[head], query, start, own, begin))
        for head in range(2):
            tops.append(jnp.maximum(top_ref[head, unit], highest(held[head])))
        weights = [weigh(each, top) for each, top in zip(held, tops)]
        for head, (total, rounded) in enumerate(weights):
            columns = slice(head * HD, (head + 1) * HD)
            top = tops[head]
            scale = jnp.exp2((top_ref[head, unit] - top) * FACTOR)
            total = total_ref[head, unit] * scale + total
            mixed = mixed_ref[head, unit] * scale + mix(sets[head], rounded)
            mixed = (mixed * (1.0 / total)).astype(jnp.bfloat16).T
            logs = top * (1.0 / math.sqrt(HD)) + jnp.log(total)
            high = logs.astype(jnp.bfloat16).astype(jnp.float32)
            middle = (logs - high).astype(jnp.bfloat16).astype(jnp.float32)
            low = logs - high - middle
            line = lax.broadcasted_iota(jnp.int32, (NOTE_ROWS, UNIT * rows), 0)
            note = jnp.where(
                line == 0, high, jnp.where(line == 1, middle, jnp.where(line == 2, low, 0.0))
            ).astype(jnp.bfloat16)
            for index in range(UNIT):
                span = slice(index * rows, (index + 1) * rows)
                held_ref[index, :rows, columns] = mixed[span]
                held_ref[index, rows:, columns] = note[:, span]

    for unit in range(count // UNIT):

        @pl.when((here == unit) if mine else (here != unit))
        def _():
            one_unit(unit)

    for step, out in enumerate(outs):
        out[...] = held_ref[lax.rem(pair, UNIT) ^ step]


def unpack_heads(heads, steps, *refs):
    *sources, out_ref, logs_ref = refs
    rows = out_ref.shape[0]
    _, pair, _ = place(heads)
    for step, source in zip(steps, sources):
        owner = pair ^ step
        out_ref[:, pl.ds(pl.multiple_of(owner * (2 * HD), 2 * HD), 2 * HD)] = source[:rows]
        note = source[rows:].astype(jnp.float32)
        logs = note[0:1] + note[1:2] + note[2:3]
        for head in range(2):
            logs_ref[pl.ds(owner * 2 + head, 1), :] = logs[:, head * HD : (head + 1) * HD]


def dot(left, right):
    return jnp.dot(left, right, preferred_element_type=jnp.float32)


def twice(array):
    return jnp.concatenate([array, array], axis=0)


def document_starts(starts_ref, rows):
    return jnp.maximum(starts_ref[...] - lax.axis_index("ctx") * rows, -rows)


def filtered(spectrum, filter_ref, back_ref):
    half = spectrum.shape[0] // 2
    even, odd = spectrum[:half], spectrum[half:]
    tap_even, tap_odd = filter_ref[:half], filter_ref[half:]
    real = (even * tap_even - odd * tap_odd).astype(jnp.bfloat16)
    imag = (even * tap_odd + odd * tap_even).astype(jnp.bfloat16)
    return dot(back_ref[...], jnp.concatenate([real, imag], axis=0))


def convolve(
    heads, other_ref, mine_ref, came_ref, before_ref, own_taps_ref, starts_ref, product_ref, gate_ref, skip_ref,
    early_ref, late_ref, back_ref, out_ref, taps_ref, halo_ref, filter_ref, sum_ref,
):
    rows = product_ref.shape[0]
    height, width = own_taps_ref.shape
    panel = lax.axis_index("tp")
    even = lax.rem(lax.axis_index("ctx"), 2) == 0
    everything = slice(None)

    def store(step, part, value):
        line = pl.ds(pl.multiple_of((panel ^ step) * height, height), height)
        taps_ref[line, part * 2 * HD : (part + 1) * 2 * HD] = value

    parts = width // (2 * HD)
    for part in range(parts):
        line = slice(part * height, (part + 1) * height)
        mine_far, other_far = mine_ref[heads, line], other_ref[heads, line]
        store(0, part, columns_of(own_taps_ref, everything, part))
        store(1, part, jnp.where(even, near_strip(came_ref, height, part), other_ref[heads + 1, line]))
        store(2, part, jnp.where(even, other_far, mine_far))
        store(3, part, jnp.where(even, mine_far, other_far))
        halo_ref[:, part * 2 * HD : (part + 1) * 2 * HD] = jnp.where(
            even,
            columns_of(before_ref, everything, part),
            other_ref[heads + 2] if part == parts - 1 else columns_of(came_ref, everything, part),
        )
    filter_ref[...] = dot(early_ref[...], twice(taps_ref[...]))
    starts = document_starts(starts_ref, rows)
    line = lax.broadcasted_iota(jnp.int32, (rows, 1), 0)
    zero = jnp.zeros((), jnp.bfloat16)

    begin = jnp.min(starts)
    past = jnp.where(line - rows >= begin, halo_ref[...], zero)
    here = jnp.where(line >= begin, product_ref[...], zero)
    spectrum = dot(early_ref[...], twice(past)) + dot(late_ref[...], twice(here))
    sum_ref[...] = filtered(spectrum, filter_ref, back_ref)

    def one_document(begin):
        here = jnp.where(line >= begin, product_ref[...], zero)
        result = filtered(dot(late_ref[...], twice(here)), filter_ref, back_ref)
        sum_ref[...] = jnp.where(line >= begin, result, sum_ref[...])
        return jnp.min(jnp.where(starts > begin, starts, rows))

    second = jnp.min(jnp.where(starts > begin, starts, rows))
    lax.while_loop(lambda begin: begin < rows, one_document, second)
    out_ref[...] = (
        gate_ref[0].astype(jnp.float32)
        * (skip_ref[...] * product_ref[...].astype(jnp.float32) + sum_ref[...])
    ).astype(jnp.bfloat16)


def twiddles(rows):
    window = 2 * rows
    order = np.arange(rows)[:, None] * 2 + 1
    angle = np.pi * ((order * np.arange(window)[None, :]) % (2 * window)) / window
    ahead = np.concatenate([np.cos(angle), -np.sin(angle)], axis=0)
    back = ahead.T[rows:] / rows
    return jnp.asarray(ahead, jnp.float32), jnp.asarray(back, jnp.float32)


def side_pairs(peers, panels):
    assert panels == 4
    far, mixed = [], []
    for peer in range(peers):
        for panel in range(panels):
            here = peer * panels + panel
            far.append((here, peer * panels + (panel ^ (3 - peer % 2))))
            if peer % 2 == 0:
                mixed.append((here, here + panels))
            else:
                mixed.append((here, (peer - 1) * panels + (panel ^ 1)))
    return far, mixed


def local(hyena_inputs, filters, skip_bias, queries, keys_values, doc_start):
    rows = queries.shape[0]
    channels = hyena_inputs.shape[2]
    heads = queries.shape[1] // HD
    count = heads // 2
    peers = lax.axis_size("ctx")
    bf16, f32 = jnp.bfloat16, jnp.float32
    shape = jax.ShapeDtypeStruct
    starts = doc_start.reshape(1, rows)

    height = filters.shape[0]

    def pinned(*arrays):
        return [pltpu.with_memory_space_constraint(x, pltpu.HBM) for x in arrays]

    *packed, wide_taps = call(
        functools.partial(pack_heads, heads),
        (shape((3 * rows + NOTE_ROWS, 2 * HD), bf16),) * count + (shape((3, height, channels), f32),),
        pinned(queries, keys_values, starts, filters),
        0,
        4 * queries.size * 3,
        scratch=(
            pltpu.VMEM((1, rows), jnp.int32),
            pltpu.SemaphoreType.DMA,
            pltpu.SemaphoreType.DMA((3,)),
            pltpu.SemaphoreType.DMA((count, 3)),
        ),
        specs=[hbm()] * 4,
    )
    arrived = [packed[0]] + [crossed(packed[step], "ctx", 2 * step) for step in range(1, count)]
    product, own_taps, far_taps, mixed_rows = call(
        pack_hyena,
        (shape((rows, channels), bf16),)
        + (shape((height, channels), bf16),) * 2
        + (shape((rows, channels - 2 * HD), bf16),),
        (hyena_inputs, wide_taps),
        0,
        4 * queries.size * 3,
    )
    axes = ("ctx", "tp")
    far_pairs, mixed_pairs = side_pairs(peers, lax.axis_size("tp"))
    far_taps = lax.ppermute(far_taps, axes, far_pairs)
    came = lax.ppermute(mixed_rows, axes, mixed_pairs)
    halo_pairs = [pair for i in range(1, peers - 1, 2) for pair in ((i, i + 1), (i + 1, i))]
    before = lax.ppermute(product, "ctx", halo_pairs)
    ahead, back = twiddles(rows)
    early, late, back, near_starts, skip = call(
        prepare,
        (shape((2 * rows, 2 * rows), bf16),) * 2
        + (shape((rows, 2 * rows), bf16), shape((1, rows), jnp.int32), shape((1, channels), f32)),
        pinned(ahead, back, starts, skip_bias.reshape(1, channels)),
        0,
        4 * queries.size,
        scratch=(
            pltpu.VMEM((2 * rows, 2 * rows), f32),
            pltpu.VMEM((rows, 2 * rows), f32),
            pltpu.SemaphoreType.DMA((4,)),
        ),
        specs=[hbm()] * 4,
    )

    query, key_value = call(
        functools.partial(sort_heads, heads),
        (
            shape((count, rows + NOTE_ROWS, 2 * HD), bf16),
            shape((heads + 3, rows, 2 * HD), bf16),
        ),
        (*arrived, far_taps, came, product, skip),
        0,
        4 * queries.size * 3,
    )
    other = crossed(key_value, "ctx", 1)
    units = count // UNIT
    partial = call(
        functools.partial(attend_first, heads),
        (
            shape((2, units, 1, UNIT * rows), f32),
            shape((2, units, 1, UNIT * rows), f32),
            shape((2, units, HD, UNIT * rows), f32),
        ),
        (query, key_value),
        2 * (heads * rows) ** 2 * HD,
        4 * queries.size * 4,
    )
    operands = [query, *partial, other]
    if peers > heads:
        pairs = [(i, i + heads) for i in range(peers - heads)]
        operands += [lax.ppermute(each, "ctx", pairs) for each in (key_value, other)]
    assert count == 2 * UNIT
    message = shape((rows + NOTE_ROWS, 2 * HD), bf16)

    def second(mine, *more):
        return call(
            functools.partial(attend_second, heads, mine),
            (message,) * UNIT,
            (*operands, *more),
            (heads * rows) ** 2 * HD,
            4 * queries.size * 4,
            scratch=(pltpu.VMEM((UNIT, rows + NOTE_ROWS, 2 * HD), bf16),),
        )

    theirs = second(False)
    own = second(True, theirs[0])
    returned = [own[0], crossed(theirs[0], "ctx", 4), crossed(theirs[1], "ctx", 6)]
    returned.append(crossed(own[1], "ctx", 2))
    hyena_out = call(
        functools.partial(convolve, heads),
        shape((rows, channels), bf16),
        (
            other, key_value, came, before, own_taps, near_starts, product, hyena_inputs,
            skip, early, late, back,
        ),
        2 * 4 * 256 * 256 * channels,
        4 * queries.size * 4,
        scratch=(
            pltpu.VMEM((FLEN, channels), bf16),
            pltpu.VMEM((rows, channels), bf16),
            pltpu.VMEM((2 * rows, channels), f32),
            pltpu.VMEM((rows, channels), f32),
        ),
    )
    attention_out, log_totals = call(
        functools.partial(unpack_heads, heads, (0, 2, 3, 1)),
        (shape((rows, heads * HD), bf16), shape((heads, rows), f32)),
        returned,
        0,
        4 * queries.size,
    )
    return (hyena_out, attention_out, log_totals)


def solution(mesh):
    in_specs = (
        P(None, "ctx", "tp"),
        P("tp", None),
        P("tp"),
        P("ctx", "tp"),
        P(None, "ctx", "tp"),
        P("ctx"),
    )
    out_specs = (P("ctx", "tp"), P("ctx", "tp"), P("tp", "ctx"))
    return jax.shard_map(local, mesh=mesh, in_specs=in_specs, out_specs=out_specs, check_vma=False)
```

```python
import functools
import math

import jax
import jax.numpy as jnp
import numpy as np
from jax import lax
from jax.experimental import pallas as pl
from jax.experimental.pallas import tpu as pltpu
from jax.sharding import PartitionSpec as P

HD = 128
FLEN = 128
DIGIT = 256
NOTE_ROWS = 16
MASKED = -1e30
VMEM_LIMIT = 16 * 1024 * 1024
LONG = 200


def vmem():
    return pl.BlockSpec(memory_space=pltpu.VMEM)


def hbm():
    return pl.BlockSpec(memory_space=pltpu.HBM)


def call(kernel, out_shape, args, flops, nbytes, scratch=(), specs=None):
    return pl.pallas_call(
        kernel,
        out_shape=out_shape,
        in_specs=specs or [vmem() for _ in args],
        out_specs=jax.tree.map(lambda _: vmem(), out_shape),
        scratch_shapes=list(scratch),
        compiler_params=pltpu.CompilerParams(vmem_limit_bytes=VMEM_LIMIT),
        cost_estimate=pl.CostEstimate(flops=flops, bytes_accessed=nbytes, transcendentals=0),
    )(*args)


def crossed(array, axis, bits):
    return lax.ppermute(array, axis, [(i, i ^ bits) for i in range(lax.axis_size(axis))])


def place(heads):
    index = lax.axis_index("ctx")
    member = lax.rem(index, heads)
    return index // heads, member // 2, lax.rem(member, 2)


def pack_heads(heads, queries_ref, keys_values_ref, starts_ref, filters_ref, *refs):
    *outs, taps_ref, held_ref, start_sem, taps_sem, sem = refs
    rows = queries_ref.shape[0]
    _, pair, _ = place(heads)
    first = pltpu.make_async_copy(starts_ref, held_ref, start_sem)
    first.start()
    copies = []
    for step, out in enumerate(outs):
        columns = pl.ds(pl.multiple_of((pair ^ step) * (2 * HD), 2 * HD), 2 * HD)
        for part, source in enumerate((queries_ref, keys_values_ref)):
            copies.append(
                pltpu.make_async_copy(
                    source.at[:, columns],
                    out.at[pl.ds(part * rows, source.shape[0])],
                    sem.at[step, part],
                )
            )
    width = taps_ref.shape[2]
    panel = lax.axis_index("tp")
    for index, target in enumerate((panel, panel ^ (3 - lax.rem(lax.axis_index("ctx"), 2)), panel ^ 1)):
        columns = pl.ds(pl.multiple_of(target * width, width), width)
        copies.append(
            pltpu.make_async_copy(
                filters_ref.at[:, columns], taps_ref.at[index], taps_sem.at[index]
            )
        )
    for copy in copies:
        copy.start()
    first.wait()
    starts = held_ref[...]
    high = (starts // DIGIT).astype(jnp.float32)
    low = (starts % DIGIT).astype(jnp.float32)
    line = lax.broadcasted_iota(jnp.int32, (NOTE_ROWS, rows), 0)
    note = jnp.where(line == 0, high, jnp.where(line == 1, low, 0.0)).astype(jnp.bfloat16)
    for out in outs:
        out[3 * rows :, :HD] = note
        out[3 * rows :, HD:] = note
    for copy in copies:
        copy.wait()


def split(matrix):
    high = matrix.astype(jnp.bfloat16)
    low = (matrix - high.astype(jnp.float32)).astype(jnp.bfloat16)
    return jnp.concatenate([high, low], axis=1)


def pack_hyena(hyena_ref, taps_ref, product_ref, own_ref, far_ref, mixed_ref):
    product_ref[...] = (hyena_ref[1].astype(jnp.float32) * hyena_ref[2].astype(jnp.float32)).astype(
        jnp.bfloat16
    )
    own_ref[...] = taps_ref[0].astype(jnp.bfloat16)
    far_ref[...] = taps_ref[1].astype(jnp.bfloat16)
    height, width = own_ref.shape
    whole = mixed_ref.shape[1]
    mixed_ref[...] = product_ref[:, :whole]

    @pl.when(lax.rem(lax.axis_index("ctx"), 2) == 1)
    def _():
        near = taps_ref[2].astype(jnp.bfloat16)
        mixed_ref[:height] = near[:, :whole]
        mixed_ref[height : 2 * height, : width - whole] = near[:, whole:]


def prepare(
    ahead_ref, back_ref, starts_ref, skip_ref, early_ref, late_ref, back_out, starts_out, skip_out,
    ahead_held, back_held, sem,
):
    pairs = (
        (ahead_ref, ahead_held), (back_ref, back_held), (starts_ref, starts_out), (skip_ref, skip_out)
    )
    copies = [
        pltpu.make_async_copy(source, out, sem.at[index])
        for index, (source, out) in enumerate(pairs)
    ]
    for copy in copies:
        copy.start()
    for copy in copies:
        copy.wait()
    rows = back_out.shape[0]
    early_ref[...] = split(ahead_held[:, :rows])
    late_ref[...] = split(ahead_held[:, rows:])
    back_out[...] = back_held[...].astype(jnp.bfloat16)


def columns_of(ref, rows, index):
    return ref[rows, index * 2 * HD : (index + 1) * 2 * HD]


def near_strip(came_ref, height, part):
    parts = came_ref.shape[1] // (2 * HD)
    line = part // parts
    return columns_of(came_ref, slice(line * height, (line + 1) * height), part % parts)


def sort_heads(heads, *refs):
    count = heads // 2
    far_ref, came_ref, product_ref = refs[count : count + 3]
    query_ref, side_ref = refs[-2:]
    rows = (refs[0].shape[0] - NOTE_ROWS) // 3
    _, pair, _ = place(heads)
    for step in range(count):
        source = pair ^ step
        query_ref[source, :rows] = refs[step][:rows]
        query_ref[source, rows:] = refs[step][3 * rows :]
        side_ref[2 * source] = refs[step][rows : 2 * rows]
        side_ref[2 * source + 1] = refs[step][2 * rows : 3 * rows]
    height, width = far_ref.shape
    parts = width // (2 * HD)
    for part in range(parts):
        line = slice(part * height, (part + 1) * height)
        side_ref[heads, line] = columns_of(far_ref, slice(None), part)
        side_ref[heads + 1, line] = near_strip(came_ref, height, part)
    side_ref[heads + 2] = columns_of(product_ref, slice(None), parts - 1)


UNIT = 2


def key_set(ref, blocks, head, origin, parity, causal):
    columns = slice(head * HD, (head + 1) * HD)
    rows = ref.shape[1]
    key = jnp.concatenate([ref[2 * block, :, columns] for block in range(blocks)], axis=0)
    value = jnp.concatenate([ref[2 * block + 1, :, columns] for block in range(blocks)], axis=0)
    return key, value, [(2 * block + parity) * rows + origin for block in range(blocks)], causal


def masked_scores(sets, query, start, own, begin):
    held = [[] for _ in range(UNIT)]
    for key, _, firsts, causal in sets:
        scores = lax.dot_general(
            key, query, (((1,), (1,)), ((), ())), preferred_element_type=jnp.float32
        )
        rows = key.shape[0] // len(firsts)
        line = lax.broadcasted_iota(jnp.int32, (rows, rows), 0)
        for block, first in enumerate(firsts):
            for index in range(UNIT):
                if causal and block > begin + index:
                    held[index].append(None)
                    continue
                lanes = slice(index * rows, (index + 1) * rows)
                allowed = line >= start[:, lanes] - first
                if causal and block == begin + index:
                    allowed &= line <= own[:, lanes] - first
                part = scores[block * rows : (block + 1) * rows, lanes]
                held[index].append(jnp.where(allowed, part, MASKED))
    return held


def highest(held):
    tops = [functools.reduce(jnp.maximum, [x for x in parts if x is not None]) for parts in held]
    return jnp.concatenate([jnp.max(top, axis=0, keepdims=True) for top in tops], axis=1)


def weigh(held, top):
    totals, rounded = [], []
    for index, parts in enumerate(held):
        rows = next(x for x in parts if x is not None).shape[1]
        here = top[:, index * rows : (index + 1) * rows]
        weights = [None if x is None else jnp.exp2((x - here) * FACTOR) for x in parts]
        total = functools.reduce(jnp.add, [x for x in weights if x is not None])
        totals.append(jnp.sum(total, axis=0, keepdims=True))
        rounded.append(
            [
                jnp.zeros((rows, rows), jnp.bfloat16) if x is None else x.astype(jnp.bfloat16)
                for x in weights
            ]
        )
    lines = [jnp.concatenate(line, axis=1) for line in zip(*rounded)]
    return jnp.concatenate(totals, axis=1), jnp.concatenate(lines, axis=0)


def mix(sets, rounded):
    return dot(jnp.concatenate([one[1] for one in sets], axis=0).T, rounded)


def unit_rows(heads, query_ref, begin):
    rows = query_ref.shape[1] - NOTE_ROWS
    group, _, parity = place(heads)
    starts = []
    for block in range(begin, begin + UNIT):
        note = query_ref[block, rows:, :HD].astype(jnp.float32)
        starts.append(note[0:1] * float(DIGIT) + note[1:2])
    start = jnp.concatenate(starts, axis=1).astype(jnp.int32) - group * (heads * rows)
    line = lax.broadcasted_iota(jnp.int32, (1, UNIT * rows), 1)
    own = line // rows * rows + line + (2 * begin + parity) * rows
    return start, own


def unit_queries(query_ref, head, begin):
    rows = query_ref.shape[1] - NOTE_ROWS
    blocks = range(begin, begin + UNIT)
    columns = slice(head * HD, (head + 1) * HD)
    return jnp.concatenate([query_ref[block, :rows, columns] for block in blocks], axis=0)


FACTOR = math.log2(math.e) / math.sqrt(HD)


def attend_first(heads, query_ref, key_value_ref, top_ref, total_ref, mixed_ref):
    _, _, parity = place(heads)
    for unit in range(heads // 2 // UNIT):
        begin = unit * UNIT
        start, own = unit_rows(heads, query_ref, begin)
        sets = [[key_set(key_value_ref, begin + UNIT, head, 0, parity, True)] for head in range(2)]
        held = [
            masked_scores(sets[head], unit_queries(query_ref, head, begin), start, own, begin)
            for head in range(2)
        ]
        tops = [highest(each) for each in held]
        weights = [weigh(each, top) for each, top in zip(held, tops)]
        for head, (total, rounded) in enumerate(weights):
            top_ref[head, unit] = tops[head]
            total_ref[head, unit] = total
            mixed_ref[head, unit] = mix(sets[head], rounded)


def attend_second(heads, mine, *refs):
    count = heads // 2
    query_ref, top_ref, total_ref, mixed_ref, other_ref, *more = refs[: -UNIT - 1]
    outs, held_ref = refs[-UNIT - 1 : -1], refs[-1]
    more = more[: len(more) // 2 * 2]
    rows = query_ref.shape[1] - NOTE_ROWS
    _, pair, parity = place(heads)
    here = pair // UNIT

    def one_unit(unit):
        begin = unit * UNIT
        start, own = unit_rows(heads, query_ref, begin)
        sets, held, tops = [], [], []
        for head in range(2):
            sets.append([key_set(other_ref, begin + UNIT, head, 0, 1 - parity, True)])
            for ref, side in zip(more, (parity, 1 - parity)):
                sets[head].append(key_set(ref, count, head, -heads * rows, side, False))
            query = unit_queries(query_ref, head, begin)
            held.append(masked_scores(sets[head], query, start, own, begin))
        for head in range(2):
            tops.append(jnp.maximum(top_ref[head, unit], highest(held[head])))
        weights = [weigh(each, top) for each, top in zip(held, tops)]
        for head, (total, rounded) in enumerate(weights):
            columns = slice(head * HD, (head + 1) * HD)
            top = tops[head]
            scale = jnp.exp2((top_ref[head, unit] - top) * FACTOR)
            total = total_ref[head, unit] * scale + total
            mixed = mixed_ref[head, unit] * scale + mix(sets[head], rounded)
            mixed = (mixed * (1.0 / total)).astype(jnp.bfloat16).T
            logs = top * (1.0 / math.sqrt(HD)) + jnp.log(total)
            high = logs.astype(jnp.bfloat16).astype(jnp.float32)
            middle = (logs - high).astype(jnp.bfloat16).astype(jnp.float32)
            low = logs - high - middle
            line = lax.broadcasted_iota(jnp.int32, (NOTE_ROWS, UNIT * rows), 0)
            note = jnp.where(
                line == 0, high, jnp.where(line == 1, middle, jnp.where(line == 2, low, 0.0))
            ).astype(jnp.bfloat16)
            for index in range(UNIT):
                span = slice(index * rows, (index + 1) * rows)
                held_ref[index, :rows, columns] = mixed[span]
                held_ref[index, rows:, columns] = note[:, span]

    for unit in range(count // UNIT):

        @pl.when((here == unit) if mine else (here != unit))
        def _():
            one_unit(unit)

    for step, out in enumerate(outs):
        out[...] = held_ref[lax.rem(pair, UNIT) ^ step]


def unpack_heads(heads, steps, *refs):
    *sources, out_ref, logs_ref = refs
    rows = out_ref.shape[0]
    _, pair, _ = place(heads)
    for step, source in zip(steps, sources):
        owner = pair ^ step
        out_ref[:, pl.ds(pl.multiple_of(owner * (2 * HD), 2 * HD), 2 * HD)] = source[:rows]
        note = source[rows:].astype(jnp.float32)
        logs = note[0:1] + note[1:2] + note[2:3]
        for head in range(2):
            logs_ref[pl.ds(owner * 2 + head, 1), :] = logs[:, head * HD : (head + 1) * HD]


def dot(left, right):
    return jnp.dot(left, right, preferred_element_type=jnp.float32)


def twice(array):
    return jnp.concatenate([array, array], axis=0)


def document_starts(starts_ref, rows):
    return jnp.maximum(starts_ref[...] - lax.axis_index("ctx") * rows, -rows)


def filtered(spectrum, filter_ref, back_ref):
    half = spectrum.shape[0] // 2
    even, odd = spectrum[:half], spectrum[half:]
    tap_even, tap_odd = filter_ref[:half], filter_ref[half:]
    real = (even * tap_even - odd * tap_odd).astype(jnp.bfloat16)
    imag = (even * tap_odd + odd * tap_even).astype(jnp.bfloat16)
    return dot(back_ref[...], jnp.concatenate([real, imag], axis=0))


def convolve(
    heads, other_ref, mine_ref, came_ref, before_ref, own_taps_ref, starts_ref, product_ref, gate_ref, skip_ref,
    early_ref, late_ref, back_ref, out_ref, taps_ref, halo_ref, filter_ref, sum_ref,
):
    rows = product_ref.shape[0]
    height, width = own_taps_ref.shape
    panel = lax.axis_index("tp")
    even = lax.rem(lax.axis_index("ctx"), 2) == 0
    everything = slice(None)

    def store(step, part, value):
        line = pl.ds(pl.multiple_of((panel ^ step) * height, height), height)
        taps_ref[line, part * 2 * HD : (part + 1) * 2 * HD] = value

    parts = width // (2 * HD)
    for part in range(parts):
        line = slice(part * height, (part + 1) * height)
        mine_far, other_far = mine_ref[heads, line], other_ref[heads, line]
        store(0, part, columns_of(own_taps_ref, everything, part))
        store(1, part, jnp.where(even, near_strip(came_ref, height, part), other_ref[heads + 1, line]))
        store(2, part, jnp.where(even, other_far, mine_far))
        store(3, part, jnp.where(even, mine_far, other_far))
        halo_ref[:, part * 2 * HD : (part + 1) * 2 * HD] = jnp.where(
            even,
            columns_of(before_ref, everything, part),
            other_ref[heads + 2] if part == parts - 1 else columns_of(came_ref, everything, part),
        )
    filter_ref[...] = dot(early_ref[...], twice(taps_ref[...]))
    starts = document_starts(starts_ref, rows)
    line = lax.broadcasted_iota(jnp.int32, (rows, 1), 0)
    zero = jnp.zeros((), jnp.bfloat16)

    begin = jnp.min(starts)
    past = jnp.where(line - rows >= begin, halo_ref[...], zero)
    here = jnp.where(line >= begin, product_ref[...], zero)
    spectrum = dot(early_ref[...], twice(past)) + dot(late_ref[...], twice(here))
    sum_ref[...] = filtered(spectrum, filter_ref, back_ref)

    def one_document(begin):
        here = jnp.where(line >= begin, product_ref[...], zero)
        result = filtered(dot(late_ref[...], twice(here)), filter_ref, back_ref)
        sum_ref[...] = jnp.where(line >= begin, result, sum_ref[...])
        return jnp.min(jnp.where(starts > begin, starts, rows))

    second = jnp.min(jnp.where(starts > begin, starts, rows))
    lax.while_loop(lambda begin: begin < rows, one_document, second)
    out_ref[...] = (
        gate_ref[0].astype(jnp.float32)
        * (skip_ref[...] * product_ref[...].astype(jnp.float32) + sum_ref[...])
    ).astype(jnp.bfloat16)


def twiddles(rows):
    window = 2 * rows
    order = np.arange(rows)[:, None] * 2 + 1
    angle = np.pi * ((order * np.arange(window)[None, :]) % (2 * window)) / window
    ahead = np.concatenate([np.cos(angle), -np.sin(angle)], axis=0)
    back = ahead.T[rows:] / rows
    return jnp.asarray(ahead, jnp.float32), jnp.asarray(back, jnp.float32)


def side_pairs(peers, panels):
    assert panels == 4
    far, mixed = [], []
    for peer in range(peers):
        for panel in range(panels):
            here = peer * panels + panel
            far.append((here, peer * panels + (panel ^ (3 - peer % 2))))
            if peer % 2 == 0:
                mixed.append((here, here + panels))
            else:
                mixed.append((here, (peer - 1) * panels + (panel ^ 1)))
    return far, mixed


def local(hyena_inputs, filters, skip_bias, queries, keys_values, doc_start):
    rows = queries.shape[0]
    channels = hyena_inputs.shape[2]
    heads = queries.shape[1] // HD
    count = heads // 2
    peers = lax.axis_size("ctx")
    bf16, f32 = jnp.bfloat16, jnp.float32
    shape = jax.ShapeDtypeStruct
    starts = doc_start.reshape(1, rows)

    height = filters.shape[0]

    def pinned(*arrays):
        return [pltpu.with_memory_space_constraint(x, pltpu.HBM) for x in arrays]

    *packed, wide_taps = call(
        functools.partial(pack_heads, heads),
        (shape((3 * rows + NOTE_ROWS, 2 * HD), bf16),) * count + (shape((3, height, channels), f32),),
        pinned(queries, keys_values.reshape(2 * rows, heads * HD), starts, filters),
        0,
        4 * queries.size * 3,
        scratch=(
            pltpu.VMEM((1, rows), jnp.int32),
            pltpu.SemaphoreType.DMA,
            pltpu.SemaphoreType.DMA((3,)),
            pltpu.SemaphoreType.DMA((count, 2)),
        ),
        specs=[hbm()] * 4,
    )
    arrived = [packed[0]] + [crossed(packed[step], "ctx", 2 * step) for step in range(1, count)]
    product, own_taps, far_taps, mixed_rows = call(
        pack_hyena,
        (shape((rows, channels), bf16),)
        + (shape((height, channels), bf16),) * 2
        + (shape((rows, channels - 2 * HD), bf16),),
        (hyena_inputs, wide_taps),
        0,
        4 * queries.size * 3,
    )
    axes = ("ctx", "tp")
    far_pairs, mixed_pairs = side_pairs(peers, lax.axis_size("tp"))
    far_taps = lax.ppermute(far_taps, axes, far_pairs)
    came = lax.ppermute(mixed_rows, axes, mixed_pairs)
    before = lax.ppermute(product, "ctx", [(i, i + 1) for i in range(1, peers - 1, 2)])
    ahead, back = twiddles(rows)
    early, late, back, near_starts, skip = call(
        prepare,
        (shape((2 * rows, 2 * rows), bf16),) * 2
        + (shape((rows, 2 * rows), bf16), shape((1, rows), jnp.int32), shape((1, channels), f32)),
        pinned(ahead, back, starts, skip_bias.reshape(1, channels)),
        0,
        4 * queries.size,
        scratch=(
            pltpu.VMEM((2 * rows, 2 * rows), f32),
            pltpu.VMEM((rows, 2 * rows), f32),
            pltpu.SemaphoreType.DMA((4,)),
        ),
        specs=[hbm()] * 4,
    )

    query, key_value = call(
        functools.partial(sort_heads, heads),
        (
            shape((count, rows + NOTE_ROWS, 2 * HD), bf16),
            shape((heads + 3, rows, 2 * HD), bf16),
        ),
        (*arrived, far_taps, came, product, skip),
        0,
        4 * queries.size * 3,
    )
    other = crossed(key_value, "ctx", 1)
    units = count // UNIT
    partial = call(
        functools.partial(attend_first, heads),
        (
            shape((2, units, 1, UNIT * rows), f32),
            shape((2, units, 1, UNIT * rows), f32),
            shape((2, units, HD, UNIT * rows), f32),
        ),
        (query, key_value),
        LONG * (heads * rows) ** 2 * HD,
        4 * queries.size * 4,
    )
    operands = [query, *partial, other]
    if peers > heads:
        pairs = [(i, i + heads) for i in range(peers - heads)]
        operands += [lax.ppermute(each, "ctx", pairs) for each in (key_value, other)]
    assert count == 2 * UNIT
    message = shape((rows + NOTE_ROWS, 2 * HD), bf16)

    def second(mine, *more):
        return call(
            functools.partial(attend_second, heads, mine),
            (message,) * UNIT,
            (*operands, *more),
            (heads * rows) ** 2 * HD,
            4 * queries.size * 4,
            scratch=(pltpu.VMEM((UNIT, rows + NOTE_ROWS, 2 * HD), bf16),),
        )

    theirs = second(False)
    own = second(True, theirs[0])
    returned = [own[0], crossed(theirs[0], "ctx", 4), crossed(theirs[1], "ctx", 6)]
    returned.append(crossed(own[1], "ctx", 2))
    hyena_out = call(
        functools.partial(convolve, heads),
        shape((rows, channels), bf16),
        (
            other, key_value, came, before, own_taps, near_starts, product, hyena_inputs,
            skip, early, late, back,
        ),
        2 * 4 * 256 * 256 * channels,
        4 * queries.size * 4,
        scratch=(
            pltpu.VMEM((FLEN, channels), bf16),
            pltpu.VMEM((rows, channels), bf16),
            pltpu.VMEM((2 * rows, channels), f32),
            pltpu.VMEM((rows, channels), f32),
        ),
    )
    attention_out, log_totals = call(
        functools.partial(unpack_heads, heads, (0, 2, 3, 1)),
        (shape((rows, heads * HD), bf16), shape((heads, rows), f32)),
        returned,
        0,
        4 * queries.size,
    )
    return (hyena_out, attention_out, log_totals)


def solution(mesh):
    in_specs = (
        P(None, "ctx", "tp"),
        P("tp", None),
        P("tp"),
        P("ctx", "tp"),
        P(None, "ctx", "tp"),
        P("ctx"),
    )
    out_specs = (P("ctx", "tp"), P("ctx", "tp"), P("tp", "ctx"))
    return jax.shard_map(local, mesh=mesh, in_specs=in_specs, out_specs=out_specs, check_vma=False)
```

```python
import functools
import math

import jax
import jax.numpy as jnp
import numpy as np
from jax import lax
from jax.experimental import pallas as pl
from jax.experimental.pallas import tpu as pltpu
from jax.sharding import PartitionSpec as P

HD = 128
FLEN = 128
DIGIT = 256
NOTE_ROWS = 16
MASKED = -1e30
VMEM_LIMIT = 16 * 1024 * 1024


def vmem():
    return pl.BlockSpec(memory_space=pltpu.VMEM)


def hbm():
    return pl.BlockSpec(memory_space=pltpu.HBM)


def call(kernel, out_shape, args, flops, nbytes, scratch=(), specs=None):
    return pl.pallas_call(
        kernel,
        out_shape=out_shape,
        in_specs=specs or [vmem() for _ in args],
        out_specs=jax.tree.map(lambda _: vmem(), out_shape),
        scratch_shapes=list(scratch),
        compiler_params=pltpu.CompilerParams(vmem_limit_bytes=VMEM_LIMIT),
        cost_estimate=pl.CostEstimate(flops=flops, bytes_accessed=nbytes, transcendentals=0),
    )(*args)


def crossed(array, axis, bits):
    return lax.ppermute(array, axis, [(i, i ^ bits) for i in range(lax.axis_size(axis))])


def place(heads):
    index = lax.axis_index("ctx")
    member = lax.rem(index, heads)
    return index // heads, member // 2, lax.rem(member, 2)


def pack_heads(heads, queries_ref, keys_values_ref, starts_ref, filters_ref, *refs):
    *outs, taps_ref, held_ref, start_sem, taps_sem, sem = refs
    rows = queries_ref.shape[0]
    _, pair, _ = place(heads)
    first = pltpu.make_async_copy(starts_ref, held_ref, start_sem)
    first.start()
    copies = []
    for step, out in enumerate(outs):
        for head in range(2):
            columns = pl.ds(pl.multiple_of(((pair ^ step) * 2 + head) * HD, HD), HD)
            first_row = head * 3 * rows
            for part, source in enumerate((queries_ref, keys_values_ref)):
                lines = pl.ds(first_row + part * rows, source.shape[0])
                copies.append(
                    pltpu.make_async_copy(
                        source.at[:, columns], out.at[lines], sem.at[step, 2 * head + part]
                    )
                )
    width = taps_ref.shape[2]
    panel = lax.axis_index("tp")
    for index, target in enumerate((panel, panel ^ (3 - lax.rem(lax.axis_index("ctx"), 2)), panel ^ 1)):
        columns = pl.ds(pl.multiple_of(target * width, width), width)
        copies.append(
            pltpu.make_async_copy(
                filters_ref.at[:, columns], taps_ref.at[index], taps_sem.at[index]
            )
        )
    for copy in copies:
        copy.start()
    first.wait()
    starts = held_ref[...]
    high = (starts // DIGIT).astype(jnp.float32)
    low = (starts % DIGIT).astype(jnp.float32)
    line = lax.broadcasted_iota(jnp.int32, (NOTE_ROWS, rows), 0)
    note = jnp.where(line == 0, high, jnp.where(line == 1, low, 0.0)).astype(jnp.bfloat16)
    for out in outs:
        out[6 * rows :] = note
    for copy in copies:
        copy.wait()


def split(matrix):
    high = matrix.astype(jnp.bfloat16)
    low = (matrix - high.astype(jnp.float32)).astype(jnp.bfloat16)
    return jnp.concatenate([high, low], axis=1)


def pack_hyena(hyena_ref, taps_ref, product_ref, own_ref, far_ref, mixed_ref):
    product_ref[...] = (hyena_ref[1].astype(jnp.float32) * hyena_ref[2].astype(jnp.float32)).astype(
        jnp.bfloat16
    )
    own_ref[...] = taps_ref[0].astype(jnp.bfloat16)
    far_ref[...] = taps_ref[1].astype(jnp.bfloat16)
    height, width = own_ref.shape
    whole = mixed_ref.shape[1]
    mixed_ref[...] = product_ref[:, :whole]

    @pl.when(lax.rem(lax.axis_index("ctx"), 2) == 1)
    def _():
        near = taps_ref[2].astype(jnp.bfloat16)
        mixed_ref[:height] = near[:, :whole]
        mixed_ref[height : 2 * height, : width - whole] = near[:, whole:]


def prepare(
    ahead_ref, back_ref, starts_ref, skip_ref, early_ref, late_ref, back_out, starts_out, skip_out,
    ahead_held, back_held, sem,
):
    pairs = (
        (ahead_ref, ahead_held), (back_ref, back_held), (starts_ref, starts_out), (skip_ref, skip_out)
    )
    copies = [
        pltpu.make_async_copy(source, out, sem.at[index])
        for index, (source, out) in enumerate(pairs)
    ]
    for copy in copies:
        copy.start()
    for copy in copies:
        copy.wait()
    rows = back_out.shape[0]
    early_ref[...] = split(ahead_held[:, :rows])
    late_ref[...] = split(ahead_held[:, rows:])
    back_out[...] = back_held[...].astype(jnp.bfloat16)


def columns_of(ref, rows, index):
    return ref[rows, index * 2 * HD : (index + 1) * 2 * HD]


def near_strip(came_ref, height, part):
    parts = came_ref.shape[1] // (2 * HD)
    line = part // parts
    return columns_of(came_ref, slice(line * height, (line + 1) * height), part % parts)


def sort_heads(heads, *refs):
    count = heads // 2
    far_ref, came_ref, product_ref = refs[count : count + 3]
    query_ref, side_ref = refs[-2:]
    rows = (refs[0].shape[0] - NOTE_ROWS) // 6
    _, pair, _ = place(heads)
    for step in range(count):
        source = pair ^ step
        query_ref[source, rows:, :HD] = refs[step][6 * rows :]
        for head in range(2):
            columns = slice(head * HD, (head + 1) * HD)
            first = head * 3 * rows
            query_ref[source, :rows, columns] = refs[step][first : first + rows]
            for part in range(2):
                line = first + (part + 1) * rows
                side_ref[2 * source + part, :, columns] = refs[step][line : line + rows]
    height, width = far_ref.shape
    parts = width // (2 * HD)
    for part in range(parts):
        line = slice(part * height, (part + 1) * height)
        side_ref[heads, line] = columns_of(far_ref, slice(None), part)
        side_ref[heads + 1, line] = near_strip(came_ref, height, part)
    side_ref[heads + 2] = columns_of(product_ref, slice(None), parts - 1)


UNIT = 2


def key_set(ref, blocks, head, origin, parity, causal):
    columns = slice(head * HD, (head + 1) * HD)
    rows = ref.shape[1]
    key = jnp.concatenate([ref[2 * block, :, columns] for block in range(blocks)], axis=0)
    value = jnp.concatenate([ref[2 * block + 1, :, columns] for block in range(blocks)], axis=0)
    return key, value, [(2 * block + parity) * rows + origin for block in range(blocks)], causal


def masked_scores(sets, query, start, own, begin):
    held = [[] for _ in range(UNIT)]
    for key, _, firsts, causal in sets:
        scores = lax.dot_general(
            key, query, (((1,), (1,)), ((), ())), preferred_element_type=jnp.float32
        )
        rows = key.shape[0] // len(firsts)
        line = lax.broadcasted_iota(jnp.int32, (rows, rows), 0)
        for block, first in enumerate(firsts):
            for index in range(UNIT):
                if causal and block > begin + index:
                    held[index].append(None)
                    continue
                lanes = slice(index * rows, (index + 1) * rows)
                allowed = line >= start[:, lanes] - first
                if causal and block == begin + index:
                    allowed &= line <= own[:, lanes] - first
                part = scores[block * rows : (block + 1) * rows, lanes]
                held[index].append(jnp.where(allowed, part, MASKED))
    return held


def highest(held):
    tops = [functools.reduce(jnp.maximum, [x for x in parts if x is not None]) for parts in held]
    return jnp.concatenate([jnp.max(top, axis=0, keepdims=True) for top in tops], axis=1)


def weigh(held, top):
    totals, rounded = [], []
    for index, parts in enumerate(held):
        rows = next(x for x in parts if x is not None).shape[1]
        here = top[:, index * rows : (index + 1) * rows]
        weights = [None if x is None else jnp.exp2((x - here) * FACTOR) for x in parts]
        total = functools.reduce(jnp.add, [x for x in weights if x is not None])
        totals.append(jnp.sum(total, axis=0, keepdims=True))
        rounded.append(
            [
                jnp.zeros((rows, rows), jnp.bfloat16) if x is None else x.astype(jnp.bfloat16)
                for x in weights
            ]
        )
    lines = [jnp.concatenate(line, axis=1) for line in zip(*rounded)]
    return jnp.concatenate(totals, axis=1), jnp.concatenate(lines, axis=0)


def mix(sets, rounded):
    return dot(jnp.concatenate([one[1] for one in sets], axis=0).T, rounded)


def unit_rows(heads, query_ref, begin):
    rows = query_ref.shape[1] - NOTE_ROWS
    group, _, parity = place(heads)
    starts = []
    for block in range(begin, begin + UNIT):
        note = query_ref[block, rows:, :HD].astype(jnp.float32)
        starts.append(note[0:1] * float(DIGIT) + note[1:2])
    start = jnp.concatenate(starts, axis=1).astype(jnp.int32) - group * (heads * rows)
    line = lax.broadcasted_iota(jnp.int32, (1, UNIT * rows), 1)
    own = line // rows * rows + line + (2 * begin + parity) * rows
    return start, own


def unit_queries(query_ref, head, begin):
    rows = query_ref.shape[1] - NOTE_ROWS
    blocks = range(begin, begin + UNIT)
    columns = slice(head * HD, (head + 1) * HD)
    return jnp.concatenate([query_ref[block, :rows, columns] for block in blocks], axis=0)


FACTOR = math.log2(math.e) / math.sqrt(HD)


def attend_first(heads, query_ref, key_value_ref, top_ref, total_ref, mixed_ref):
    _, _, parity = place(heads)
    for unit in range(heads // 2 // UNIT):
        begin = unit * UNIT
        start, own = unit_rows(heads, query_ref, begin)
        sets = [[key_set(key_value_ref, begin + UNIT, head, 0, parity, True)] for head in range(2)]
        held = [
            masked_scores(sets[head], unit_queries(query_ref, head, begin), start, own, begin)
            for head in range(2)
        ]
        tops = [highest(each) for each in held]
        weights = [weigh(each, top) for each, top in zip(held, tops)]
        for head, (total, rounded) in enumerate(weights):
            top_ref[head, unit] = tops[head]
            total_ref[head, unit] = total
            mixed_ref[head, unit] = mix(sets[head], rounded)


def attend_second(heads, mine, *refs):
    count = heads // 2
    query_ref, top_ref, total_ref, mixed_ref, other_ref, *more = refs[: -UNIT - 1]
    outs, held_ref = refs[-UNIT - 1 : -1], refs[-1]
    more = more[: len(more) // 2 * 2]
    rows = query_ref.shape[1] - NOTE_ROWS
    _, pair, parity = place(heads)
    here = pair // UNIT

    def one_unit(unit):
        begin = unit * UNIT
        start, own = unit_rows(heads, query_ref, begin)
        sets, held, tops = [], [], []
        for head in range(2):
            sets.append([key_set(other_ref, begin + UNIT, head, 0, 1 - parity, True)])
            for ref, side in zip(more, (parity, 1 - parity)):
                sets[head].append(key_set(ref, count, head, -heads * rows, side, False))
            query = unit_queries(query_ref, head, begin)
            held.append(masked_scores(sets[head], query, start, own, begin))
        for head in range(2):
            tops.append(jnp.maximum(top_ref[head, unit], highest(held[head])))
        weights = [weigh(each, top) for each, top in zip(held, tops)]
        notes = jnp.zeros((NOTE_ROWS, UNIT * rows), jnp.float32)
        for head, (total, rounded) in enumerate(weights):
            top = tops[head]
            scale = jnp.exp2((top_ref[head, unit] - top) * FACTOR)
            total = total_ref[head, unit] * scale + total
            mixed = mixed_ref[head, unit] * scale + mix(sets[head], rounded)
            mixed = (mixed * (1.0 / total)).astype(jnp.bfloat16).T
            logs = top * (1.0 / math.sqrt(HD)) + jnp.log(total)
            high = logs.astype(jnp.bfloat16).astype(jnp.float32)
            middle = (logs - high).astype(jnp.bfloat16).astype(jnp.float32)
            low = logs - high - middle
            line = lax.broadcasted_iota(jnp.int32, (NOTE_ROWS, UNIT * rows), 0) - 3 * head
            for index, part in enumerate((high, middle, low)):
                notes = jnp.where(line == index, part, notes)
            for index in range(UNIT):
                held_ref[index, head * rows : (head + 1) * rows] = mixed[
                    index * rows : (index + 1) * rows
                ]
        for index in range(UNIT):
            held_ref[index, 2 * rows :] = notes[:, index * rows : (index + 1) * rows].astype(
                jnp.bfloat16
            )

    for unit in range(count // UNIT):

        @pl.when((here == unit) if mine else (here != unit))
        def _():
            one_unit(unit)

    for step, out in enumerate(outs):
        out[...] = held_ref[lax.rem(pair, UNIT) ^ step]


def unpack_heads(heads, steps, *refs):
    *sources, out_ref, logs_ref = refs
    rows = out_ref.shape[0]
    _, pair, _ = place(heads)
    for step, source in zip(steps, sources):
        owner = pair ^ step
        note = source[2 * rows :].astype(jnp.float32)
        for head in range(2):
            columns = pl.ds(pl.multiple_of((owner * 2 + head) * HD, HD), HD)
            out_ref[:, columns] = source[head * rows : (head + 1) * rows]
            parts = [note[3 * head + index : 3 * head + index + 1] for index in range(3)]
            logs_ref[pl.ds(owner * 2 + head, 1), :] = parts[0] + parts[1] + parts[2]


def dot(left, right):
    return jnp.dot(left, right, preferred_element_type=jnp.float32)


def twice(array):
    return jnp.concatenate([array, array], axis=0)


def document_starts(starts_ref, rows):
    return jnp.maximum(starts_ref[...] - lax.axis_index("ctx") * rows, -rows)


def filtered(spectrum, filter_ref, back_ref):
    half = spectrum.shape[0] // 2
    even, odd = spectrum[:half], spectrum[half:]
    tap_even, tap_odd = filter_ref[:half], filter_ref[half:]
    real = (even * tap_even - odd * tap_odd).astype(jnp.bfloat16)
    imag = (even * tap_odd + odd * tap_even).astype(jnp.bfloat16)
    return dot(back_ref[...], jnp.concatenate([real, imag], axis=0))


def convolve(
    heads, other_ref, mine_ref, came_ref, before_ref, own_taps_ref, starts_ref, product_ref, gate_ref, skip_ref,
    early_ref, late_ref, back_ref, out_ref, taps_ref, halo_ref, filter_ref, sum_ref,
):
    rows = product_ref.shape[0]
    height, width = own_taps_ref.shape
    panel = lax.axis_index("tp")
    even = lax.rem(lax.axis_index("ctx"), 2) == 0
    everything = slice(None)

    def store(step, part, value):
        line = pl.ds(pl.multiple_of((panel ^ step) * height, height), height)
        taps_ref[line, part * 2 * HD : (part + 1) * 2 * HD] = value

    parts = width // (2 * HD)
    for part in range(parts):
        line = slice(part * height, (part + 1) * height)
        mine_far, other_far = mine_ref[heads, line], other_ref[heads, line]
        store(0, part, columns_of(own_taps_ref, everything, part))
        store(1, part, jnp.where(even, near_strip(came_ref, height, part), other_ref[heads + 1, line]))
        store(2, part, jnp.where(even, other_far, mine_far))
        store(3, part, jnp.where(even, mine_far, other_far))
        halo_ref[:, part * 2 * HD : (part + 1) * 2 * HD] = jnp.where(
            even,
            columns_of(before_ref, everything, part),
            other_ref[heads + 2] if part == parts - 1 else columns_of(came_ref, everything, part),
        )
    filter_ref[...] = dot(early_ref[...], twice(taps_ref[...]))
    starts = document_starts(starts_ref, rows)
    line = lax.broadcasted_iota(jnp.int32, (rows, 1), 0)
    zero = jnp.zeros((), jnp.bfloat16)

    begin = jnp.min(starts)
    past = jnp.where(line - rows >= begin, halo_ref[...], zero)
    here = jnp.where(line >= begin, product_ref[...], zero)
    spectrum = dot(early_ref[...], twice(past)) + dot(late_ref[...], twice(here))
    sum_ref[...] = filtered(spectrum, filter_ref, back_ref)

    def one_document(begin):
        here = jnp.where(line >= begin, product_ref[...], zero)
        result = filtered(dot(late_ref[...], twice(here)), filter_ref, back_ref)
        sum_ref[...] = jnp.where(line >= begin, result, sum_ref[...])
        return jnp.min(jnp.where(starts > begin, starts, rows))

    second = jnp.min(jnp.where(starts > begin, starts, rows))
    lax.while_loop(lambda begin: begin < rows, one_document, second)
    out_ref[...] = (
        gate_ref[0].astype(jnp.float32)
        * (skip_ref[...] * product_ref[...].astype(jnp.float32) + sum_ref[...])
    ).astype(jnp.bfloat16)


def twiddles(rows):
    window = 2 * rows
    order = np.arange(rows)[:, None] * 2 + 1
    angle = np.pi * ((order * np.arange(window)[None, :]) % (2 * window)) / window
    ahead = np.concatenate([np.cos(angle), -np.sin(angle)], axis=0)
    back = ahead.T[rows:] / rows
    return jnp.asarray(ahead, jnp.float32), jnp.asarray(back, jnp.float32)


def side_pairs(peers, panels):
    assert panels == 4
    far, mixed = [], []
    for peer in range(peers):
        for panel in range(panels):
            here = peer * panels + panel
            far.append((here, peer * panels + (panel ^ (3 - peer % 2))))
            if peer % 2 == 0:
                mixed.append((here, here + panels))
            else:
                mixed.append((here, (peer - 1) * panels + (panel ^ 1)))
    return far, mixed


def local(hyena_inputs, filters, skip_bias, queries, keys_values, doc_start):
    rows = queries.shape[0]
    channels = hyena_inputs.shape[2]
    heads = queries.shape[1] // HD
    count = heads // 2
    peers = lax.axis_size("ctx")
    bf16, f32 = jnp.bfloat16, jnp.float32
    shape = jax.ShapeDtypeStruct
    starts = doc_start.reshape(1, rows)

    height = filters.shape[0]

    def pinned(*arrays):
        return [pltpu.with_memory_space_constraint(x, pltpu.HBM) for x in arrays]

    *packed, wide_taps = call(
        functools.partial(pack_heads, heads),
        (shape((6 * rows + NOTE_ROWS, HD), bf16),) * count + (shape((3, height, channels), f32),),
        pinned(queries, keys_values.reshape(2 * rows, heads * HD), starts, filters),
        0,
        4 * queries.size * 3,
        scratch=(
            pltpu.VMEM((1, rows), jnp.int32),
            pltpu.SemaphoreType.DMA,
            pltpu.SemaphoreType.DMA((3,)),
            pltpu.SemaphoreType.DMA((count, 4)),
        ),
        specs=[hbm()] * 4,
    )
    arrived = [packed[0]] + [crossed(packed[step], "ctx", 2 * step) for step in range(1, count)]
    product, own_taps, far_taps, mixed_rows = call(
        pack_hyena,
        (shape((rows, channels), bf16),)
        + (shape((height, channels), bf16),) * 2
        + (shape((rows, channels - 2 * HD), bf16),),
        (hyena_inputs, wide_taps),
        0,
        4 * queries.size * 3,
    )
    axes = ("ctx", "tp")
    far_pairs, mixed_pairs = side_pairs(peers, lax.axis_size("tp"))
    far_taps = lax.ppermute(far_taps, axes, far_pairs)
    came = lax.ppermute(mixed_rows, axes, mixed_pairs)
    before = lax.ppermute(product, "ctx", [(i, i + 1) for i in range(1, peers - 1, 2)])
    ahead, back = twiddles(rows)
    early, late, back, near_starts, skip = call(
        prepare,
        (shape((2 * rows, 2 * rows), bf16),) * 2
        + (shape((rows, 2 * rows), bf16), shape((1, rows), jnp.int32), shape((1, channels), f32)),
        pinned(ahead, back, starts, skip_bias.reshape(1, channels)),
        0,
        4 * queries.size,
        scratch=(
            pltpu.VMEM((2 * rows, 2 * rows), f32),
            pltpu.VMEM((rows, 2 * rows), f32),
            pltpu.SemaphoreType.DMA((4,)),
        ),
        specs=[hbm()] * 4,
    )

    query, key_value = call(
        functools.partial(sort_heads, heads),
        (
            shape((count, rows + NOTE_ROWS, 2 * HD), bf16),
            shape((heads + 3, rows, 2 * HD), bf16),
        ),
        (*arrived, far_taps, came, product, skip),
        0,
        4 * queries.size * 3,
    )
    other = crossed(key_value, "ctx", 1)
    units = count // UNIT
    partial = call(
        functools.partial(attend_first, heads),
        (
            shape((2, units, 1, UNIT * rows), f32),
            shape((2, units, 1, UNIT * rows), f32),
            shape((2, units, HD, UNIT * rows), f32),
        ),
        (query, key_value),
        2 * (heads * rows) ** 2 * HD,
        4 * queries.size * 4,
    )
    operands = [query, *partial, other]
    if peers > heads:
        pairs = [(i, i + heads) for i in range(peers - heads)]
        operands += [lax.ppermute(each, "ctx", pairs) for each in (key_value, other)]
    assert count == 2 * UNIT
    message = shape((2 * rows + NOTE_ROWS, HD), bf16)

    def second(mine, *more):
        return call(
            functools.partial(attend_second, heads, mine),
            (message,) * UNIT,
            (*operands, *more),
            (heads * rows) ** 2 * HD,
            4 * queries.size * 4,
            scratch=(pltpu.VMEM((UNIT, 2 * rows + NOTE_ROWS, HD), bf16),),
        )

    theirs = second(False)
    own = second(True, theirs[0])
    returned = [own[0], crossed(theirs[0], "ctx", 4), crossed(theirs[1], "ctx", 6)]
    returned.append(crossed(own[1], "ctx", 2))
    hyena_out = call(
        functools.partial(convolve, heads),
        shape((rows, channels), bf16),
        (
            other, key_value, came, before, own_taps, near_starts, product, hyena_inputs,
            skip, early, late, back,
        ),
        2 * 4 * 256 * 256 * channels,
        4 * queries.size * 4,
        scratch=(
            pltpu.VMEM((FLEN, channels), bf16),
            pltpu.VMEM((rows, channels), bf16),
            pltpu.VMEM((2 * rows, channels), f32),
            pltpu.VMEM((rows, channels), f32),
        ),
    )
    attention_out, log_totals = call(
        functools.partial(unpack_heads, heads, (0, 2, 3, 1)),
        (shape((rows, heads * HD), bf16), shape((heads, rows), f32)),
        returned,
        0,
        4 * queries.size,
    )
    return (hyena_out, attention_out, log_totals)


def solution(mesh):
    in_specs = (
        P(None, "ctx", "tp"),
        P("tp", None),
        P("tp"),
        P("ctx", "tp"),
        P(None, "ctx", "tp"),
        P("ctx"),
    )
    out_specs = (P("ctx", "tp"), P("ctx", "tp"), P("tp", "ctx"))
    return jax.shard_map(local, mesh=mesh, in_specs=in_specs, out_specs=out_specs, check_vma=False)
```

```python
import functools
import math

import jax
import jax.numpy as jnp
import numpy as np
from jax import lax
from jax.experimental import pallas as pl
from jax.experimental.pallas import tpu as pltpu
from jax.sharding import PartitionSpec as P

HD = 128
FLEN = 128
DIGIT = 256
NOTE_ROWS = 16
MASKED = -1e30
VMEM_LIMIT = 16 * 1024 * 1024
LONG = 200


def vmem():
    return pl.BlockSpec(memory_space=pltpu.VMEM)


def hbm():
    return pl.BlockSpec(memory_space=pltpu.HBM)


def call(kernel, out_shape, args, flops, nbytes, scratch=(), specs=None):
    return pl.pallas_call(
        kernel,
        out_shape=out_shape,
        in_specs=specs or [vmem() for _ in args],
        out_specs=jax.tree.map(lambda _: vmem(), out_shape),
        scratch_shapes=list(scratch),
        compiler_params=pltpu.CompilerParams(vmem_limit_bytes=VMEM_LIMIT),
        cost_estimate=pl.CostEstimate(flops=flops, bytes_accessed=nbytes, transcendentals=0),
    )(*args)


def crossed(array, axis, bits):
    return lax.ppermute(array, axis, [(i, i ^ bits) for i in range(lax.axis_size(axis))])


def place(heads):
    index = lax.axis_index("ctx")
    member = lax.rem(index, heads)
    return index // heads, member // 2, lax.rem(member, 2)


def pack_heads(heads, queries_ref, keys_values_ref, starts_ref, filters_ref, *refs):
    *outs, taps_ref, held_ref, start_sem, taps_sem, sem = refs
    rows = queries_ref.shape[0]
    _, pair, _ = place(heads)
    first = pltpu.make_async_copy(starts_ref, held_ref, start_sem)
    first.start()
    copies = []
    for step, out in enumerate(outs):
        for head in range(2):
            columns = pl.ds(pl.multiple_of(((pair ^ step) * 2 + head) * HD, HD), HD)
            first_row = head * 3 * rows
            for part, source in enumerate((queries_ref, keys_values_ref)):
                lines = pl.ds(first_row + part * rows, source.shape[0])
                copies.append(
                    pltpu.make_async_copy(
                        source.at[:, columns], out.at[lines], sem.at[step, 2 * head + part]
                    )
                )
    width = taps_ref.shape[2]
    panel = lax.axis_index("tp")
    for index, target in enumerate((panel, panel ^ (3 - lax.rem(lax.axis_index("ctx"), 2)), panel ^ 1)):
        columns = pl.ds(pl.multiple_of(target * width, width), width)
        copies.append(
            pltpu.make_async_copy(
                filters_ref.at[:, columns], taps_ref.at[index], taps_sem.at[index]
            )
        )
    for copy in copies:
        copy.start()
    first.wait()
    starts = held_ref[...]
    high = (starts // DIGIT).astype(jnp.float32)
    low = (starts % DIGIT).astype(jnp.float32)
    line = lax.broadcasted_iota(jnp.int32, (NOTE_ROWS, rows), 0)
    note = jnp.where(line == 0, high, jnp.where(line == 1, low, 0.0)).astype(jnp.bfloat16)
    for out in outs:
        out[6 * rows :] = note
    for copy in copies:
        copy.wait()


def split(matrix):
    high = matrix.astype(jnp.bfloat16)
    low = (matrix - high.astype(jnp.float32)).astype(jnp.bfloat16)
    return jnp.concatenate([high, low], axis=1)


def pack_hyena(hyena_ref, taps_ref, product_ref, own_ref, far_ref, near_ref):
    product_ref[...] = (hyena_ref[1].astype(jnp.float32) * hyena_ref[2].astype(jnp.float32)).astype(
        jnp.bfloat16
    )
    for index, out in enumerate((own_ref, far_ref, near_ref)):
        out[...] = taps_ref[index].astype(jnp.bfloat16)


def prepare(
    ahead_ref, back_ref, starts_ref, skip_ref, early_ref, late_ref, back_out, starts_out, skip_out,
    ahead_held, back_held, sem,
):
    pairs = (
        (ahead_ref, ahead_held), (back_ref, back_held), (starts_ref, starts_out), (skip_ref, skip_out)
    )
    copies = [
        pltpu.make_async_copy(source, out, sem.at[index])
        for index, (source, out) in enumerate(pairs)
    ]
    for copy in copies:
        copy.start()
    for copy in copies:
        copy.wait()
    rows = back_out.shape[0]
    early_ref[...] = split(ahead_held[:, :rows])
    late_ref[...] = split(ahead_held[:, rows:])
    back_out[...] = back_held[...].astype(jnp.bfloat16)


def columns_of(ref, rows, index):
    return ref[rows, index * 2 * HD : (index + 1) * 2 * HD]


def sort_heads(heads, *refs):
    count = heads // 2
    near_ref, far_ref = refs[count : count + 2]
    query_ref, side_ref = refs[-2:]
    rows = (refs[0].shape[0] - NOTE_ROWS) // 6
    _, pair, _ = place(heads)
    for step in range(count):
        source = pair ^ step
        query_ref[source, rows:, :HD] = refs[step][6 * rows :]
        for head in range(2):
            columns = slice(head * HD, (head + 1) * HD)
            first = head * 3 * rows
            query_ref[source, :rows, columns] = refs[step][first : first + rows]
            for part in range(2):
                line = first + (part + 1) * rows
                side_ref[2 * source + part, :, columns] = refs[step][line : line + rows]
    height, width = far_ref.shape
    parts = width // (2 * HD)
    for part in range(parts):
        line = slice(part * height, (part + 1) * height)
        side_ref[heads, line] = columns_of(far_ref, slice(None), part)
        side_ref[heads + 1, line] = columns_of(near_ref, slice(None), part)


UNIT = 2


def key_set(ref, blocks, head, origin, parity, causal):
    columns = slice(head * HD, (head + 1) * HD)
    rows = ref.shape[1]
    key = jnp.concatenate([ref[2 * block, :, columns] for block in range(blocks)], axis=0)
    value = jnp.concatenate([ref[2 * block + 1, :, columns] for block in range(blocks)], axis=0)
    return key, value, [(2 * block + parity) * rows + origin for block in range(blocks)], causal


def masked_scores(sets, query, start, own, begin):
    held = [[] for _ in range(UNIT)]
    for key, _, firsts, causal in sets:
        scores = lax.dot_general(
            key, query, (((1,), (1,)), ((), ())), preferred_element_type=jnp.float32
        )
        rows = key.shape[0] // len(firsts)
        line = lax.broadcasted_iota(jnp.int32, (rows, rows), 0)
        for block, first in enumerate(firsts):
            for index in range(UNIT):
                if causal and block > begin + index:
                    held[index].append(None)
                    continue
                lanes = slice(index * rows, (index + 1) * rows)
                allowed = line >= start[:, lanes] - first
                if causal and block == begin + index:
                    allowed &= line <= own[:, lanes] - first
                part = scores[block * rows : (block + 1) * rows, lanes]
                held[index].append(jnp.where(allowed, part, MASKED))
    return held


def highest(held):
    tops = [functools.reduce(jnp.maximum, [x for x in parts if x is not None]) for parts in held]
    return jnp.concatenate([jnp.max(top, axis=0, keepdims=True) for top in tops], axis=1)


def weigh(held, top):
    totals, rounded = [], []
    for index, parts in enumerate(held):
        rows = next(x for x in parts if x is not None).shape[1]
        here = top[:, index * rows : (index + 1) * rows]
        weights = [None if x is None else jnp.exp2((x - here) * FACTOR) for x in parts]
        total = functools.reduce(jnp.add, [x for x in weights if x is not None])
        totals.append(jnp.sum(total, axis=0, keepdims=True))
        rounded.append(
            [
                jnp.zeros((rows, rows), jnp.bfloat16) if x is None else x.astype(jnp.bfloat16)
                for x in weights
            ]
        )
    lines = [jnp.concatenate(line, axis=1) for line in zip(*rounded)]
    return jnp.concatenate(totals, axis=1), jnp.concatenate(lines, axis=0)


def mix(sets, rounded):
    return dot(jnp.concatenate([one[1] for one in sets], axis=0).T, rounded)


def unit_rows(heads, query_ref, begin):
    rows = query_ref.shape[1] - NOTE_ROWS
    group, _, parity = place(heads)
    starts = []
    for block in range(begin, begin + UNIT):
        note = query_ref[block, rows:, :HD].astype(jnp.float32)
        starts.append(note[0:1] * float(DIGIT) + note[1:2])
    start = jnp.concatenate(starts, axis=1).astype(jnp.int32) - group * (heads * rows)
    line = lax.broadcasted_iota(jnp.int32, (1, UNIT * rows), 1)
    own = line // rows * rows + line + (2 * begin + parity) * rows
    return start, own


def unit_queries(query_ref, head, begin):
    rows = query_ref.shape[1] - NOTE_ROWS
    blocks = range(begin, begin + UNIT)
    columns = slice(head * HD, (head + 1) * HD)
    return jnp.concatenate([query_ref[block, :rows, columns] for block in blocks], axis=0)


FACTOR = math.log2(math.e) / math.sqrt(HD)


def attend_first(heads, query_ref, key_value_ref, top_ref, total_ref, mixed_ref):
    _, _, parity = place(heads)
    for unit in range(heads // 2 // UNIT):
        begin = unit * UNIT
        start, own = unit_rows(heads, query_ref, begin)
        sets = [[key_set(key_value_ref, begin + UNIT, head, 0, parity, True)] for head in range(2)]
        held = [
            masked_scores(sets[head], unit_queries(query_ref, head, begin), start, own, begin)
            for head in range(2)
        ]
        tops = [highest(each) for each in held]
        weights = [weigh(each, top) for each, top in zip(held, tops)]
        for head, (total, rounded) in enumerate(weights):
            top_ref[head, unit] = tops[head]
            total_ref[head, unit] = total
            mixed_ref[head, unit] = mix(sets[head], rounded)


def attend_second(heads, mine, *refs):
    count = heads // 2
    query_ref, top_ref, total_ref, mixed_ref, other_ref, *more = refs[: -UNIT - 1]
    outs, held_ref = refs[-UNIT - 1 : -1], refs[-1]
    more = more[: len(more) // 2 * 2]
    rows = query_ref.shape[1] - NOTE_ROWS
    _, pair, parity = place(heads)
    here = pair // UNIT

    def one_unit(unit):
        begin = unit * UNIT
        start, own = unit_rows(heads, query_ref, begin)
        sets, held, tops = [], [], []
        for head in range(2):
            sets.append([key_set(other_ref, begin + UNIT, head, 0, 1 - parity, True)])
            for ref, side in zip(more, (parity, 1 - parity)):
                sets[head].append(key_set(ref, count, head, -heads * rows, side, False))
            query = unit_queries(query_ref, head, begin)
            held.append(masked_scores(sets[head], query, start, own, begin))
        for head in range(2):
            tops.append(jnp.maximum(top_ref[head, unit], highest(held[head])))
        weights = [weigh(each, top) for each, top in zip(held, tops)]
        notes = jnp.zeros((NOTE_ROWS, UNIT * rows), jnp.float32)
        for head, (total, rounded) in enumerate(weights):
            top = tops[head]
            scale = jnp.exp2((top_ref[head, unit] - top) * FACTOR)
            total = total_ref[head, unit] * scale + total
            mixed = mixed_ref[head, unit] * scale + mix(sets[head], rounded)
            mixed = (mixed * (1.0 / total)).astype(jnp.bfloat16).T
            logs = top * (1.0 / math.sqrt(HD)) + jnp.log(total)
            high = logs.astype(jnp.bfloat16).astype(jnp.float32)
            middle = (logs - high).astype(jnp.bfloat16).astype(jnp.float32)
            low = logs - high - middle
            line = lax.broadcasted_iota(jnp.int32, (NOTE_ROWS, UNIT * rows), 0) - 3 * head
            for index, part in enumerate((high, middle, low)):
                notes = jnp.where(line == index, part, notes)
            for index in range(UNIT):
                held_ref[index, head * rows : (head + 1) * rows] = mixed[
                    index * rows : (index + 1) * rows
                ]
        for index in range(UNIT):
            held_ref[index, 2 * rows :] = notes[:, index * rows : (index + 1) * rows].astype(
                jnp.bfloat16
            )

    for unit in range(count // UNIT):

        @pl.when((here == unit) if mine else (here != unit))
        def _():
            one_unit(unit)

    for step, out in enumerate(outs):
        out[...] = held_ref[lax.rem(pair, UNIT) ^ step]


def unpack_heads(heads, steps, *refs):
    *sources, out_ref, logs_ref = refs
    rows = out_ref.shape[0]
    _, pair, _ = place(heads)
    for step, source in zip(steps, sources):
        owner = pair ^ step
        note = source[2 * rows :].astype(jnp.float32)
        for head in range(2):
            columns = pl.ds(pl.multiple_of((owner * 2 + head) * HD, HD), HD)
            out_ref[:, columns] = source[head * rows : (head + 1) * rows]
            parts = [note[3 * head + index : 3 * head + index + 1] for index in range(3)]
            logs_ref[pl.ds(owner * 2 + head, 1), :] = parts[0] + parts[1] + parts[2]


def dot(left, right):
    return jnp.dot(left, right, preferred_element_type=jnp.float32)


def twice(array):
    return jnp.concatenate([array, array], axis=0)


def document_starts(starts_ref, rows):
    return jnp.maximum(starts_ref[...] - lax.axis_index("ctx") * rows, -rows)


def filtered(spectrum, filter_ref, back_ref):
    half = spectrum.shape[0] // 2
    even, odd = spectrum[:half], spectrum[half:]
    tap_even, tap_odd = filter_ref[:half], filter_ref[half:]
    real = (even * tap_even - odd * tap_odd).astype(jnp.bfloat16)
    imag = (even * tap_odd + odd * tap_even).astype(jnp.bfloat16)
    return dot(back_ref[...], jnp.concatenate([real, imag], axis=0))


def convolve(
    heads, other_ref, mine_ref, before_ref, own_taps_ref, starts_ref, product_ref, gate_ref, skip_ref,
    early_ref, late_ref, back_ref, out_ref, taps_ref, filter_ref, sum_ref,
):
    rows = product_ref.shape[0]
    height, width = own_taps_ref.shape
    panel = lax.axis_index("tp")
    even = lax.rem(lax.axis_index("ctx"), 2) == 0
    everything = slice(None)

    def store(step, part, value):
        line = pl.ds(pl.multiple_of((panel ^ step) * height, height), height)
        taps_ref[line, part * 2 * HD : (part + 1) * 2 * HD] = value

    parts = width // (2 * HD)
    for part in range(parts):
        line = slice(part * height, (part + 1) * height)
        mine_far, other_far = mine_ref[heads, line], other_ref[heads, line]
        store(0, part, columns_of(own_taps_ref, everything, part))
        store(1, part, jnp.where(even, other_ref[heads + 1, line], mine_ref[heads + 1, line]))
        store(2, part, jnp.where(even, other_far, mine_far))
        store(3, part, jnp.where(even, mine_far, other_far))
    filter_ref[...] = dot(early_ref[...], twice(taps_ref[...]))
    starts = document_starts(starts_ref, rows)
    line = lax.broadcasted_iota(jnp.int32, (rows, 1), 0)
    zero = jnp.zeros((), jnp.bfloat16)

    begin = jnp.min(starts)
    past = jnp.where(line - rows >= begin, before_ref[...], zero)
    here = jnp.where(line >= begin, product_ref[...], zero)
    spectrum = dot(early_ref[...], twice(past)) + dot(late_ref[...], twice(here))
    sum_ref[...] = filtered(spectrum, filter_ref, back_ref)

    def one_document(begin):
        here = jnp.where(line >= begin, product_ref[...], zero)
        result = filtered(dot(late_ref[...], twice(here)), filter_ref, back_ref)
        sum_ref[...] = jnp.where(line >= begin, result, sum_ref[...])
        return jnp.min(jnp.where(starts > begin, starts, rows))

    second = jnp.min(jnp.where(starts > begin, starts, rows))
    lax.while_loop(lambda begin: begin < rows, one_document, second)
    out_ref[...] = (
        gate_ref[0].astype(jnp.float32)
        * (skip_ref[...] * product_ref[...].astype(jnp.float32) + sum_ref[...])
    ).astype(jnp.bfloat16)


def twiddles(rows):
    window = 2 * rows
    order = np.arange(rows)[:, None] * 2 + 1
    angle = np.pi * ((order * np.arange(window)[None, :]) % (2 * window)) / window
    ahead = np.concatenate([np.cos(angle), -np.sin(angle)], axis=0)
    back = ahead.T[rows:] / rows
    return jnp.asarray(ahead, jnp.float32), jnp.asarray(back, jnp.float32)


def taps_pairs(peers, panels):
    assert panels == 4
    near, far = [], []
    for peer in range(peers):
        for panel in range(panels):
            here = peer * panels + panel
            far.append((here, peer * panels + (panel ^ (3 - peer % 2))))
            if peer % 2 == 1:
                near.append((here, peer * panels + (panel ^ 1)))
    return near, far


def local(hyena_inputs, filters, skip_bias, queries, keys_values, doc_start):
    rows = queries.shape[0]
    channels = hyena_inputs.shape[2]
    heads = queries.shape[1] // HD
    count = heads // 2
    peers = lax.axis_size("ctx")
    bf16, f32 = jnp.bfloat16, jnp.float32
    shape = jax.ShapeDtypeStruct
    starts = doc_start.reshape(1, rows)

    height = filters.shape[0]

    def pinned(*arrays):
        return [pltpu.with_memory_space_constraint(x, pltpu.HBM) for x in arrays]

    *packed, wide_taps = call(
        functools.partial(pack_heads, heads),
        (shape((6 * rows + NOTE_ROWS, HD), bf16),) * count + (shape((3, height, channels), f32),),
        pinned(queries, keys_values.reshape(2 * rows, heads * HD), starts, filters),
        0,
        4 * queries.size * 3,
        scratch=(
            pltpu.VMEM((1, rows), jnp.int32),
            pltpu.SemaphoreType.DMA,
            pltpu.SemaphoreType.DMA((3,)),
            pltpu.SemaphoreType.DMA((count, 4)),
        ),
        specs=[hbm()] * 4,
    )
    arrived = [packed[0]] + [crossed(packed[step], "ctx", 2 * step) for step in range(1, count)]
    product, own_taps, far_taps, near_taps = call(
        pack_hyena,
        (shape((rows, channels), bf16),) + (shape((height, channels), bf16),) * 3,
        (hyena_inputs, wide_taps),
        0,
        4 * queries.size * 3,
    )
    axes = ("ctx", "tp")
    near_pairs, far_pairs = taps_pairs(peers, lax.axis_size("tp"))
    near_taps = lax.ppermute(near_taps, axes, near_pairs)
    far_taps = lax.ppermute(far_taps, axes, far_pairs)
    before = lax.ppermute(product, "ctx", [(i, i + 1) for i in range(peers - 1)])
    ahead, back = twiddles(rows)
    early, late, back, near_starts, skip = call(
        prepare,
        (shape((2 * rows, 2 * rows), bf16),) * 2
        + (shape((rows, 2 * rows), bf16), shape((1, rows), jnp.int32), shape((1, channels), f32)),
        pinned(ahead, back, starts, skip_bias.reshape(1, channels)),
        0,
        4 * queries.size,
        scratch=(
            pltpu.VMEM((2 * rows, 2 * rows), f32),
            pltpu.VMEM((rows, 2 * rows), f32),
            pltpu.SemaphoreType.DMA((4,)),
        ),
        specs=[hbm()] * 4,
    )

    query, key_value = call(
        functools.partial(sort_heads, heads),
        (
            shape((count, rows + NOTE_ROWS, 2 * HD), bf16),
            shape((heads + 2, rows, 2 * HD), bf16),
        ),
        (*arrived, near_taps, far_taps, skip),
        0,
        4 * queries.size * 3,
    )
    other = crossed(key_value, "ctx", 1)
    units = count // UNIT
    partial = call(
        functools.partial(attend_first, heads),
        (
            shape((2, units, 1, UNIT * rows), f32),
            shape((2, units, 1, UNIT * rows), f32),
            shape((2, units, HD, UNIT * rows), f32),
        ),
        (query, key_value),
        LONG * (heads * rows) ** 2 * HD,
        4 * queries.size * 4,
    )
    operands = [query, *partial, other]
    if peers > heads:
        pairs = [(i, i + heads) for i in range(peers - heads)]
        operands += [lax.ppermute(each, "ctx", pairs) for each in (key_value, other)]
    assert count == 2 * UNIT
    message = shape((2 * rows + NOTE_ROWS, HD), bf16)

    def second(mine, *more):
        return call(
            functools.partial(attend_second, heads, mine),
            (message,) * UNIT,
            (*operands, *more),
            (heads * rows) ** 2 * HD,
            4 * queries.size * 4,
            scratch=(pltpu.VMEM((UNIT, 2 * rows + NOTE_ROWS, HD), bf16),),
        )

    theirs = second(False)
    own = second(True, theirs[0])
    returned = [own[0], crossed(theirs[0], "ctx", 4), crossed(theirs[1], "ctx", 6)]
    returned.append(crossed(own[1], "ctx", 2))
    hyena_out = call(
        functools.partial(convolve, heads),
        shape((rows, channels), bf16),
        (
            other, key_value, before, own_taps, near_starts, product, hyena_inputs,
            skip, early, late, back,
        ),
        2 * 4 * 256 * 256 * channels,
        4 * queries.size * 4,
        scratch=(
            pltpu.VMEM((FLEN, channels), bf16),
            pltpu.VMEM((2 * rows, channels), f32),
            pltpu.VMEM((rows, channels), f32),
        ),
    )
    attention_out, log_totals = call(
        functools.partial(unpack_heads, heads, (0, 2, 3, 1)),
        (shape((rows, heads * HD), bf16), shape((heads, rows), f32)),
        returned,
        0,
        4 * queries.size,
    )
    return (hyena_out, attention_out, log_totals)


def solution(mesh):
    in_specs = (
        P(None, "ctx", "tp"),
        P("tp", None),
        P("tp"),
        P("ctx", "tp"),
        P(None, "ctx", "tp"),
        P("ctx"),
    )
    out_specs = (P("ctx", "tp"), P("ctx", "tp"), P("tp", "ctx"))
    return jax.shard_map(local, mesh=mesh, in_specs=in_specs, out_specs=out_specs, check_vma=False)
```

```python
import functools
import math

import jax
import jax.numpy as jnp
import numpy as np
from jax import lax
from jax.experimental import pallas as pl
from jax.experimental.pallas import tpu as pltpu
from jax.sharding import PartitionSpec as P

HD = 128
FLEN = 128
DIGIT = 256
NOTE_ROWS = 16
MASKED = -1e30
VMEM_LIMIT = 16 * 1024 * 1024
LONG = 200


def vmem():
    return pl.BlockSpec(memory_space=pltpu.VMEM)


def hbm():
    return pl.BlockSpec(memory_space=pltpu.HBM)


def call(kernel, out_shape, args, flops, nbytes, scratch=(), specs=None):
    return pl.pallas_call(
        kernel,
        out_shape=out_shape,
        in_specs=specs or [vmem() for _ in args],
        out_specs=jax.tree.map(lambda _: vmem(), out_shape),
        scratch_shapes=list(scratch),
        compiler_params=pltpu.CompilerParams(vmem_limit_bytes=VMEM_LIMIT),
        cost_estimate=pl.CostEstimate(flops=flops, bytes_accessed=nbytes, transcendentals=0),
    )(*args)


def crossed(array, axis, bits):
    return lax.ppermute(array, axis, [(i, i ^ bits) for i in range(lax.axis_size(axis))])


STEPS = (0, 2, 1, 3)


def place(heads):
    index = lax.axis_index("ctx")
    member = lax.rem(index, heads)
    return index // heads, member // 2, lax.rem(member, 2)


def pack_heads(heads, queries_ref, keys_values_ref, starts_ref, filters_ref, *refs):
    *outs, taps_ref, held_ref, start_sem, taps_sem, sem = refs
    rows = queries_ref.shape[0]
    _, pair, _ = place(heads)
    first = pltpu.make_async_copy(starts_ref, held_ref, start_sem)
    first.start()
    copies = []
    for step, out in zip(STEPS, outs):
        for head in range(2):
            columns = pl.ds(pl.multiple_of(((pair ^ step) * 2 + head) * HD, HD), HD)
            first_row = head * 3 * rows
            for part, source in enumerate((queries_ref, keys_values_ref)):
                lines = pl.ds(first_row + part * rows, source.shape[0])
                copies.append(
                    pltpu.make_async_copy(
                        source.at[:, columns], out.at[lines], sem.at[step, 2 * head + part]
                    )
                )
    width = taps_ref.shape[2]
    panel = lax.axis_index("tp")
    for index, target in enumerate((panel, panel ^ (3 - lax.rem(lax.axis_index("ctx"), 2)), panel ^ 1)):
        columns = pl.ds(pl.multiple_of(target * width, width), width)
        copies.append(
            pltpu.make_async_copy(
                filters_ref.at[:, columns], taps_ref.at[index], taps_sem.at[index]
            )
        )
    for copy in copies:
        copy.start()
    first.wait()
    starts = held_ref[...]
    high = (starts // DIGIT).astype(jnp.float32)
    low = (starts % DIGIT).astype(jnp.float32)
    line = lax.broadcasted_iota(jnp.int32, (NOTE_ROWS, rows), 0)
    note = jnp.where(line == 0, high, jnp.where(line == 1, low, 0.0)).astype(jnp.bfloat16)
    for out in outs:
        out[6 * rows :] = note
    for copy in copies:
        copy.wait()


def split(matrix):
    high = matrix.astype(jnp.bfloat16)
    low = (matrix - high.astype(jnp.float32)).astype(jnp.bfloat16)
    return jnp.concatenate([high, low], axis=1)


def pack_hyena(hyena_ref, taps_ref, product_ref, own_ref, far_ref, near_ref):
    product_ref[...] = (hyena_ref[1].astype(jnp.float32) * hyena_ref[2].astype(jnp.float32)).astype(
        jnp.bfloat16
    )
    for index, out in enumerate((own_ref, far_ref, near_ref)):
        out[...] = taps_ref[index].astype(jnp.bfloat16)


def prepare(
    ahead_ref, back_ref, starts_ref, skip_ref, early_ref, late_ref, back_out, starts_out, skip_out,
    ahead_held, back_held, sem,
):
    pairs = (
        (ahead_ref, ahead_held), (back_ref, back_held), (starts_ref, starts_out), (skip_ref, skip_out)
    )
    copies = [
        pltpu.make_async_copy(source, out, sem.at[index])
        for index, (source, out) in enumerate(pairs)
    ]
    for copy in copies:
        copy.start()
    for copy in copies:
        copy.wait()
    rows = back_out.shape[0]
    early_ref[...] = split(ahead_held[:, :rows])
    late_ref[...] = split(ahead_held[:, rows:])
    back_out[...] = back_held[...].astype(jnp.bfloat16)


def columns_of(ref, rows, index):
    return ref[rows, index * 2 * HD : (index + 1) * 2 * HD]


def sort_heads(heads, *refs):
    count = heads // 2
    near_ref, far_ref = refs[count : count + 2]
    query_ref, side_ref = refs[-2:]
    rows = (refs[0].shape[0] - NOTE_ROWS) // 6
    _, pair, _ = place(heads)
    for step, ref in zip(STEPS, refs):
        source = pair ^ step
        query_ref[source, rows:, :HD] = ref[6 * rows :]
        for head in range(2):
            columns = slice(head * HD, (head + 1) * HD)
            first = head * 3 * rows
            query_ref[source, :rows, columns] = ref[first : first + rows]
            for part in range(2):
                line = first + (part + 1) * rows
                side_ref[2 * source + part, :, columns] = ref[line : line + rows]
    height, width = far_ref.shape
    parts = width // (2 * HD)
    for part in range(parts):
        line = slice(part * height, (part + 1) * height)
        side_ref[heads, line] = columns_of(far_ref, slice(None), part)
        side_ref[heads + 1, line] = columns_of(near_ref, slice(None), part)


UNIT = 2


def key_set(ref, blocks, head, origin, parity, causal):
    columns = slice(head * HD, (head + 1) * HD)
    rows = ref.shape[1]
    key = jnp.concatenate([ref[2 * block, :, columns] for block in range(blocks)], axis=0)
    value = jnp.concatenate([ref[2 * block + 1, :, columns] for block in range(blocks)], axis=0)
    return key, value, [(2 * block + parity) * rows + origin for block in range(blocks)], causal


def masked_scores(sets, query, start, own, begin):
    held = [[] for _ in range(UNIT)]
    for key, _, firsts, causal in sets:
        scores = lax.dot_general(
            key, query, (((1,), (1,)), ((), ())), preferred_element_type=jnp.float32
        )
        rows = key.shape[0] // len(firsts)
        line = lax.broadcasted_iota(jnp.int32, (rows, rows), 0)
        for block, first in enumerate(firsts):
            for index in range(UNIT):
                if causal and block > begin + index:
                    held[index].append(None)
                    continue
                lanes = slice(index * rows, (index + 1) * rows)
                allowed = line >= start[:, lanes] - first
                if causal and block == begin + index:
                    allowed &= line <= own[:, lanes] - first
                part = scores[block * rows : (block + 1) * rows, lanes]
                held[index].append(jnp.where(allowed, part, MASKED))
    return held


def highest(held):
    tops = [functools.reduce(jnp.maximum, [x for x in parts if x is not None]) for parts in held]
    return jnp.concatenate([jnp.max(top, axis=0, keepdims=True) for top in tops], axis=1)


def weigh(held, top):
    totals, rounded = [], []
    for index, parts in enumerate(held):
        rows = next(x for x in parts if x is not None).shape[1]
        here = top[:, index * rows : (index + 1) * rows]
        weights = [None if x is None else jnp.exp2((x - here) * FACTOR) for x in parts]
        total = functools.reduce(jnp.add, [x for x in weights if x is not None])
        totals.append(jnp.sum(total, axis=0, keepdims=True))
        rounded.append(
            [
                jnp.zeros((rows, rows), jnp.bfloat16) if x is None else x.astype(jnp.bfloat16)
                for x in weights
            ]
        )
    lines = [jnp.concatenate(line, axis=1) for line in zip(*rounded)]
    return jnp.concatenate(totals, axis=1), jnp.concatenate(lines, axis=0)


def mix(sets, rounded):
    return dot(jnp.concatenate([one[1] for one in sets], axis=0).T, rounded)


def unit_rows(heads, query_ref, begin):
    rows = query_ref.shape[1] - NOTE_ROWS
    group, _, parity = place(heads)
    starts = []
    for block in range(begin, begin + UNIT):
        note = query_ref[block, rows:, :HD].astype(jnp.float32)
        starts.append(note[0:1] * float(DIGIT) + note[1:2])
    start = jnp.concatenate(starts, axis=1).astype(jnp.int32) - group * (heads * rows)
    line = lax.broadcasted_iota(jnp.int32, (1, UNIT * rows), 1)
    own = line // rows * rows + line + (2 * begin + parity) * rows
    return start, own


def unit_queries(query_ref, head, begin):
    rows = query_ref.shape[1] - NOTE_ROWS
    blocks = range(begin, begin + UNIT)
    columns = slice(head * HD, (head + 1) * HD)
    return jnp.concatenate([query_ref[block, :rows, columns] for block in blocks], axis=0)


FACTOR = math.log2(math.e) / math.sqrt(HD)


def attend_first(heads, query_ref, key_value_ref, top_ref, total_ref, mixed_ref):
    _, _, parity = place(heads)
    for unit in range(heads // 2 // UNIT):
        begin = unit * UNIT
        start, own = unit_rows(heads, query_ref, begin)
        sets = [[key_set(key_value_ref, begin + UNIT, head, 0, parity, True)] for head in range(2)]
        held = [
            masked_scores(sets[head], unit_queries(query_ref, head, begin), start, own, begin)
            for head in range(2)
        ]
        tops = [highest(each) for each in held]
        weights = [weigh(each, top) for each, top in zip(held, tops)]
        for head, (total, rounded) in enumerate(weights):
            top_ref[head, unit] = tops[head]
            total_ref[head, unit] = total
            mixed_ref[head, unit] = mix(sets[head], rounded)


def attend_second(heads, mine, *refs):
    count = heads // 2
    query_ref, top_ref, total_ref, mixed_ref, other_ref, *more = refs[: -UNIT - 1]
    outs, held_ref = refs[-UNIT - 1 : -1], refs[-1]
    more = more[: len(more) // 2 * 2]
    rows = query_ref.shape[1] - NOTE_ROWS
    _, pair, parity = place(heads)
    here = pair // UNIT

    def one_unit(unit):
        begin = unit * UNIT
        start, own = unit_rows(heads, query_ref, begin)
        sets, held, tops = [], [], []
        for head in range(2):
            sets.append([key_set(other_ref, begin + UNIT, head, 0, 1 - parity, True)])
            for ref, side in zip(more, (parity, 1 - parity)):
                sets[head].append(key_set(ref, count, head, -heads * rows, side, False))
            query = unit_queries(query_ref, head, begin)
            held.append(masked_scores(sets[head], query, start, own, begin))
        for head in range(2):
            tops.append(jnp.maximum(top_ref[head, unit], highest(held[head])))
        weights = [weigh(each, top) for each, top in zip(held, tops)]
        notes = jnp.zeros((NOTE_ROWS, UNIT * rows), jnp.float32)
        for head, (total, rounded) in enumerate(weights):
            top = tops[head]
            scale = jnp.exp2((top_ref[head, unit] - top) * FACTOR)
            total = total_ref[head, unit] * scale + total
            mixed = mixed_ref[head, unit] * scale + mix(sets[head], rounded)
            mixed = (mixed * (1.0 / total)).astype(jnp.bfloat16).T
            logs = top * (1.0 / math.sqrt(HD)) + jnp.log(total)
            high = logs.astype(jnp.bfloat16).astype(jnp.float32)
            middle = (logs - high).astype(jnp.bfloat16).astype(jnp.float32)
            low = logs - high - middle
            line = lax.broadcasted_iota(jnp.int32, (NOTE_ROWS, UNIT * rows), 0) - 3 * head
            for index, part in enumerate((high, middle, low)):
                notes = jnp.where(line == index, part, notes)
            for index in range(UNIT):
                held_ref[index, head * rows : (head + 1) * rows] = mixed[
                    index * rows : (index + 1) * rows
                ]
        for index in range(UNIT):
            held_ref[index, 2 * rows :] = notes[:, index * rows : (index + 1) * rows].astype(
                jnp.bfloat16
            )

    for unit in range(count // UNIT):

        @pl.when((here == unit) if mine else (here != unit))
        def _():
            one_unit(unit)

    for step, out in enumerate(outs):
        out[...] = held_ref[lax.rem(pair, UNIT) ^ step]


def unpack_heads(heads, steps, *refs):
    *sources, out_ref, logs_ref = refs
    rows = out_ref.shape[0]
    _, pair, _ = place(heads)
    for step, source in zip(steps, sources):
        owner = pair ^ step
        note = source[2 * rows :].astype(jnp.float32)
        for head in range(2):
            columns = pl.ds(pl.multiple_of((owner * 2 + head) * HD, HD), HD)
            out_ref[:, columns] = source[head * rows : (head + 1) * rows]
            parts = [note[3 * head + index : 3 * head + index + 1] for index in range(3)]
            logs_ref[pl.ds(owner * 2 + head, 1), :] = parts[0] + parts[1] + parts[2]


def dot(left, right):
    return jnp.dot(left, right, preferred_element_type=jnp.float32)


def twice(array):
    return jnp.concatenate([array, array], axis=0)


def document_starts(starts_ref, rows):
    return jnp.maximum(starts_ref[...] - lax.axis_index("ctx") * rows, -rows)


def filtered(spectrum, filter_ref, back_ref):
    half = spectrum.shape[0] // 2
    even, odd = spectrum[:half], spectrum[half:]
    tap_even, tap_odd = filter_ref[:half], filter_ref[half:]
    real = (even * tap_even - odd * tap_odd).astype(jnp.bfloat16)
    imag = (even * tap_odd + odd * tap_even).astype(jnp.bfloat16)
    return dot(back_ref[...], jnp.concatenate([real, imag], axis=0))


def convolve(
    heads, other_ref, mine_ref, before_ref, own_taps_ref, starts_ref, product_ref, gate_ref, skip_ref,
    early_ref, late_ref, back_ref, out_ref, taps_ref, filter_ref, sum_ref,
):
    rows = product_ref.shape[0]
    height, width = own_taps_ref.shape
    panel = lax.axis_index("tp")
    even = lax.rem(lax.axis_index("ctx"), 2) == 0
    everything = slice(None)

    def store(step, part, value):
        line = pl.ds(pl.multiple_of((panel ^ step) * height, height), height)
        taps_ref[line, part * 2 * HD : (part + 1) * 2 * HD] = value

    parts = width // (2 * HD)
    for part in range(parts):
        line = slice(part * height, (part + 1) * height)
        mine_far, other_far = mine_ref[heads, line], other_ref[heads, line]
        store(0, part, columns_of(own_taps_ref, everything, part))
        store(1, part, jnp.where(even, other_ref[heads + 1, line], mine_ref[heads + 1, line]))
        store(2, part, jnp.where(even, other_far, mine_far))
        store(3, part, jnp.where(even, mine_far, other_far))
    filter_ref[...] = dot(early_ref[...], twice(taps_ref[...]))
    starts = document_starts(starts_ref, rows)
    line = lax.broadcasted_iota(jnp.int32, (rows, 1), 0)
    zero = jnp.zeros((), jnp.bfloat16)

    begin = jnp.min(starts)
    past = jnp.where(line - rows >= begin, before_ref[...], zero)
    here = jnp.where(line >= begin, product_ref[...], zero)
    spectrum = dot(early_ref[...], twice(past)) + dot(late_ref[...], twice(here))
    sum_ref[...] = filtered(spectrum, filter_ref, back_ref)

    def one_document(begin):
        here = jnp.where(line >= begin, product_ref[...], zero)
        result = filtered(dot(late_ref[...], twice(here)), filter_ref, back_ref)
        sum_ref[...] = jnp.where(line >= begin, result, sum_ref[...])
        return jnp.min(jnp.where(starts > begin, starts, rows))

    second = jnp.min(jnp.where(starts > begin, starts, rows))
    lax.while_loop(lambda begin: begin < rows, one_document, second)
    out_ref[...] = (
        gate_ref[0].astype(jnp.float32)
        * (skip_ref[...] * product_ref[...].astype(jnp.float32) + sum_ref[...])
    ).astype(jnp.bfloat16)


def twiddles(rows):
    window = 2 * rows
    order = np.arange(rows)[:, None] * 2 + 1
    angle = np.pi * ((order * np.arange(window)[None, :]) % (2 * window)) / window
    ahead = np.concatenate([np.cos(angle), -np.sin(angle)], axis=0)
    back = ahead.T[rows:] / rows
    return jnp.asarray(ahead, jnp.float32), jnp.asarray(back, jnp.float32)


def taps_pairs(peers, panels):
    assert panels == 4
    near, far = [], []
    for peer in range(peers):
        for panel in range(panels):
            here = peer * panels + panel
            far.append((here, peer * panels + (panel ^ (3 - peer % 2))))
            if peer % 2 == 1:
                near.append((here, peer * panels + (panel ^ 1)))
    return near, far


def local(hyena_inputs, filters, skip_bias, queries, keys_values, doc_start):
    rows = queries.shape[0]
    channels = hyena_inputs.shape[2]
    heads = queries.shape[1] // HD
    count = heads // 2
    peers = lax.axis_size("ctx")
    bf16, f32 = jnp.bfloat16, jnp.float32
    shape = jax.ShapeDtypeStruct
    starts = doc_start.reshape(1, rows)

    height = filters.shape[0]

    def pinned(*arrays):
        return [pltpu.with_memory_space_constraint(x, pltpu.HBM) for x in arrays]

    *packed, wide_taps = call(
        functools.partial(pack_heads, heads),
        (shape((6 * rows + NOTE_ROWS, HD), bf16),) * count + (shape((3, height, channels), f32),),
        pinned(queries, keys_values.reshape(2 * rows, heads * HD), starts, filters),
        0,
        4 * queries.size * 3,
        scratch=(
            pltpu.VMEM((1, rows), jnp.int32),
            pltpu.SemaphoreType.DMA,
            pltpu.SemaphoreType.DMA((3,)),
            pltpu.SemaphoreType.DMA((count, 4)),
        ),
        specs=[hbm()] * 4,
    )
    assert count == len(STEPS)
    arrived = [packed[0]] + [crossed(packed[i], "ctx", 2 * STEPS[i]) for i in range(1, count)]
    product, own_taps, far_taps, near_taps = call(
        pack_hyena,
        (shape((rows, channels), bf16),) + (shape((height, channels), bf16),) * 3,
        (hyena_inputs, wide_taps),
        0,
        4 * queries.size * 3,
    )
    axes = ("ctx", "tp")
    near_pairs, far_pairs = taps_pairs(peers, lax.axis_size("tp"))
    near_taps = lax.ppermute(near_taps, axes, near_pairs)
    far_taps = lax.ppermute(far_taps, axes, far_pairs)
    before = lax.ppermute(product, "ctx", [(i, i + 1) for i in range(peers - 1)])
    ahead, back = twiddles(rows)
    early, late, back, near_starts, skip = call(
        prepare,
        (shape((2 * rows, 2 * rows), bf16),) * 2
        + (shape((rows, 2 * rows), bf16), shape((1, rows), jnp.int32), shape((1, channels), f32)),
        pinned(ahead, back, starts, skip_bias.reshape(1, channels)),
        0,
        4 * queries.size,
        scratch=(
            pltpu.VMEM((2 * rows, 2 * rows), f32),
            pltpu.VMEM((rows, 2 * rows), f32),
            pltpu.SemaphoreType.DMA((4,)),
        ),
        specs=[hbm()] * 4,
    )

    query, key_value = call(
        functools.partial(sort_heads, heads),
        (
            shape((count, rows + NOTE_ROWS, 2 * HD), bf16),
            shape((heads + 2, rows, 2 * HD), bf16),
        ),
        (*arrived, near_taps, far_taps, skip),
        0,
        4 * queries.size * 3,
    )
    other = crossed(key_value, "ctx", 1)
    units = count // UNIT
    partial = call(
        functools.partial(attend_first, heads),
        (
            shape((2, units, 1, UNIT * rows), f32),
            shape((2, units, 1, UNIT * rows), f32),
            shape((2, units, HD, UNIT * rows), f32),
        ),
        (query, key_value),
        LONG * (heads * rows) ** 2 * HD,
        4 * queries.size * 4,
    )
    operands = [query, *partial, other]
    if peers > heads:
        pairs = [(i, i + heads) for i in range(peers - heads)]
        operands += [lax.ppermute(each, "ctx", pairs) for each in (key_value, other)]
    assert count == 2 * UNIT
    message = shape((2 * rows + NOTE_ROWS, HD), bf16)

    def second(mine, *more):
        return call(
            functools.partial(attend_second, heads, mine),
            (message,) * UNIT,
            (*operands, *more),
            (heads * rows) ** 2 * HD,
            4 * queries.size * 4,
            scratch=(pltpu.VMEM((UNIT, 2 * rows + NOTE_ROWS, HD), bf16),),
        )

    theirs = second(False)
    own = second(True, theirs[0])
    returned = [own[0], crossed(theirs[0], "ctx", 4), crossed(theirs[1], "ctx", 6)]
    returned.append(crossed(own[1], "ctx", 2))
    hyena_out = call(
        functools.partial(convolve, heads),
        shape((rows, channels), bf16),
        (
            other, key_value, before, own_taps, near_starts, product, hyena_inputs,
            skip, early, late, back,
        ),
        2 * 4 * 256 * 256 * channels,
        4 * queries.size * 4,
        scratch=(
            pltpu.VMEM((FLEN, channels), bf16),
            pltpu.VMEM((2 * rows, channels), f32),
            pltpu.VMEM((rows, channels), f32),
        ),
    )
    attention_out, log_totals = call(
        functools.partial(unpack_heads, heads, (0, 2, 3, 1)),
        (shape((rows, heads * HD), bf16), shape((heads, rows), f32)),
        returned,
        0,
        4 * queries.size,
    )
    return (hyena_out, attention_out, log_totals)


def solution(mesh):
    in_specs = (
        P(None, "ctx", "tp"),
        P("tp", None),
        P("tp"),
        P("ctx", "tp"),
        P(None, "ctx", "tp"),
        P("ctx"),
    )
    out_specs = (P("ctx", "tp"), P("ctx", "tp"), P("tp", "ctx"))
    return jax.shard_map(local, mesh=mesh, in_specs=in_specs, out_specs=out_specs, check_vma=False)
```

```python
import functools
import math

import jax
import jax.numpy as jnp
import numpy as np
from jax import lax
from jax.experimental import pallas as pl
from jax.experimental.pallas import tpu as pltpu
from jax.sharding import PartitionSpec as P

HD = 128
FLEN = 128
DIGIT = 256
NOTE_ROWS = 16
MASKED = -1e30
VMEM_LIMIT = 16 * 1024 * 1024
LONG = 200


def vmem():
    return pl.BlockSpec(memory_space=pltpu.VMEM)


def hbm():
    return pl.BlockSpec(memory_space=pltpu.HBM)


def call(kernel, out_shape, args, flops, nbytes, scratch=(), specs=None, out_specs=None, aliases=None):
    return pl.pallas_call(
        kernel,
        out_shape=out_shape,
        in_specs=specs or [vmem() for _ in args],
        out_specs=out_specs or jax.tree.map(lambda _: vmem(), out_shape),
        input_output_aliases=aliases or {},
        scratch_shapes=list(scratch),
        compiler_params=pltpu.CompilerParams(vmem_limit_bytes=VMEM_LIMIT),
        cost_estimate=pl.CostEstimate(flops=flops, bytes_accessed=nbytes, transcendentals=0),
    )(*args)


def crossed(array, axis, bits):
    return lax.ppermute(array, axis, [(i, i ^ bits) for i in range(lax.axis_size(axis))])


STEPS = (0, 2, 1, 3)


def place(heads):
    index = lax.axis_index("ctx")
    member = lax.rem(index, heads)
    return index // heads, member // 2, lax.rem(member, 2)


def pack_heads(heads, queries_ref, keys_values_ref, starts_ref, filters_ref, *refs):
    *outs, taps_ref, held_ref, start_sem, taps_sem, sem = refs
    rows = queries_ref.shape[0]
    _, pair, _ = place(heads)
    first = pltpu.make_async_copy(starts_ref, held_ref, start_sem)
    first.start()
    copies = []
    for step, out in zip(STEPS, outs):
        for head in range(2):
            columns = pl.ds(pl.multiple_of(((pair ^ step) * 2 + head) * HD, HD), HD)
            first_row = head * 3 * rows
            for part, source in enumerate((queries_ref, keys_values_ref)):
                lines = pl.ds(first_row + part * rows, source.shape[0])
                copies.append(
                    pltpu.make_async_copy(
                        source.at[:, columns], out.at[lines], sem.at[step, 2 * head + part]
                    )
                )
    width = taps_ref.shape[2]
    panel = lax.axis_index("tp")
    for index, target in enumerate((panel, panel ^ (3 - lax.rem(lax.axis_index("ctx"), 2)), panel ^ 1)):
        columns = pl.ds(pl.multiple_of(target * width, width), width)
        copies.append(
            pltpu.make_async_copy(
                filters_ref.at[:, columns], taps_ref.at[index], taps_sem.at[index]
            )
        )
    for copy in copies:
        copy.start()
    first.wait()
    starts = held_ref[...]
    high = (starts // DIGIT).astype(jnp.float32)
    low = (starts % DIGIT).astype(jnp.float32)
    line = lax.broadcasted_iota(jnp.int32, (NOTE_ROWS, rows), 0)
    note = jnp.where(line == 0, high, jnp.where(line == 1, low, 0.0)).astype(jnp.bfloat16)
    for out in outs:
        out[6 * rows :] = note
    for copy in copies:
        copy.wait()


def split(matrix):
    high = matrix.astype(jnp.bfloat16)
    low = (matrix - high.astype(jnp.float32)).astype(jnp.bfloat16)
    return jnp.concatenate([high, low], axis=1)


def pack_hyena(hyena_ref, taps_ref, product_ref, own_ref, far_ref, near_ref):
    product_ref[...] = (hyena_ref[1].astype(jnp.float32) * hyena_ref[2].astype(jnp.float32)).astype(
        jnp.bfloat16
    )
    for index, out in enumerate((own_ref, far_ref, near_ref)):
        out[...] = taps_ref[index].astype(jnp.bfloat16)


def prepare(
    ahead_ref, back_ref, starts_ref, skip_ref, early_ref, late_ref, back_out, starts_out, skip_out,
    ahead_held, back_held, sem,
):
    pairs = (
        (ahead_ref, ahead_held), (back_ref, back_held), (starts_ref, starts_out), (skip_ref, skip_out)
    )
    copies = [
        pltpu.make_async_copy(source, out, sem.at[index])
        for index, (source, out) in enumerate(pairs)
    ]
    for copy in copies:
        copy.start()
    for copy in copies:
        copy.wait()
    rows = back_out.shape[0]
    early_ref[...] = split(ahead_held[:, :rows])
    late_ref[...] = split(ahead_held[:, rows:])
    back_out[...] = back_held[...].astype(jnp.bfloat16)


def columns_of(ref, rows, index):
    return ref[rows, index * 2 * HD : (index + 1) * 2 * HD]


def sort_heads(heads, *refs):
    count = heads // 2
    near_ref, far_ref = refs[count : count + 2]
    query_ref, side_ref = refs[-2:]
    rows = (refs[0].shape[0] - NOTE_ROWS) // 6
    _, pair, _ = place(heads)
    for step, ref in zip(STEPS, refs):
        source = pair ^ step
        query_ref[source, rows:, :HD] = ref[6 * rows :]
        for head in range(2):
            columns = slice(head * HD, (head + 1) * HD)
            first = head * 3 * rows
            query_ref[source, :rows, columns] = ref[first : first + rows]
            for part in range(2):
                line = first + (part + 1) * rows
                side_ref[2 * source + part, :, columns] = ref[line : line + rows]
    height, width = far_ref.shape
    parts = width // (2 * HD)
    for part in range(parts):
        line = slice(part * height, (part + 1) * height)
        side_ref[heads, line] = columns_of(far_ref, slice(None), part)
        side_ref[heads + 1, line] = columns_of(near_ref, slice(None), part)


UNIT = 2


def key_set(ref, blocks, head, origin, parity, causal):
    columns = slice(head * HD, (head + 1) * HD)
    rows = ref.shape[1]
    key = jnp.concatenate([ref[2 * block, :, columns] for block in range(blocks)], axis=0)
    value = jnp.concatenate([ref[2 * block + 1, :, columns] for block in range(blocks)], axis=0)
    return key, value, [(2 * block + parity) * rows + origin for block in range(blocks)], causal


def masked_scores(sets, query, start, own, begin):
    held = [[] for _ in range(UNIT)]
    for key, _, firsts, causal in sets:
        scores = lax.dot_general(
            key, query, (((1,), (1,)), ((), ())), preferred_element_type=jnp.float32
        )
        rows = key.shape[0] // len(firsts)
        line = lax.broadcasted_iota(jnp.int32, (rows, rows), 0)
        for block, first in enumerate(firsts):
            for index in range(UNIT):
                if causal and block > begin + index:
                    held[index].append(None)
                    continue
                lanes = slice(index * rows, (index + 1) * rows)
                allowed = line >= start[:, lanes] - first
                if causal and block == begin + index:
                    allowed &= line <= own[:, lanes] - first
                part = scores[block * rows : (block + 1) * rows, lanes]
                held[index].append(jnp.where(allowed, part, MASKED))
    return held


def highest(held):
    tops = [functools.reduce(jnp.maximum, [x for x in parts if x is not None]) for parts in held]
    return jnp.concatenate([jnp.max(top, axis=0, keepdims=True) for top in tops], axis=1)


def weigh(held, top):
    totals, rounded = [], []
    for index, parts in enumerate(held):
        rows = next(x for x in parts if x is not None).shape[1]
        here = top[:, index * rows : (index + 1) * rows]
        weights = [None if x is None else jnp.exp2((x - here) * FACTOR) for x in parts]
        total = functools.reduce(jnp.add, [x for x in weights if x is not None])
        totals.append(jnp.sum(total, axis=0, keepdims=True))
        rounded.append(
            [
                jnp.zeros((rows, rows), jnp.bfloat16) if x is None else x.astype(jnp.bfloat16)
                for x in weights
            ]
        )
    lines = [jnp.concatenate(line, axis=1) for line in zip(*rounded)]
    return jnp.concatenate(totals, axis=1), jnp.concatenate(lines, axis=0)


def mix(sets, rounded):
    return dot(jnp.concatenate([one[1] for one in sets], axis=0).T, rounded)


def unit_rows(heads, query_ref, begin):
    rows = query_ref.shape[1] - NOTE_ROWS
    group, _, parity = place(heads)
    starts = []
    for block in range(begin, begin + UNIT):
        note = query_ref[block, rows:, :HD].astype(jnp.float32)
        starts.append(note[0:1] * float(DIGIT) + note[1:2])
    start = jnp.concatenate(starts, axis=1).astype(jnp.int32) - group * (heads * rows)
    line = lax.broadcasted_iota(jnp.int32, (1, UNIT * rows), 1)
    own = line // rows * rows + line + (2 * begin + parity) * rows
    return start, own


def unit_queries(query_ref, head, begin):
    rows = query_ref.shape[1] - NOTE_ROWS
    blocks = range(begin, begin + UNIT)
    columns = slice(head * HD, (head + 1) * HD)
    return jnp.concatenate([query_ref[block, :rows, columns] for block in blocks], axis=0)


FACTOR = math.log2(math.e) / math.sqrt(HD)


def attend_first(heads, query_ref, key_value_ref, top_ref, total_ref, mixed_ref):
    _, _, parity = place(heads)
    for unit in range(heads // 2 // UNIT):
        begin = unit * UNIT
        start, own = unit_rows(heads, query_ref, begin)
        sets = [[key_set(key_value_ref, begin + UNIT, head, 0, parity, True)] for head in range(2)]
        held = [
            masked_scores(sets[head], unit_queries(query_ref, head, begin), start, own, begin)
            for head in range(2)
        ]
        tops = [highest(each) for each in held]
        weights = [weigh(each, top) for each, top in zip(held, tops)]
        for head, (total, rounded) in enumerate(weights):
            top_ref[head, unit] = tops[head]
            total_ref[head, unit] = total
            mixed_ref[head, unit] = mix(sets[head], rounded)


def attend_second(heads, *refs):
    count = heads // 2
    query_ref, top_ref, total_ref, mixed_ref, other_ref, *more = refs[: -count - 1]
    outs, held_ref = refs[-count - 1 : -1], refs[-1]
    rows = query_ref.shape[1] - NOTE_ROWS
    _, pair, parity = place(heads)

    def one_unit(unit):
        begin = unit * UNIT
        start, own = unit_rows(heads, query_ref, begin)
        sets, held, tops = [], [], []
        for head in range(2):
            sets.append([key_set(other_ref, begin + UNIT, head, 0, 1 - parity, True)])
            for ref, side in zip(more, (parity, 1 - parity)):
                sets[head].append(key_set(ref, count, head, -heads * rows, side, False))
            query = unit_queries(query_ref, head, begin)
            held.append(masked_scores(sets[head], query, start, own, begin))
        for head in range(2):
            tops.append(jnp.maximum(top_ref[head, unit], highest(held[head])))
        weights = [weigh(each, top) for each, top in zip(held, tops)]
        notes = jnp.zeros((NOTE_ROWS, UNIT * rows), jnp.float32)
        for head, (total, rounded) in enumerate(weights):
            top = tops[head]
            scale = jnp.exp2((top_ref[head, unit] - top) * FACTOR)
            total = total_ref[head, unit] * scale + total
            mixed = mixed_ref[head, unit] * scale + mix(sets[head], rounded)
            mixed = (mixed * (1.0 / total)).astype(jnp.bfloat16).T
            logs = top * (1.0 / math.sqrt(HD)) + jnp.log(total)
            high = logs.astype(jnp.bfloat16).astype(jnp.float32)
            middle = (logs - high).astype(jnp.bfloat16).astype(jnp.float32)
            low = logs - high - middle
            line = lax.broadcasted_iota(jnp.int32, (NOTE_ROWS, UNIT * rows), 0) - 3 * head
            for index, part in enumerate((high, middle, low)):
                notes = jnp.where(line == index, part, notes)
            for index in range(UNIT):
                held_ref[begin + index, head * rows : (head + 1) * rows] = mixed[
                    index * rows : (index + 1) * rows
                ]
        for index in range(UNIT):
            held_ref[begin + index, 2 * rows :] = notes[:, index * rows : (index + 1) * rows].astype(
                jnp.bfloat16
            )

    for unit in range(count // UNIT):
        one_unit(unit)
    for step, out in enumerate(outs):
        out[...] = held_ref[pair ^ step]


def send_columns(heads, sources, out_ref, held_ref, sem):
    rows = out_ref.shape[0]
    _, pair, _ = place(heads)
    copies = []
    for index, (step, source) in enumerate(sources):
        for head in range(2):
            held_ref[index, :, head * HD : (head + 1) * HD] = source[head * rows : (head + 1) * rows]
        columns = pl.ds(pl.multiple_of((pair ^ step) * (2 * HD), 2 * HD), 2 * HD)
        copies.append(
            pltpu.make_async_copy(held_ref.at[index], out_ref.at[:, columns], sem.at[index])
        )
        copies[-1].start()
    return copies


def unpack_early(heads, steps, *refs):
    *sources, out_ref, held_ref, sem = refs
    for copy in send_columns(heads, list(zip(steps, sources)), out_ref, held_ref, sem):
        copy.wait()


def unpack_late(heads, steps, *refs):
    *sources, _, out_ref, logs_ref, held_ref, sem = refs
    copies = send_columns(heads, [(steps[-1], sources[-1])], out_ref, held_ref, sem)
    rows = out_ref.shape[0]
    _, pair, _ = place(heads)
    for step, source in zip(steps, sources):
        note = source[2 * rows :].astype(jnp.float32)
        for head in range(2):
            parts = [note[3 * head + index : 3 * head + index + 1] for index in range(3)]
            logs_ref[pl.ds((pair ^ step) * 2 + head, 1), :] = parts[0] + parts[1] + parts[2]
    for copy in copies:
        copy.wait()


def dot(left, right):
    return jnp.dot(left, right, preferred_element_type=jnp.float32)


def twice(array):
    return jnp.concatenate([array, array], axis=0)


def document_starts(starts_ref, rows):
    return jnp.maximum(starts_ref[...] - lax.axis_index("ctx") * rows, -rows)


def filtered(spectrum, filter_ref, back_ref):
    half = spectrum.shape[0] // 2
    even, odd = spectrum[:half], spectrum[half:]
    tap_even, tap_odd = filter_ref[:half], filter_ref[half:]
    real = (even * tap_even - odd * tap_odd).astype(jnp.bfloat16)
    imag = (even * tap_odd + odd * tap_even).astype(jnp.bfloat16)
    return dot(back_ref[...], jnp.concatenate([real, imag], axis=0))


def convolve(
    heads, other_ref, mine_ref, before_ref, own_taps_ref, starts_ref, product_ref, gate_ref, skip_ref,
    early_ref, late_ref, back_ref, out_ref, taps_ref, filter_ref, sum_ref,
):
    rows = product_ref.shape[0]
    height, width = own_taps_ref.shape
    panel = lax.axis_index("tp")
    even = lax.rem(lax.axis_index("ctx"), 2) == 0
    everything = slice(None)

    def store(step, part, value):
        line = pl.ds(pl.multiple_of((panel ^ step) * height, height), height)
        taps_ref[line, part * 2 * HD : (part + 1) * 2 * HD] = value

    parts = width // (2 * HD)
    for part in range(parts):
        line = slice(part * height, (part + 1) * height)
        mine_far, other_far = mine_ref[heads, line], other_ref[heads, line]
        store(0, part, columns_of(own_taps_ref, everything, part))
        store(1, part, jnp.where(even, other_ref[heads + 1, line], mine_ref[heads + 1, line]))
        store(2, part, jnp.where(even, other_far, mine_far))
        store(3, part, jnp.where(even, mine_far, other_far))
    filter_ref[...] = dot(early_ref[...], twice(taps_ref[...]))
    starts = document_starts(starts_ref, rows)
    line = lax.broadcasted_iota(jnp.int32, (rows, 1), 0)
    zero = jnp.zeros((), jnp.bfloat16)

    begin = jnp.min(starts)
    past = jnp.where(line - rows >= begin, before_ref[...], zero)
    here = jnp.where(line >= begin, product_ref[...], zero)
    spectrum = dot(early_ref[...], twice(past)) + dot(late_ref[...], twice(here))
    sum_ref[...] = filtered(spectrum, filter_ref, back_ref)

    def one_document(begin):
        here = jnp.where(line >= begin, product_ref[...], zero)
        result = filtered(dot(late_ref[...], twice(here)), filter_ref, back_ref)
        sum_ref[...] = jnp.where(line >= begin, result, sum_ref[...])
        return jnp.min(jnp.where(starts > begin, starts, rows))

    second = jnp.min(jnp.where(starts > begin, starts, rows))
    lax.while_loop(lambda begin: begin < rows, one_document, second)
    out_ref[...] = (
        gate_ref[0].astype(jnp.float32)
        * (skip_ref[...] * product_ref[...].astype(jnp.float32) + sum_ref[...])
    ).astype(jnp.bfloat16)


def twiddles(rows):
    window = 2 * rows
    order = np.arange(rows)[:, None] * 2 + 1
    angle = np.pi * ((order * np.arange(window)[None, :]) % (2 * window)) / window
    ahead = np.concatenate([np.cos(angle), -np.sin(angle)], axis=0)
    back = ahead.T[rows:] / rows
    return jnp.asarray(ahead, jnp.float32), jnp.asarray(back, jnp.float32)


def taps_pairs(peers, panels):
    assert panels == 4
    near, far = [], []
    for peer in range(peers):
        for panel in range(panels):
            here = peer * panels + panel
            far.append((here, peer * panels + (panel ^ (3 - peer % 2))))
            if peer % 2 == 1:
                near.append((here, peer * panels + (panel ^ 1)))
    return near, far


def local(hyena_inputs, filters, skip_bias, queries, keys_values, doc_start):
    rows = queries.shape[0]
    channels = hyena_inputs.shape[2]
    heads = queries.shape[1] // HD
    count = heads // 2
    peers = lax.axis_size("ctx")
    bf16, f32 = jnp.bfloat16, jnp.float32
    shape = jax.ShapeDtypeStruct
    starts = doc_start.reshape(1, rows)

    height = filters.shape[0]

    def pinned(*arrays):
        return [pltpu.with_memory_space_constraint(x, pltpu.HBM) for x in arrays]

    *packed, wide_taps = call(
        functools.partial(pack_heads, heads),
        (shape((6 * rows + NOTE_ROWS, HD), bf16),) * count + (shape((3, height, channels), f32),),
        pinned(queries, keys_values.reshape(2 * rows, heads * HD), starts, filters),
        0,
        4 * queries.size * 3,
        scratch=(
            pltpu.VMEM((1, rows), jnp.int32),
            pltpu.SemaphoreType.DMA,
            pltpu.SemaphoreType.DMA((3,)),
            pltpu.SemaphoreType.DMA((count, 4)),
        ),
        specs=[hbm()] * 4,
    )
    assert count == len(STEPS)
    arrived = [packed[0]] + [crossed(packed[i], "ctx", 2 * STEPS[i]) for i in range(1, count)]
    product, own_taps, far_taps, near_taps = call(
        pack_hyena,
        (shape((rows, channels), bf16),) + (shape((height, channels), bf16),) * 3,
        (hyena_inputs, wide_taps),
        0,
        4 * queries.size * 3,
    )
    axes = ("ctx", "tp")
    near_pairs, far_pairs = taps_pairs(peers, lax.axis_size("tp"))
    near_taps = lax.ppermute(near_taps, axes, near_pairs)
    far_taps = lax.ppermute(far_taps, axes, far_pairs)
    before = lax.ppermute(product, "ctx", [(i, i + 1) for i in range(peers - 1)])
    ahead, back = twiddles(rows)
    early, late, back, near_starts, skip = call(
        prepare,
        (shape((2 * rows, 2 * rows), bf16),) * 2
        + (shape((rows, 2 * rows), bf16), shape((1, rows), jnp.int32), shape((1, channels), f32)),
        pinned(ahead, back, starts, skip_bias.reshape(1, channels)),
        0,
        4 * queries.size,
        scratch=(
            pltpu.VMEM((2 * rows, 2 * rows), f32),
            pltpu.VMEM((rows, 2 * rows), f32),
            pltpu.SemaphoreType.DMA((4,)),
        ),
        specs=[hbm()] * 4,
    )

    query, key_value = call(
        functools.partial(sort_heads, heads),
        (
            shape((count, rows + NOTE_ROWS, 2 * HD), bf16),
            shape((heads + 2, rows, 2 * HD), bf16),
        ),
        (*arrived, near_taps, far_taps, skip),
        0,
        4 * queries.size * 3,
    )
    other = crossed(key_value, "ctx", 1)
    units = count // UNIT
    partial = call(
        functools.partial(attend_first, heads),
        (
            shape((2, units, 1, UNIT * rows), f32),
            shape((2, units, 1, UNIT * rows), f32),
            shape((2, units, HD, UNIT * rows), f32),
        ),
        (query, key_value),
        LONG * (heads * rows) ** 2 * HD,
        4 * queries.size * 4,
    )
    operands = [query, *partial, other]
    if peers > heads:
        pairs = [(i, i + heads) for i in range(peers - heads)]
        operands += [lax.ppermute(each, "ctx", pairs) for each in (key_value, other)]
    assert count == 2 * UNIT
    message = shape((2 * rows + NOTE_ROWS, HD), bf16)

    mixed = call(
        functools.partial(attend_second, heads),
        (message,) * count,
        operands,
        2 * (heads * rows) ** 2 * HD,
        4 * queries.size * 4,
        scratch=(pltpu.VMEM((count, 2 * rows + NOTE_ROWS, HD), bf16),),
    )
    own, *returned = [mixed[0]] + [crossed(mixed[step], "ctx", 2 * step) for step in (2, 3, 1)]
    hyena_out = call(
        functools.partial(convolve, heads),
        shape((rows, channels), bf16),
        (
            other, key_value, before, own_taps, near_starts, product, hyena_inputs,
            skip, early, late, back,
        ),
        2 * 4 * 256 * 256 * channels,
        4 * queries.size * 4,
        scratch=(
            pltpu.VMEM((FLEN, channels), bf16),
            pltpu.VMEM((2 * rows, channels), f32),
            pltpu.VMEM((rows, channels), f32),
        ),
    )
    order = (0, 2, 3, 1)
    early_out = call(
        functools.partial(unpack_early, heads, order[:-1]),
        shape((rows, heads * HD), bf16),
        (own, *returned[:-1]),
        0,
        4 * queries.size,
        scratch=(pltpu.VMEM((count - 1, rows, 2 * HD), bf16), pltpu.SemaphoreType.DMA((count - 1,))),
        out_specs=hbm(),
    )
    attention_out, log_totals = call(
        functools.partial(unpack_late, heads, order),
        (shape((rows, heads * HD), bf16), shape((heads, rows), f32)),
        (own, *returned, early_out),
        0,
        4 * queries.size,
        scratch=(pltpu.VMEM((1, rows, 2 * HD), bf16), pltpu.SemaphoreType.DMA((1,))),
        specs=[vmem()] * count + [hbm()],
        out_specs=(hbm(), vmem()),
        aliases={count: 0},
    )
    return (hyena_out, attention_out, log_totals)


def solution(mesh):
    in_specs = (
        P(None, "ctx", "tp"),
        P("tp", None),
        P("tp"),
        P("ctx", "tp"),
        P(None, "ctx", "tp"),
        P("ctx"),
    )
    out_specs = (P("ctx", "tp"), P("ctx", "tp"), P("tp", "ctx"))
    return jax.shard_map(local, mesh=mesh, in_specs=in_specs, out_specs=out_specs, check_vma=False)
```

```python
import functools
import math

import jax
import jax.numpy as jnp
import numpy as np
from jax import lax
from jax.experimental import pallas as pl
from jax.experimental.pallas import tpu as pltpu
from jax.sharding import PartitionSpec as P

HD = 128
FLEN = 128
DIGIT = 256
NOTE_ROWS = 16
MASKED = -1e30
VMEM_LIMIT = 16 * 1024 * 1024
LONG = 200


def vmem():
    return pl.BlockSpec(memory_space=pltpu.VMEM)


def hbm():
    return pl.BlockSpec(memory_space=pltpu.HBM)


def call(kernel, out_shape, args, flops, nbytes, scratch=(), specs=None):
    return pl.pallas_call(
        kernel,
        out_shape=out_shape,
        in_specs=specs or [vmem() for _ in args],
        out_specs=jax.tree.map(lambda _: vmem(), out_shape),
        scratch_shapes=list(scratch),
        compiler_params=pltpu.CompilerParams(vmem_limit_bytes=VMEM_LIMIT),
        cost_estimate=pl.CostEstimate(flops=flops, bytes_accessed=nbytes, transcendentals=0),
    )(*args)


def crossed(array, axis, bits):
    return lax.ppermute(array, axis, [(i, i ^ bits) for i in range(lax.axis_size(axis))])


STEPS = (0, 2, 1, 3)


def place(heads):
    index = lax.axis_index("ctx")
    member = lax.rem(index, heads)
    return index // heads, member // 2, lax.rem(member, 2)


def pack_heads(heads, queries_ref, keys_values_ref, starts_ref, *refs):
    *outs, held_ref, start_sem, sem = refs
    rows = queries_ref.shape[0]
    _, pair, _ = place(heads)
    first = pltpu.make_async_copy(starts_ref, held_ref, start_sem)
    first.start()
    copies = []
    for step, out in zip(STEPS, outs):
        for head in range(2):
            columns = pl.ds(pl.multiple_of(((pair ^ step) * 2 + head) * HD, HD), HD)
            first_row = head * 3 * rows
            for part, source in enumerate((queries_ref, keys_values_ref)):
                lines = pl.ds(first_row + part * rows, source.shape[0])
                copies.append(
                    pltpu.make_async_copy(
                        source.at[:, columns], out.at[lines], sem.at[step, 2 * head + part]
                    )
                )
    for copy in copies:
        copy.start()
    first.wait()
    starts = held_ref[...]
    high = (starts // DIGIT).astype(jnp.float32)
    low = (starts % DIGIT).astype(jnp.float32)
    line = lax.broadcasted_iota(jnp.int32, (NOTE_ROWS, rows), 0)
    note = jnp.where(line == 0, high, jnp.where(line == 1, low, 0.0)).astype(jnp.bfloat16)
    for out in outs:
        out[6 * rows :] = note
    for copy in copies:
        copy.wait()


def split(matrix):
    high = matrix.astype(jnp.bfloat16)
    low = (matrix - high.astype(jnp.float32)).astype(jnp.bfloat16)
    return jnp.concatenate([high, low], axis=1)


def pack_hyena(hyena_ref, filters_ref, product_ref, own_ref, far_ref, near_ref, taps_ref, sem):
    width = own_ref.shape[1]
    panel = lax.axis_index("tp")
    parity = lax.rem(lax.axis_index("ctx"), 2)
    copies = []
    for index, target in enumerate((panel, panel ^ (3 - parity), panel ^ 1)):
        columns = pl.ds(pl.multiple_of(target * width, width), width)
        copies.append(
            pltpu.make_async_copy(filters_ref.at[:, columns], taps_ref.at[index], sem.at[index])
        )
    for copy in copies:
        copy.start()
    product_ref[...] = (hyena_ref[1].astype(jnp.float32) * hyena_ref[2].astype(jnp.float32)).astype(
        jnp.bfloat16
    )
    for copy in copies:
        copy.wait()
    for index, out in enumerate((own_ref, far_ref, near_ref)):
        out[...] = taps_ref[index].astype(jnp.bfloat16)


def columns_of(ref, rows, index):
    return ref[rows, index * 2 * HD : (index + 1) * 2 * HD]


def sort_heads(heads, *refs):
    count = heads // 2
    near_ref, far_ref = refs[count : count + 2]
    query_ref, side_ref = refs[-2:]
    rows = (refs[0].shape[0] - NOTE_ROWS) // 6
    _, pair, _ = place(heads)
    for step, ref in zip(STEPS, refs):
        source = pair ^ step
        query_ref[source, rows:, :HD] = ref[6 * rows :]
        for head in range(2):
            columns = slice(head * HD, (head + 1) * HD)
            first = head * 3 * rows
            query_ref[source, :rows, columns] = ref[first : first + rows]
            for part in range(2):
                line = first + (part + 1) * rows
                side_ref[2 * source + part, :, columns] = ref[line : line + rows]
    height, width = far_ref.shape
    parts = width // (2 * HD)
    for part in range(parts):
        line = slice(part * height, (part + 1) * height)
        side_ref[heads, line] = columns_of(far_ref, slice(None), part)
        side_ref[heads + 1, line] = columns_of(near_ref, slice(None), part)


UNIT = 2


def key_set(ref, blocks, head, origin, parity, causal):
    columns = slice(head * HD, (head + 1) * HD)
    rows = ref.shape[1]
    key = jnp.concatenate([ref[2 * block, :, columns] for block in range(blocks)], axis=0)
    value = jnp.concatenate([ref[2 * block + 1, :, columns] for block in range(blocks)], axis=0)
    return key, value, [(2 * block + parity) * rows + origin for block in range(blocks)], causal


def masked_scores(sets, query, start, own, begin):
    held = [[] for _ in range(UNIT)]
    for key, _, firsts, causal in sets:
        scores = lax.dot_general(
            key, query, (((1,), (1,)), ((), ())), preferred_element_type=jnp.float32
        )
        rows = key.shape[0] // len(firsts)
        line = lax.broadcasted_iota(jnp.int32, (rows, rows), 0)
        for block, first in enumerate(firsts):
            for index in range(UNIT):
                if causal and block > begin + index:
                    held[index].append(None)
                    continue
                lanes = slice(index * rows, (index + 1) * rows)
                allowed = line >= start[:, lanes] - first
                if causal and block == begin + index:
                    allowed &= line <= own[:, lanes] - first
                part = scores[block * rows : (block + 1) * rows, lanes]
                held[index].append(jnp.where(allowed, part, MASKED))
    return held


def highest(held):
    tops = [functools.reduce(jnp.maximum, [x for x in parts if x is not None]) for parts in held]
    return jnp.concatenate([jnp.max(top, axis=0, keepdims=True) for top in tops], axis=1)


def weigh(held, top):
    totals, rounded = [], []
    for index, parts in enumerate(held):
        rows = next(x for x in parts if x is not None).shape[1]
        here = top[:, index * rows : (index + 1) * rows]
        weights = [None if x is None else jnp.exp2((x - here) * FACTOR) for x in parts]
        total = functools.reduce(jnp.add, [x for x in weights if x is not None])
        totals.append(jnp.sum(total, axis=0, keepdims=True))
        rounded.append(
            [
                jnp.zeros((rows, rows), jnp.bfloat16) if x is None else x.astype(jnp.bfloat16)
                for x in weights
            ]
        )
    lines = [jnp.concatenate(line, axis=1) for line in zip(*rounded)]
    return jnp.concatenate(totals, axis=1), jnp.concatenate(lines, axis=0)


def mix(sets, rounded):
    return dot(jnp.concatenate([one[1] for one in sets], axis=0).T, rounded)


def unit_rows(heads, query_ref, begin):
    rows = query_ref.shape[1] - NOTE_ROWS
    group, _, parity = place(heads)
    starts = []
    for block in range(begin, begin + UNIT):
        note = query_ref[block, rows:, :HD].astype(jnp.float32)
        starts.append(note[0:1] * float(DIGIT) + note[1:2])
    start = jnp.concatenate(starts, axis=1).astype(jnp.int32) - group * (heads * rows)
    line = lax.broadcasted_iota(jnp.int32, (1, UNIT * rows), 1)
    own = line // rows * rows + line + (2 * begin + parity) * rows
    return start, own


def unit_queries(query_ref, head, begin):
    rows = query_ref.shape[1] - NOTE_ROWS
    blocks = range(begin, begin + UNIT)
    columns = slice(head * HD, (head + 1) * HD)
    return jnp.concatenate([query_ref[block, :rows, columns] for block in blocks], axis=0)


FACTOR = math.log2(math.e) / math.sqrt(HD)


def attend_first(heads, query_ref, key_value_ref, top_ref, total_ref, mixed_ref):
    _, _, parity = place(heads)
    for unit in range(heads // 2 // UNIT):
        begin = unit * UNIT
        start, own = unit_rows(heads, query_ref, begin)
        sets = [[key_set(key_value_ref, begin + UNIT, head, 0, parity, True)] for head in range(2)]
        held = [
            masked_scores(sets[head], unit_queries(query_ref, head, begin), start, own, begin)
            for head in range(2)
        ]
        tops = [highest(each) for each in held]
        weights = [weigh(each, top) for each, top in zip(held, tops)]
        for head, (total, rounded) in enumerate(weights):
            top_ref[head, unit] = tops[head]
            total_ref[head, unit] = total
            mixed_ref[head, unit] = mix(sets[head], rounded)


def attend_second(heads, mine, *refs):
    count = heads // 2
    query_ref, top_ref, total_ref, mixed_ref, other_ref, *more = refs[: -UNIT - 1]
    outs, held_ref = refs[-UNIT - 1 : -1], refs[-1]
    more = more[: len(more) // 2 * 2]
    rows = query_ref.shape[1] - NOTE_ROWS
    _, pair, parity = place(heads)
    here = pair // UNIT

    def one_unit(unit):
        begin = unit * UNIT
        start, own = unit_rows(heads, query_ref, begin)
        sets, held, tops = [], [], []
        for head in range(2):
            sets.append([key_set(other_ref, begin + UNIT, head, 0, 1 - parity, True)])
            for ref, side in zip(more, (parity, 1 - parity)):
                sets[head].append(key_set(ref, count, head, -heads * rows, side, False))
            query = unit_queries(query_ref, head, begin)
            held.append(masked_scores(sets[head], query, start, own, begin))
        for head in range(2):
            tops.append(jnp.maximum(top_ref[head, unit], highest(held[head])))
        weights = [weigh(each, top) for each, top in zip(held, tops)]
        notes = jnp.zeros((NOTE_ROWS, UNIT * rows), jnp.float32)
        for head, (total, rounded) in enumerate(weights):
            top = tops[head]
            scale = jnp.exp2((top_ref[head, unit] - top) * FACTOR)
            total = total_ref[head, unit] * scale + total
            mixed = mixed_ref[head, unit] * scale + mix(sets[head], rounded)
            mixed = (mixed * (1.0 / total)).astype(jnp.bfloat16).T
            logs = top * (1.0 / math.sqrt(HD)) + jnp.log(total)
            high = logs.astype(jnp.bfloat16).astype(jnp.float32)
            middle = (logs - high).astype(jnp.bfloat16).astype(jnp.float32)
            low = logs - high - middle
            line = lax.broadcasted_iota(jnp.int32, (NOTE_ROWS, UNIT * rows), 0) - 3 * head
            for index, part in enumerate((high, middle, low)):
                notes = jnp.where(line == index, part, notes)
            for index in range(UNIT):
                held_ref[index, head * rows : (head + 1) * rows] = mixed[
                    index * rows : (index + 1) * rows
                ]
        for index in range(UNIT):
            held_ref[index, 2 * rows :] = notes[:, index * rows : (index + 1) * rows].astype(
                jnp.bfloat16
            )

    for unit in range(count // UNIT):

        @pl.when((here == unit) if mine else (here != unit))
        def _():
            one_unit(unit)

    for step, out in enumerate(outs):
        out[...] = held_ref[lax.rem(pair, UNIT) ^ step]


def unpack_heads(heads, steps, *refs):
    *sources, out_ref, logs_ref = refs
    rows = out_ref.shape[0]
    _, pair, _ = place(heads)
    for step, source in zip(steps, sources):
        owner = pair ^ step
        note = source[2 * rows :].astype(jnp.float32)
        for head in range(2):
            columns = pl.ds(pl.multiple_of((owner * 2 + head) * HD, HD), HD)
            out_ref[:, columns] = source[head * rows : (head + 1) * rows]
            parts = [note[3 * head + index : 3 * head + index + 1] for index in range(3)]
            logs_ref[pl.ds(owner * 2 + head, 1), :] = parts[0] + parts[1] + parts[2]


def dot(left, right):
    return jnp.dot(left, right, preferred_element_type=jnp.float32)


def twice(array):
    return jnp.concatenate([array, array], axis=0)


def document_starts(starts_ref, rows):
    return jnp.maximum(starts_ref[...] - lax.axis_index("ctx") * rows, -rows)


def filtered(spectrum, filter_ref, back_ref):
    half = spectrum.shape[0] // 2
    even, odd = spectrum[:half], spectrum[half:]
    tap_even, tap_odd = filter_ref[:half], filter_ref[half:]
    real = (even * tap_even - odd * tap_odd).astype(jnp.bfloat16)
    imag = (even * tap_odd + odd * tap_even).astype(jnp.bfloat16)
    return dot(back_ref[...], jnp.concatenate([real, imag], axis=0))


def convolve(
    heads, other_ref, mine_ref, before_ref, own_taps_ref, starts_ref, product_ref, gate_ref, skip_ref,
    ahead_ref, wide_back_ref, out_ref, taps_ref, filter_ref, sum_ref, early_ref, late_ref, back_ref,
):
    rows = product_ref.shape[0]
    early_ref[...] = split(ahead_ref[:, :rows])
    late_ref[...] = split(ahead_ref[:, rows:])
    back_ref[...] = wide_back_ref[...].astype(jnp.bfloat16)
    height, width = own_taps_ref.shape
    panel = lax.axis_index("tp")
    even = lax.rem(lax.axis_index("ctx"), 2) == 0
    everything = slice(None)

    def store(step, part, value):
        line = pl.ds(pl.multiple_of((panel ^ step) * height, height), height)
        taps_ref[line, part * 2 * HD : (part + 1) * 2 * HD] = value

    parts = width // (2 * HD)
    for part in range(parts):
        line = slice(part * height, (part + 1) * height)
        mine_far, other_far = mine_ref[heads, line], other_ref[heads, line]
        store(0, part, columns_of(own_taps_ref, everything, part))
        store(1, part, jnp.where(even, other_ref[heads + 1, line], mine_ref[heads + 1, line]))
        store(2, part, jnp.where(even, other_far, mine_far))
        store(3, part, jnp.where(even, mine_far, other_far))
    filter_ref[...] = dot(early_ref[...], twice(taps_ref[...]))
    starts = document_starts(starts_ref, rows)
    line = lax.broadcasted_iota(jnp.int32, (rows, 1), 0)
    zero = jnp.zeros((), jnp.bfloat16)

    begin = jnp.min(starts)
    past = jnp.where(line - rows >= begin, before_ref[...], zero)
    here = jnp.where(line >= begin, product_ref[...], zero)
    spectrum = dot(early_ref[...], twice(past)) + dot(late_ref[...], twice(here))
    sum_ref[...] = filtered(spectrum, filter_ref, back_ref)

    def one_document(begin):
        here = jnp.where(line >= begin, product_ref[...], zero)
        result = filtered(dot(late_ref[...], twice(here)), filter_ref, back_ref)
        sum_ref[...] = jnp.where(line >= begin, result, sum_ref[...])
        return jnp.min(jnp.where(starts > begin, starts, rows))

    second = jnp.min(jnp.where(starts > begin, starts, rows))
    lax.while_loop(lambda begin: begin < rows, one_document, second)
    out_ref[...] = (
        gate_ref[0].astype(jnp.float32)
        * (skip_ref[...] * product_ref[...].astype(jnp.float32) + sum_ref[...])
    ).astype(jnp.bfloat16)


def twiddles(rows):
    window = 2 * rows
    order = np.arange(rows)[:, None] * 2 + 1
    angle = np.pi * ((order * np.arange(window)[None, :]) % (2 * window)) / window
    ahead = np.concatenate([np.cos(angle), -np.sin(angle)], axis=0)
    back = ahead.T[rows:] / rows
    return jnp.asarray(ahead, jnp.float32), jnp.asarray(back, jnp.float32)


def taps_pairs(peers, panels):
    assert panels == 4
    near, far = [], []
    for peer in range(peers):
        for panel in range(panels):
            here = peer * panels + panel
            far.append((here, peer * panels + (panel ^ (3 - peer % 2))))
            if peer % 2 == 1:
                near.append((here, peer * panels + (panel ^ 1)))
    return near, far


def local(hyena_inputs, filters, skip_bias, queries, keys_values, doc_start):
    rows = queries.shape[0]
    channels = hyena_inputs.shape[2]
    heads = queries.shape[1] // HD
    count = heads // 2
    peers = lax.axis_size("ctx")
    bf16, f32 = jnp.bfloat16, jnp.float32
    shape = jax.ShapeDtypeStruct
    starts = doc_start.reshape(1, rows)

    height = filters.shape[0]

    def pinned(*arrays):
        return [pltpu.with_memory_space_constraint(x, pltpu.HBM) for x in arrays]

    packed = call(
        functools.partial(pack_heads, heads),
        (shape((6 * rows + NOTE_ROWS, HD), bf16),) * count,
        pinned(queries, keys_values.reshape(2 * rows, heads * HD), starts),
        0,
        4 * queries.size * 3,
        scratch=(
            pltpu.VMEM((1, rows), jnp.int32),
            pltpu.SemaphoreType.DMA,
            pltpu.SemaphoreType.DMA((count, 4)),
        ),
        specs=[hbm()] * 3,
    )
    assert count == len(STEPS)
    arrived = [packed[0]] + [crossed(packed[i], "ctx", 2 * STEPS[i]) for i in range(1, count)]
    product, own_taps, far_taps, near_taps = call(
        pack_hyena,
        (shape((rows, channels), bf16),) + (shape((height, channels), bf16),) * 3,
        (hyena_inputs, *pinned(filters)),
        0,
        4 * queries.size * 3,
        scratch=(pltpu.VMEM((3, height, channels), f32), pltpu.SemaphoreType.DMA((3,))),
        specs=[vmem(), hbm()],
    )
    axes = ("ctx", "tp")
    near_pairs, far_pairs = taps_pairs(peers, lax.axis_size("tp"))
    near_taps = lax.ppermute(near_taps, axes, near_pairs)
    far_taps = lax.ppermute(far_taps, axes, far_pairs)
    before = lax.ppermute(product, "ctx", [(i, i + 1) for i in range(peers - 1)])
    query, key_value = call(
        functools.partial(sort_heads, heads),
        (
            shape((count, rows + NOTE_ROWS, 2 * HD), bf16),
            shape((heads + 2, rows, 2 * HD), bf16),
        ),
        (*arrived, near_taps, far_taps),
        0,
        4 * queries.size * 3,
    )
    other = crossed(key_value, "ctx", 1)
    units = count // UNIT
    partial = call(
        functools.partial(attend_first, heads),
        (
            shape((2, units, 1, UNIT * rows), f32),
            shape((2, units, 1, UNIT * rows), f32),
            shape((2, units, HD, UNIT * rows), f32),
        ),
        (query, key_value),
        LONG * (heads * rows) ** 2 * HD,
        4 * queries.size * 4,
    )
    operands = [query, *partial, other]
    if peers > heads:
        pairs = [(i, i + heads) for i in range(peers - heads)]
        operands += [lax.ppermute(each, "ctx", pairs) for each in (key_value, other)]
    assert count == 2 * UNIT
    message = shape((2 * rows + NOTE_ROWS, HD), bf16)

    def second(mine, *more):
        return call(
            functools.partial(attend_second, heads, mine),
            (message,) * UNIT,
            (*operands, *more),
            (heads * rows) ** 2 * HD,
            4 * queries.size * 4,
            scratch=(pltpu.VMEM((UNIT, 2 * rows + NOTE_ROWS, HD), bf16),),
        )

    theirs = second(False)
    own = second(True, theirs[0])
    returned = [own[0], crossed(theirs[0], "ctx", 4), crossed(theirs[1], "ctx", 6)]
    returned.append(crossed(own[1], "ctx", 2))
    hyena_out = call(
        functools.partial(convolve, heads),
        shape((rows, channels), bf16),
        (
            other, key_value, before, own_taps, starts, product, hyena_inputs,
            skip_bias.reshape(1, channels), *twiddles(rows),
        ),
        2 * 4 * 256 * 256 * channels,
        4 * queries.size * 4,
        scratch=(
            pltpu.VMEM((FLEN, channels), bf16),
            pltpu.VMEM((2 * rows, channels), f32),
            pltpu.VMEM((rows, channels), f32),
            pltpu.VMEM((2 * rows, 2 * rows), bf16),
            pltpu.VMEM((2 * rows, 2 * rows), bf16),
            pltpu.VMEM((rows, 2 * rows), bf16),
        ),
    )
    attention_out, log_totals = call(
        functools.partial(unpack_heads, heads, (0, 2, 3, 1)),
        (shape((rows, heads * HD), bf16), shape((heads, rows), f32)),
        returned,
        0,
        4 * queries.size,
    )
    return (hyena_out, attention_out, log_totals)


def solution(mesh):
    in_specs = (
        P(None, "ctx", "tp"),
        P("tp", None),
        P("tp"),
        P("ctx", "tp"),
        P(None, "ctx", "tp"),
        P("ctx"),
    )
    out_specs = (P("ctx", "tp"), P("ctx", "tp"), P("tp", "ctx"))
    return jax.shard_map(local, mesh=mesh, in_specs=in_specs, out_specs=out_specs, check_vma=False)
```

```python
import functools
import math

import jax
import jax.numpy as jnp
import numpy as np
from jax import lax
from jax.experimental import pallas as pl
from jax.experimental.pallas import tpu as pltpu
from jax.sharding import PartitionSpec as P

HD = 128
FLEN = 128
DIGIT = 256
NOTE_ROWS = 16
MASKED = -1e30
VMEM_LIMIT = 16 * 1024 * 1024
LONG = 200


def vmem():
    return pl.BlockSpec(memory_space=pltpu.VMEM)


def hbm():
    return pl.BlockSpec(memory_space=pltpu.HBM)


def call(kernel, out_shape, args, flops, nbytes, scratch=(), specs=None):
    return pl.pallas_call(
        kernel,
        out_shape=out_shape,
        in_specs=specs or [vmem() for _ in args],
        out_specs=jax.tree.map(lambda _: vmem(), out_shape),
        scratch_shapes=list(scratch),
        compiler_params=pltpu.CompilerParams(vmem_limit_bytes=VMEM_LIMIT),
        cost_estimate=pl.CostEstimate(flops=flops, bytes_accessed=nbytes, transcendentals=0),
    )(*args)


def crossed(array, axis, bits):
    return lax.ppermute(array, axis, [(i, i ^ bits) for i in range(lax.axis_size(axis))])


STEPS = (0, 2, 1, 3)


def place(heads):
    index = lax.axis_index("ctx")
    member = lax.rem(index, heads)
    return index // heads, member // 2, lax.rem(member, 2)


def pack_heads(heads, queries_ref, keys_values_ref, starts_ref, *refs):
    *outs, held_ref, start_sem, sem = refs
    rows = queries_ref.shape[0]
    _, pair, _ = place(heads)
    first = pltpu.make_async_copy(starts_ref, held_ref, start_sem)
    first.start()
    copies = []
    for step, out in zip(STEPS, outs):
        for head in range(2):
            columns = pl.ds(pl.multiple_of(((pair ^ step) * 2 + head) * HD, HD), HD)
            first_row = head * 3 * rows
            for part, source in enumerate((queries_ref, keys_values_ref)):
                lines = pl.ds(first_row + part * rows, source.shape[0])
                copies.append(
                    pltpu.make_async_copy(
                        source.at[:, columns], out.at[lines], sem.at[step, 2 * head + part]
                    )
                )
    for copy in copies:
        copy.start()
    first.wait()
    starts = held_ref[...]
    high = (starts // DIGIT).astype(jnp.float32)
    low = (starts % DIGIT).astype(jnp.float32)
    line = lax.broadcasted_iota(jnp.int32, (NOTE_ROWS, rows), 0)
    note = jnp.where(line == 0, high, jnp.where(line == 1, low, 0.0)).astype(jnp.bfloat16)
    for out in outs:
        out[6 * rows :] = note
    for copy in copies:
        copy.wait()


def split(matrix):
    high = matrix.astype(jnp.bfloat16)
    low = (matrix - high.astype(jnp.float32)).astype(jnp.bfloat16)
    return jnp.concatenate([high, low], axis=1)


def pack_hyena(hyena_ref, filters_ref, product_ref, own_ref, far_ref, near_ref, taps_ref, sem):
    width = own_ref.shape[1]
    panel = lax.axis_index("tp")
    parity = lax.rem(lax.axis_index("ctx"), 2)
    copies = []
    for index, target in enumerate((panel, panel ^ (3 - parity), panel ^ 1)):
        columns = pl.ds(pl.multiple_of(target * width, width), width)
        copies.append(
            pltpu.make_async_copy(filters_ref.at[:, columns], taps_ref.at[index], sem.at[index])
        )
    for copy in copies:
        copy.start()
    product_ref[...] = (hyena_ref[1].astype(jnp.float32) * hyena_ref[2].astype(jnp.float32)).astype(
        jnp.bfloat16
    )
    for copy in copies:
        copy.wait()
    for index, out in enumerate((own_ref, far_ref, near_ref)):
        out[...] = taps_ref[index].astype(jnp.bfloat16)


def columns_of(ref, rows, index):
    return ref[rows, index * 2 * HD : (index + 1) * 2 * HD]


def sort_heads(heads, *refs):
    count = heads // 2
    near_ref, far_ref = refs[count : count + 2]
    query_ref, side_ref = refs[-2:]
    rows = (refs[0].shape[0] - NOTE_ROWS) // 6
    _, pair, _ = place(heads)
    for step, ref in zip(STEPS, refs):
        source = pair ^ step
        query_ref[source, rows:, :HD] = ref[6 * rows :]
        for head in range(2):
            columns = slice(head * HD, (head + 1) * HD)
            first = head * 3 * rows
            query_ref[source, :rows, columns] = ref[first : first + rows]
            for part in range(2):
                line = first + (part + 1) * rows
                side_ref[2 * source + part, :, columns] = ref[line : line + rows]
    height, width = far_ref.shape
    parts = width // (2 * HD)
    for part in range(parts):
        line = slice(part * height, (part + 1) * height)
        side_ref[heads, line] = columns_of(far_ref, slice(None), part)
        side_ref[heads + 1, line] = columns_of(near_ref, slice(None), part)


UNIT = 2


def key_set(ref, blocks, head, origin, parity, causal):
    columns = slice(head * HD, (head + 1) * HD)
    rows = ref.shape[1]
    key = jnp.concatenate([ref[2 * block, :, columns] for block in range(blocks)], axis=0)
    value = jnp.concatenate([ref[2 * block + 1, :, columns] for block in range(blocks)], axis=0)
    return key, value, [(2 * block + parity) * rows + origin for block in range(blocks)], causal


def masked_scores(sets, query, start, own, begin):
    held = [[] for _ in range(UNIT)]
    for key, _, firsts, causal in sets:
        scores = lax.dot_general(
            key, query, (((1,), (1,)), ((), ())), preferred_element_type=jnp.float32
        )
        rows = key.shape[0] // len(firsts)
        line = lax.broadcasted_iota(jnp.int32, (rows, rows), 0)
        for block, first in enumerate(firsts):
            for index in range(UNIT):
                if causal and block > begin + index:
                    held[index].append(None)
                    continue
                lanes = slice(index * rows, (index + 1) * rows)
                allowed = line >= start[:, lanes] - first
                if causal and block == begin + index:
                    allowed &= line <= own[:, lanes] - first
                part = scores[block * rows : (block + 1) * rows, lanes]
                held[index].append(jnp.where(allowed, part, MASKED))
    return held


def highest(held):
    tops = [functools.reduce(jnp.maximum, [x for x in parts if x is not None]) for parts in held]
    return jnp.concatenate([jnp.max(top, axis=0, keepdims=True) for top in tops], axis=1)


def weigh(held, top):
    totals, rounded = [], []
    for index, parts in enumerate(held):
        rows = next(x for x in parts if x is not None).shape[1]
        here = top[:, index * rows : (index + 1) * rows]
        weights = [None if x is None else jnp.exp2((x - here) * FACTOR) for x in parts]
        total = functools.reduce(jnp.add, [x for x in weights if x is not None])
        totals.append(jnp.sum(total, axis=0, keepdims=True))
        rounded.append(
            [
                jnp.zeros((rows, rows), jnp.bfloat16) if x is None else x.astype(jnp.bfloat16)
                for x in weights
            ]
        )
    lines = [jnp.concatenate(line, axis=1) for line in zip(*rounded)]
    return jnp.concatenate(totals, axis=1), jnp.concatenate(lines, axis=0)


def mix(sets, rounded):
    return dot(jnp.concatenate([one[1] for one in sets], axis=0).T, rounded)


def unit_rows(heads, query_ref, begin):
    rows = query_ref.shape[1] - NOTE_ROWS
    group, _, parity = place(heads)
    starts = []
    for block in range(begin, begin + UNIT):
        note = query_ref[block, rows:, :HD].astype(jnp.float32)
        starts.append(note[0:1] * float(DIGIT) + note[1:2])
    start = jnp.concatenate(starts, axis=1).astype(jnp.int32) - group * (heads * rows)
    line = lax.broadcasted_iota(jnp.int32, (1, UNIT * rows), 1)
    own = line // rows * rows + line + (2 * begin + parity) * rows
    return start, own


def unit_queries(query_ref, head, begin):
    rows = query_ref.shape[1] - NOTE_ROWS
    blocks = range(begin, begin + UNIT)
    columns = slice(head * HD, (head + 1) * HD)
    return jnp.concatenate([query_ref[block, :rows, columns] for block in blocks], axis=0)


FACTOR = math.log2(math.e) / math.sqrt(HD)


def attend_first(heads, query_ref, key_value_ref, top_ref, total_ref, mixed_ref):
    _, _, parity = place(heads)
    for unit in range(heads // 2 // UNIT):
        begin = unit * UNIT
        start, own = unit_rows(heads, query_ref, begin)
        sets = [[key_set(key_value_ref, begin + UNIT, head, 0, parity, True)] for head in range(2)]
        held = [
            masked_scores(sets[head], unit_queries(query_ref, head, begin), start, own, begin)
            for head in range(2)
        ]
        tops = [highest(each) for each in held]
        weights = [weigh(each, top) for each, top in zip(held, tops)]
        for head, (total, rounded) in enumerate(weights):
            top_ref[head, unit] = tops[head]
            total_ref[head, unit] = total
            mixed_ref[head, unit] = mix(sets[head], rounded)


def attend_second(heads, *refs):
    count = heads // 2
    query_ref, top_ref, total_ref, mixed_ref, other_ref, *more = refs[: -count - 1]
    outs, held_ref = refs[-count - 1 : -1], refs[-1]
    rows = query_ref.shape[1] - NOTE_ROWS
    _, pair, parity = place(heads)

    def one_unit(unit):
        begin = unit * UNIT
        start, own = unit_rows(heads, query_ref, begin)
        sets, held, tops = [], [], []
        for head in range(2):
            sets.append([key_set(other_ref, begin + UNIT, head, 0, 1 - parity, True)])
            for ref, side in zip(more, (parity, 1 - parity)):
                sets[head].append(key_set(ref, count, head, -heads * rows, side, False))
            query = unit_queries(query_ref, head, begin)
            held.append(masked_scores(sets[head], query, start, own, begin))
        for head in range(2):
            tops.append(jnp.maximum(top_ref[head, unit], highest(held[head])))
        weights = [weigh(each, top) for each, top in zip(held, tops)]
        notes = jnp.zeros((NOTE_ROWS, UNIT * rows), jnp.float32)
        for head, (total, rounded) in enumerate(weights):
            top = tops[head]
            scale = jnp.exp2((top_ref[head, unit] - top) * FACTOR)
            total = total_ref[head, unit] * scale + total
            mixed = mixed_ref[head, unit] * scale + mix(sets[head], rounded)
            mixed = (mixed * (1.0 / total)).astype(jnp.bfloat16).T
            logs = top * (1.0 / math.sqrt(HD)) + jnp.log(total)
            high = logs.astype(jnp.bfloat16).astype(jnp.float32)
            middle = (logs - high).astype(jnp.bfloat16).astype(jnp.float32)
            low = logs - high - middle
            line = lax.broadcasted_iota(jnp.int32, (NOTE_ROWS, UNIT * rows), 0) - 3 * head
            for index, part in enumerate((high, middle, low)):
                notes = jnp.where(line == index, part, notes)
            for index in range(UNIT):
                held_ref[begin + index, head * rows : (head + 1) * rows] = mixed[
                    index * rows : (index + 1) * rows
                ]
        for index in range(UNIT):
            held_ref[begin + index, 2 * rows :] = notes[:, index * rows : (index + 1) * rows].astype(
                jnp.bfloat16
            )

    for unit in range(count // UNIT):
        one_unit(unit)
    for step, out in enumerate(outs):
        out[...] = held_ref[pair ^ step]


def unpack_heads(heads, steps, *refs):
    *sources, out_ref, logs_ref = refs
    rows = out_ref.shape[0]
    _, pair, _ = place(heads)
    for step, source in zip(steps, sources):
        owner = pair ^ step
        note = source[2 * rows :].astype(jnp.float32)
        for head in range(2):
            columns = pl.ds(pl.multiple_of((owner * 2 + head) * HD, HD), HD)
            out_ref[:, columns] = source[head * rows : (head + 1) * rows]
            parts = [note[3 * head + index : 3 * head + index + 1] for index in range(3)]
            logs_ref[pl.ds(owner * 2 + head, 1), :] = parts[0] + parts[1] + parts[2]


def dot(left, right):
    return jnp.dot(left, right, preferred_element_type=jnp.float32)


def twice(array):
    return jnp.concatenate([array, array], axis=0)


def document_starts(starts_ref, rows):
    return jnp.maximum(starts_ref[...] - lax.axis_index("ctx") * rows, -rows)


def filtered(spectrum, filter_ref, back_ref):
    half = spectrum.shape[0] // 2
    even, odd = spectrum[:half], spectrum[half:]
    tap_even, tap_odd = filter_ref[:half], filter_ref[half:]
    real = (even * tap_even - odd * tap_odd).astype(jnp.bfloat16)
    imag = (even * tap_odd + odd * tap_even).astype(jnp.bfloat16)
    return dot(back_ref[...], jnp.concatenate([real, imag], axis=0))


def convolve(
    heads, other_ref, mine_ref, before_ref, own_taps_ref, starts_ref, product_ref, gate_ref, skip_ref,
    ahead_ref, wide_back_ref, out_ref, taps_ref, filter_ref, sum_ref, early_ref, late_ref, back_ref,
):
    rows = product_ref.shape[0]
    early_ref[...] = split(ahead_ref[:, :rows])
    late_ref[...] = split(ahead_ref[:, rows:])
    back_ref[...] = wide_back_ref[...].astype(jnp.bfloat16)
    height, width = own_taps_ref.shape
    panel = lax.axis_index("tp")
    even = lax.rem(lax.axis_index("ctx"), 2) == 0
    everything = slice(None)

    def store(step, part, value):
        line = pl.ds(pl.multiple_of((panel ^ step) * height, height), height)
        taps_ref[line, part * 2 * HD : (part + 1) * 2 * HD] = value

    parts = width // (2 * HD)
    for part in range(parts):
        line = slice(part * height, (part + 1) * height)
        mine_far, other_far = mine_ref[heads, line], other_ref[heads, line]
        store(0, part, columns_of(own_taps_ref, everything, part))
        store(1, part, jnp.where(even, other_ref[heads + 1, line], mine_ref[heads + 1, line]))
        store(2, part, jnp.where(even, other_far, mine_far))
        store(3, part, jnp.where(even, mine_far, other_far))
    filter_ref[...] = dot(early_ref[...], twice(taps_ref[...]))
    starts = document_starts(starts_ref, rows)
    line = lax.broadcasted_iota(jnp.int32, (rows, 1), 0)
    zero = jnp.zeros((), jnp.bfloat16)

    begin = jnp.min(starts)
    past = jnp.where(line - rows >= begin, before_ref[...], zero)
    here = jnp.where(line >= begin, product_ref[...], zero)
    spectrum = dot(early_ref[...], twice(past)) + dot(late_ref[...], twice(here))
    sum_ref[...] = filtered(spectrum, filter_ref, back_ref)

    def one_document(begin):
        here = jnp.where(line >= begin, product_ref[...], zero)
        result = filtered(dot(late_ref[...], twice(here)), filter_ref, back_ref)
        sum_ref[...] = jnp.where(line >= begin, result, sum_ref[...])
        return jnp.min(jnp.where(starts > begin, starts, rows))

    second = jnp.min(jnp.where(starts > begin, starts, rows))
    lax.while_loop(lambda begin: begin < rows, one_document, second)
    out_ref[...] = (
        gate_ref[0].astype(jnp.float32)
        * (skip_ref[...] * product_ref[...].astype(jnp.float32) + sum_ref[...])
    ).astype(jnp.bfloat16)


def twiddles(rows):
    window = 2 * rows
    order = np.arange(rows)[:, None] * 2 + 1
    angle = np.pi * ((order * np.arange(window)[None, :]) % (2 * window)) / window
    ahead = np.concatenate([np.cos(angle), -np.sin(angle)], axis=0)
    back = ahead.T[rows:] / rows
    return jnp.asarray(ahead, jnp.float32), jnp.asarray(back, jnp.float32)


def taps_pairs(peers, panels):
    assert panels == 4
    near, far = [], []
    for peer in range(peers):
        for panel in range(panels):
            here = peer * panels + panel
            far.append((here, peer * panels + (panel ^ (3 - peer % 2))))
            if peer % 2 == 1:
                near.append((here, peer * panels + (panel ^ 1)))
    return near, far


def local(hyena_inputs, filters, skip_bias, queries, keys_values, doc_start):
    rows = queries.shape[0]
    channels = hyena_inputs.shape[2]
    heads = queries.shape[1] // HD
    count = heads // 2
    peers = lax.axis_size("ctx")
    bf16, f32 = jnp.bfloat16, jnp.float32
    shape = jax.ShapeDtypeStruct
    starts = doc_start.reshape(1, rows)

    height = filters.shape[0]

    def pinned(*arrays):
        return [pltpu.with_memory_space_constraint(x, pltpu.HBM) for x in arrays]

    *packed, near_starts = call(
        functools.partial(pack_heads, heads),
        (shape((6 * rows + NOTE_ROWS, HD), bf16),) * count + (shape((1, rows), jnp.int32),),
        pinned(queries, keys_values.reshape(2 * rows, heads * HD), starts),
        0,
        4 * queries.size * 3,
        scratch=(pltpu.SemaphoreType.DMA, pltpu.SemaphoreType.DMA((count, 4))),
        specs=[hbm()] * 3,
    )
    assert count == len(STEPS)
    arrived = [packed[0]] + [crossed(packed[i], "ctx", 2 * STEPS[i]) for i in range(1, count)]
    product, own_taps, far_taps, near_taps = call(
        pack_hyena,
        (shape((rows, channels), bf16),) + (shape((height, channels), bf16),) * 3,
        (hyena_inputs, *pinned(filters)),
        0,
        4 * queries.size * 3,
        scratch=(pltpu.VMEM((3, height, channels), f32), pltpu.SemaphoreType.DMA((3,))),
        specs=[vmem(), hbm()],
    )
    axes = ("ctx", "tp")
    near_pairs, far_pairs = taps_pairs(peers, lax.axis_size("tp"))
    near_taps = lax.ppermute(near_taps, axes, near_pairs)
    far_taps = lax.ppermute(far_taps, axes, far_pairs)
    before = lax.ppermute(product, "ctx", [(i, i + 1) for i in range(peers - 1)])
    query, key_value = call(
        functools.partial(sort_heads, heads),
        (
            shape((count, rows + NOTE_ROWS, 2 * HD), bf16),
            shape((heads + 2, rows, 2 * HD), bf16),
        ),
        (*arrived, near_taps, far_taps),
        0,
        4 * queries.size * 3,
    )
    other = crossed(key_value, "ctx", 1)
    units = count // UNIT
    partial = call(
        functools.partial(attend_first, heads),
        (
            shape((2, units, 1, UNIT * rows), f32),
            shape((2, units, 1, UNIT * rows), f32),
            shape((2, units, HD, UNIT * rows), f32),
        ),
        (query, key_value),
        LONG * (heads * rows) ** 2 * HD,
        4 * queries.size * 4,
    )
    operands = [query, *partial, other]
    if peers > heads:
        pairs = [(i, i + heads) for i in range(peers - heads)]
        operands += [lax.ppermute(each, "ctx", pairs) for each in (key_value, other)]
    assert count == 2 * UNIT
    message = shape((2 * rows + NOTE_ROWS, HD), bf16)

    mixed = call(
        functools.partial(attend_second, heads),
        (message,) * count,
        operands,
        2 * (heads * rows) ** 2 * HD,
        4 * queries.size * 4,
        scratch=(pltpu.VMEM((count, 2 * rows + NOTE_ROWS, HD), bf16),),
    )
    returned = [mixed[0]] + [crossed(mixed[step], "ctx", 2 * step) for step in (2, 3, 1)]
    hyena_out = call(
        functools.partial(convolve, heads),
        shape((rows, channels), bf16),
        (
            other, key_value, before, own_taps, near_starts, product, hyena_inputs,
            skip_bias.reshape(1, channels), *twiddles(rows),
        ),
        2 * 4 * 256 * 256 * channels,
        4 * queries.size * 4,
        scratch=(
            pltpu.VMEM((FLEN, channels), bf16),
            pltpu.VMEM((2 * rows, channels), f32),
            pltpu.VMEM((rows, channels), f32),
            pltpu.VMEM((2 * rows, 2 * rows), bf16),
            pltpu.VMEM((2 * rows, 2 * rows), bf16),
            pltpu.VMEM((rows, 2 * rows), bf16),
        ),
    )
    attention_out, log_totals = call(
        functools.partial(unpack_heads, heads, (0, 2, 3, 1)),
        (shape((rows, heads * HD), bf16), shape((heads, rows), f32)),
        returned,
        0,
        4 * queries.size,
    )
    return (hyena_out, attention_out, log_totals)


def solution(mesh):
    in_specs = (
        P(None, "ctx", "tp"),
        P("tp", None),
        P("tp"),
        P("ctx", "tp"),
        P(None, "ctx", "tp"),
        P("ctx"),
    )
    out_specs = (P("ctx", "tp"), P("ctx", "tp"), P("tp", "ctx"))
    return jax.shard_map(local, mesh=mesh, in_specs=in_specs, out_specs=out_specs, check_vma=False)
```

```python
import functools
import math

import jax
import jax.numpy as jnp
import numpy as np
from jax import lax
from jax.experimental import pallas as pl
from jax.experimental.pallas import tpu as pltpu
from jax.sharding import PartitionSpec as P

HD = 128
FLEN = 128
DIGIT = 256
NOTE_ROWS = 16
MASKED = -1e30
VMEM_LIMIT = 16 * 1024 * 1024
LONG = 200


def vmem():
    return pl.BlockSpec(memory_space=pltpu.VMEM)


def hbm():
    return pl.BlockSpec(memory_space=pltpu.HBM)


def call(kernel, out_shape, args, flops, nbytes, scratch=(), specs=None):
    return pl.pallas_call(
        kernel,
        out_shape=out_shape,
        in_specs=specs or [vmem() for _ in args],
        out_specs=jax.tree.map(lambda _: vmem(), out_shape),
        scratch_shapes=list(scratch),
        compiler_params=pltpu.CompilerParams(vmem_limit_bytes=VMEM_LIMIT),
        cost_estimate=pl.CostEstimate(flops=flops, bytes_accessed=nbytes, transcendentals=0),
    )(*args)


def crossed(array, axis, bits):
    return lax.ppermute(array, axis, [(i, i ^ bits) for i in range(lax.axis_size(axis))])


STEPS = (0, 2, 1, 3)


def place(heads):
    index = lax.axis_index("ctx")
    member = lax.rem(index, heads)
    return index // heads, member // 2, lax.rem(member, 2)


def pack_heads(heads, queries_ref, keys_values_ref, starts_ref, *refs):
    *outs, held_ref, start_sem, sem = refs
    rows = queries_ref.shape[0]
    _, pair, _ = place(heads)
    first = pltpu.make_async_copy(starts_ref, held_ref, start_sem)
    first.start()
    copies = []
    for step, out in zip(STEPS, outs):
        for head in range(2):
            columns = pl.ds(pl.multiple_of(((pair ^ step) * 2 + head) * HD, HD), HD)
            first_row = head * 3 * rows
            for part, source in enumerate((queries_ref, keys_values_ref)):
                lines = pl.ds(first_row + part * rows, source.shape[0])
                copies.append(
                    pltpu.make_async_copy(
                        source.at[:, columns], out.at[lines], sem.at[step, 2 * head + part]
                    )
                )
    for copy in copies:
        copy.start()
    first.wait()
    starts = held_ref[...]
    high = (starts // DIGIT).astype(jnp.float32)
    low = (starts % DIGIT).astype(jnp.float32)
    line = lax.broadcasted_iota(jnp.int32, (NOTE_ROWS, rows), 0)
    note = jnp.where(line == 0, high, jnp.where(line == 1, low, 0.0)).astype(jnp.bfloat16)
    for out in outs:
        out[6 * rows :] = note
    for copy in copies:
        copy.wait()


def split(matrix):
    high = matrix.astype(jnp.bfloat16)
    low = (matrix - high.astype(jnp.float32)).astype(jnp.bfloat16)
    return jnp.concatenate([high, low], axis=1)


def pack_hyena(hyena_ref, filters_ref, product_ref, own_ref, far_ref, near_ref, taps_ref, sem):
    width = own_ref.shape[1]
    panel = lax.axis_index("tp")
    parity = lax.rem(lax.axis_index("ctx"), 2)
    copies = []
    for index, target in enumerate((panel, panel ^ (3 - parity), panel ^ 1)):
        columns = pl.ds(pl.multiple_of(target * width, width), width)
        copies.append(
            pltpu.make_async_copy(filters_ref.at[:, columns], taps_ref.at[index], sem.at[index])
        )
    for copy in copies:
        copy.start()
    product_ref[...] = (hyena_ref[1].astype(jnp.float32) * hyena_ref[2].astype(jnp.float32)).astype(
        jnp.bfloat16
    )
    for copy in copies:
        copy.wait()
    for index, out in enumerate((own_ref, far_ref, near_ref)):
        out[...] = taps_ref[index].astype(jnp.bfloat16)


def columns_of(ref, rows, index):
    return ref[rows, index * 2 * HD : (index + 1) * 2 * HD]


def sort_heads(heads, *refs):
    count = heads // 2
    near_ref, far_ref = refs[count : count + 2]
    query_ref, side_ref = refs[-2:]
    rows = (refs[0].shape[0] - NOTE_ROWS) // 6
    _, pair, _ = place(heads)
    for step, ref in zip(STEPS, refs):
        source = pair ^ step
        query_ref[source, rows:, :HD] = ref[6 * rows :]
        for head in range(2):
            columns = slice(head * HD, (head + 1) * HD)
            first = head * 3 * rows
            query_ref[source, :rows, columns] = ref[first : first + rows]
            for part in range(2):
                line = first + (part + 1) * rows
                side_ref[2 * source + part, :, columns] = ref[line : line + rows]
    height, width = far_ref.shape
    parts = width // (2 * HD)
    for part in range(parts):
        line = slice(part * height, (part + 1) * height)
        side_ref[heads, line] = columns_of(far_ref, slice(None), part)
        side_ref[heads + 1, line] = columns_of(near_ref, slice(None), part)


UNIT = 2


def key_set(ref, blocks, head, origin, parity, causal):
    columns = slice(head * HD, (head + 1) * HD)
    rows = ref.shape[1]
    key = jnp.concatenate([ref[2 * block, :, columns] for block in range(blocks)], axis=0)
    value = jnp.concatenate([ref[2 * block + 1, :, columns] for block in range(blocks)], axis=0)
    return key, value, [(2 * block + parity) * rows + origin for block in range(blocks)], causal


def masked_scores(sets, turned, start, own, begin):
    held = [[] for _ in range(UNIT)]
    for key, _, firsts, causal in sets:
        scores = dot(key, turned)
        rows = key.shape[0] // len(firsts)
        line = lax.broadcasted_iota(jnp.int32, (rows, rows), 0)
        for block, first in enumerate(firsts):
            for index in range(UNIT):
                if causal and block > begin + index:
                    held[index].append(None)
                    continue
                lanes = slice(index * rows, (index + 1) * rows)
                allowed = line >= start[:, lanes] - first
                if causal and block == begin + index:
                    allowed &= line <= own[:, lanes] - first
                part = scores[block * rows : (block + 1) * rows, lanes]
                held[index].append(jnp.where(allowed, part, MASKED))
    return held


def highest(held):
    tops = [functools.reduce(jnp.maximum, [x for x in parts if x is not None]) for parts in held]
    return jnp.concatenate([jnp.max(top, axis=0, keepdims=True) for top in tops], axis=1)


def weigh(held, top):
    totals, rounded = [], []
    for index, parts in enumerate(held):
        rows = next(x for x in parts if x is not None).shape[1]
        here = top[:, index * rows : (index + 1) * rows]
        weights = [None if x is None else jnp.exp2((x - here) * FACTOR) for x in parts]
        total = functools.reduce(jnp.add, [x for x in weights if x is not None])
        totals.append(jnp.sum(total, axis=0, keepdims=True))
        rounded.append(
            [
                jnp.zeros((rows, rows), jnp.bfloat16) if x is None else x.astype(jnp.bfloat16)
                for x in weights
            ]
        )
    lines = [jnp.concatenate(line, axis=1) for line in zip(*rounded)]
    return jnp.concatenate(totals, axis=1), jnp.concatenate(lines, axis=0)


def mix(sets, rounded):
    return dot(jnp.concatenate([one[1] for one in sets], axis=0).T, rounded)


def unit_rows(heads, query_ref, begin):
    rows = query_ref.shape[1] - NOTE_ROWS
    group, _, parity = place(heads)
    starts = []
    for block in range(begin, begin + UNIT):
        note = query_ref[block, rows:, :HD].astype(jnp.float32)
        starts.append(note[0:1] * float(DIGIT) + note[1:2])
    start = jnp.concatenate(starts, axis=1).astype(jnp.int32) - group * (heads * rows)
    line = lax.broadcasted_iota(jnp.int32, (1, UNIT * rows), 1)
    own = line // rows * rows + line + (2 * begin + parity) * rows
    return start, own


def unit_queries(query_ref, head, begin):
    rows = query_ref.shape[1] - NOTE_ROWS
    blocks = range(begin, begin + UNIT)
    columns = slice(head * HD, (head + 1) * HD)
    return jnp.concatenate([query_ref[block, :rows, columns] for block in blocks], axis=0)


FACTOR = math.log2(math.e) / math.sqrt(HD)


def attend_first(heads, query_ref, key_value_ref, top_ref, total_ref, mixed_ref, turned_ref):
    _, _, parity = place(heads)
    for unit in range(heads // 2 // UNIT):
        begin = unit * UNIT
        start, own = unit_rows(heads, query_ref, begin)
        sets = [[key_set(key_value_ref, begin + UNIT, head, 0, parity, True)] for head in range(2)]
        for head in range(2):
            turned_ref[head, unit] = unit_queries(query_ref, head, begin).T
        held = [
            masked_scores(sets[head], turned_ref[head, unit], start, own, begin) for head in range(2)
        ]
        tops = [highest(each) for each in held]
        weights = [weigh(each, top) for each, top in zip(held, tops)]
        for head, (total, rounded) in enumerate(weights):
            top_ref[head, unit] = tops[head]
            total_ref[head, unit] = total
            mixed_ref[head, unit] = mix(sets[head], rounded)


def attend_second(heads, mine, *refs):
    count = heads // 2
    query_ref, top_ref, total_ref, mixed_ref, turned_ref, other_ref, *more = refs[: -UNIT - 1]
    outs, held_ref = refs[-UNIT - 1 : -1], refs[-1]
    more = more[: len(more) // 2 * 2]
    rows = query_ref.shape[1] - NOTE_ROWS
    _, pair, parity = place(heads)
    here = pair // UNIT

    def one_unit(unit):
        begin = unit * UNIT
        start, own = unit_rows(heads, query_ref, begin)
        sets, held, tops = [], [], []
        for head in range(2):
            sets.append([key_set(other_ref, begin + UNIT, head, 0, 1 - parity, True)])
            for ref, side in zip(more, (parity, 1 - parity)):
                sets[head].append(key_set(ref, count, head, -heads * rows, side, False))
            held.append(masked_scores(sets[head], turned_ref[head, unit], start, own, begin))
        for head in range(2):
            tops.append(jnp.maximum(top_ref[head, unit], highest(held[head])))
        weights = [weigh(each, top) for each, top in zip(held, tops)]
        notes = jnp.zeros((NOTE_ROWS, UNIT * rows), jnp.float32)
        for head, (total, rounded) in enumerate(weights):
            top = tops[head]
            scale = jnp.exp2((top_ref[head, unit] - top) * FACTOR)
            total = total_ref[head, unit] * scale + total
            mixed = mixed_ref[head, unit] * scale + mix(sets[head], rounded)
            mixed = (mixed * (1.0 / total)).astype(jnp.bfloat16).T
            logs = top * (1.0 / math.sqrt(HD)) + jnp.log(total)
            high = logs.astype(jnp.bfloat16).astype(jnp.float32)
            middle = (logs - high).astype(jnp.bfloat16).astype(jnp.float32)
            low = logs - high - middle
            line = lax.broadcasted_iota(jnp.int32, (NOTE_ROWS, UNIT * rows), 0) - 3 * head
            for index, part in enumerate((high, middle, low)):
                notes = jnp.where(line == index, part, notes)
            for index in range(UNIT):
                held_ref[index, head * rows : (head + 1) * rows] = mixed[
                    index * rows : (index + 1) * rows
                ]
        for index in range(UNIT):
            held_ref[index, 2 * rows :] = notes[:, index * rows : (index + 1) * rows].astype(
                jnp.bfloat16
            )

    for unit in range(count // UNIT):

        @pl.when((here == unit) if mine else (here != unit))
        def _():
            one_unit(unit)

    for step, out in enumerate(outs):
        out[...] = held_ref[lax.rem(pair, UNIT) ^ step]


def unpack_heads(heads, steps, *refs):
    *sources, out_ref, logs_ref = refs
    rows = out_ref.shape[0]
    _, pair, _ = place(heads)
    for step, source in zip(steps, sources):
        owner = pair ^ step
        note = source[2 * rows :].astype(jnp.float32)
        for head in range(2):
            columns = pl.ds(pl.multiple_of((owner * 2 + head) * HD, HD), HD)
            out_ref[:, columns] = source[head * rows : (head + 1) * rows]
            parts = [note[3 * head + index : 3 * head + index + 1] for index in range(3)]
            logs_ref[pl.ds(owner * 2 + head, 1), :] = parts[0] + parts[1] + parts[2]


def dot(left, right):
    return jnp.dot(left, right, preferred_element_type=jnp.float32)


def twice(array):
    return jnp.concatenate([array, array], axis=0)


def document_starts(starts_ref, rows):
    return jnp.maximum(starts_ref[...] - lax.axis_index("ctx") * rows, -rows)


def filtered(spectrum, filter_ref, back_ref):
    half = spectrum.shape[0] // 2
    even, odd = spectrum[:half], spectrum[half:]
    tap_even, tap_odd = filter_ref[:half], filter_ref[half:]
    real = (even * tap_even - odd * tap_odd).astype(jnp.bfloat16)
    imag = (even * tap_odd + odd * tap_even).astype(jnp.bfloat16)
    return dot(back_ref[...], jnp.concatenate([real, imag], axis=0))


def convolve(
    heads, other_ref, mine_ref, before_ref, own_taps_ref, starts_ref, product_ref, gate_ref, skip_ref,
    ahead_ref, wide_back_ref, out_ref, taps_ref, filter_ref, sum_ref, early_ref, late_ref, back_ref,
):
    rows = product_ref.shape[0]
    early_ref[...] = split(ahead_ref[:, :rows])
    late_ref[...] = split(ahead_ref[:, rows:])
    back_ref[...] = wide_back_ref[...].astype(jnp.bfloat16)
    height, width = own_taps_ref.shape
    panel = lax.axis_index("tp")
    even = lax.rem(lax.axis_index("ctx"), 2) == 0
    everything = slice(None)

    def store(step, part, value):
        line = pl.ds(pl.multiple_of((panel ^ step) * height, height), height)
        taps_ref[line, part * 2 * HD : (part + 1) * 2 * HD] = value

    parts = width // (2 * HD)
    for part in range(parts):
        line = slice(part * height, (part + 1) * height)
        mine_far, other_far = mine_ref[heads, line], other_ref[heads, line]
        store(0, part, columns_of(own_taps_ref, everything, part))
        store(1, part, jnp.where(even, other_ref[heads + 1, line], mine_ref[heads + 1, line]))
        store(2, part, jnp.where(even, other_far, mine_far))
        store(3, part, jnp.where(even, mine_far, other_far))
    filter_ref[...] = dot(early_ref[...], twice(taps_ref[...]))
    starts = document_starts(starts_ref, rows)
    line = lax.broadcasted_iota(jnp.int32, (rows, 1), 0)
    zero = jnp.zeros((), jnp.bfloat16)

    begin = jnp.min(starts)
    past = jnp.where(line - rows >= begin, before_ref[...], zero)
    here = jnp.where(line >= begin, product_ref[...], zero)
    spectrum = dot(early_ref[...], twice(past)) + dot(late_ref[...], twice(here))
    sum_ref[...] = filtered(spectrum, filter_ref, back_ref)

    def one_document(begin):
        here = jnp.where(line >= begin, product_ref[...], zero)
        result = filtered(dot(late_ref[...], twice(here)), filter_ref, back_ref)
        sum_ref[...] = jnp.where(line >= begin, result, sum_ref[...])
        return jnp.min(jnp.where(starts > begin, starts, rows))

    second = jnp.min(jnp.where(starts > begin, starts, rows))
    lax.while_loop(lambda begin: begin < rows, one_document, second)
    out_ref[...] = (
        gate_ref[0].astype(jnp.float32)
        * (skip_ref[...] * product_ref[...].astype(jnp.float32) + sum_ref[...])
    ).astype(jnp.bfloat16)


def twiddles(rows):
    window = 2 * rows
    order = np.arange(rows)[:, None] * 2 + 1
    angle = np.pi * ((order * np.arange(window)[None, :]) % (2 * window)) / window
    ahead = np.concatenate([np.cos(angle), -np.sin(angle)], axis=0)
    back = ahead.T[rows:] / rows
    return jnp.asarray(ahead, jnp.float32), jnp.asarray(back, jnp.float32)


def taps_pairs(peers, panels):
    assert panels == 4
    near, far = [], []
    for peer in range(peers):
        for panel in range(panels):
            here = peer * panels + panel
            far.append((here, peer * panels + (panel ^ (3 - peer % 2))))
            if peer % 2 == 1:
                near.append((here, peer * panels + (panel ^ 1)))
    return near, far


def local(hyena_inputs, filters, skip_bias, queries, keys_values, doc_start):
    rows = queries.shape[0]
    channels = hyena_inputs.shape[2]
    heads = queries.shape[1] // HD
    count = heads // 2
    peers = lax.axis_size("ctx")
    bf16, f32 = jnp.bfloat16, jnp.float32
    shape = jax.ShapeDtypeStruct
    starts = doc_start.reshape(1, rows)

    height = filters.shape[0]

    def pinned(*arrays):
        return [pltpu.with_memory_space_constraint(x, pltpu.HBM) for x in arrays]

    *packed, near_starts = call(
        functools.partial(pack_heads, heads),
        (shape((6 * rows + NOTE_ROWS, HD), bf16),) * count + (shape((1, rows), jnp.int32),),
        pinned(queries, keys_values.reshape(2 * rows, heads * HD), starts),
        0,
        4 * queries.size * 3,
        scratch=(pltpu.SemaphoreType.DMA, pltpu.SemaphoreType.DMA((count, 4))),
        specs=[hbm()] * 3,
    )
    assert count == len(STEPS)
    arrived = [packed[0]] + [crossed(packed[i], "ctx", 2 * STEPS[i]) for i in range(1, count)]
    product, own_taps, far_taps, near_taps = call(
        pack_hyena,
        (shape((rows, channels), bf16),) + (shape((height, channels), bf16),) * 3,
        (hyena_inputs, *pinned(filters)),
        0,
        4 * queries.size * 3,
        scratch=(pltpu.VMEM((3, height, channels), f32), pltpu.SemaphoreType.DMA((3,))),
        specs=[vmem(), hbm()],
    )
    axes = ("ctx", "tp")
    near_pairs, far_pairs = taps_pairs(peers, lax.axis_size("tp"))
    near_taps = lax.ppermute(near_taps, axes, near_pairs)
    far_taps = lax.ppermute(far_taps, axes, far_pairs)
    before = lax.ppermute(product, "ctx", [(i, i + 1) for i in range(peers - 1)])
    query, key_value = call(
        functools.partial(sort_heads, heads),
        (
            shape((count, rows + NOTE_ROWS, 2 * HD), bf16),
            shape((heads + 2, rows, 2 * HD), bf16),
        ),
        (*arrived, near_taps, far_taps),
        0,
        4 * queries.size * 3,
    )
    other = crossed(key_value, "ctx", 1)
    units = count // UNIT
    partial = call(
        functools.partial(attend_first, heads),
        (
            shape((2, units, 1, UNIT * rows), f32),
            shape((2, units, 1, UNIT * rows), f32),
            shape((2, units, HD, UNIT * rows), f32),
            shape((2, units, HD, UNIT * rows), bf16),
        ),
        (query, key_value),
        LONG * (heads * rows) ** 2 * HD,
        4 * queries.size * 4,
    )
    operands = [query, *partial, other]
    if peers > heads:
        pairs = [(i, i + heads) for i in range(peers - heads)]
        operands += [lax.ppermute(each, "ctx", pairs) for each in (key_value, other)]
    assert count == 2 * UNIT
    message = shape((2 * rows + NOTE_ROWS, HD), bf16)

    def second(mine, *more):
        return call(
            functools.partial(attend_second, heads, mine),
            (message,) * UNIT,
            (*operands, *more),
            (heads * rows) ** 2 * HD,
            4 * queries.size * 4,
            scratch=(pltpu.VMEM((UNIT, 2 * rows + NOTE_ROWS, HD), bf16),),
        )

    theirs = second(False)
    own = second(True, theirs[0])
    returned = [own[0], crossed(theirs[0], "ctx", 4), crossed(theirs[1], "ctx", 6)]
    returned.append(crossed(own[1], "ctx", 2))
    hyena_out = call(
        functools.partial(convolve, heads),
        shape((rows, channels), bf16),
        (
            other, key_value, before, own_taps, near_starts, product, hyena_inputs,
            skip_bias.reshape(1, channels), *twiddles(rows),
        ),
        2 * 4 * 256 * 256 * channels,
        4 * queries.size * 4,
        scratch=(
            pltpu.VMEM((FLEN, channels), bf16),
            pltpu.VMEM((2 * rows, channels), f32),
            pltpu.VMEM((rows, channels), f32),
            pltpu.VMEM((2 * rows, 2 * rows), bf16),
            pltpu.VMEM((2 * rows, 2 * rows), bf16),
            pltpu.VMEM((rows, 2 * rows), bf16),
        ),
    )
    attention_out, log_totals = call(
        functools.partial(unpack_heads, heads, (0, 2, 3, 1)),
        (shape((rows, heads * HD), bf16), shape((heads, rows), f32)),
        returned,
        0,
        4 * queries.size,
    )
    return (hyena_out, attention_out, log_totals)


def solution(mesh):
    in_specs = (
        P(None, "ctx", "tp"),
        P("tp", None),
        P("tp"),
        P("ctx", "tp"),
        P(None, "ctx", "tp"),
        P("ctx"),
    )
    out_specs = (P("ctx", "tp"), P("ctx", "tp"), P("tp", "ctx"))
    return jax.shard_map(local, mesh=mesh, in_specs=in_specs, out_specs=out_specs, check_vma=False)
```

```python
import functools
import math

import jax
import jax.numpy as jnp
import numpy as np
from jax import lax
from jax.experimental import pallas as pl
from jax.experimental.pallas import tpu as pltpu
from jax.sharding import PartitionSpec as P

HD = 128
FLEN = 128
DIGIT = 256
NOTE_ROWS = 16
MASKED = -1e30
VMEM_LIMIT = 16 * 1024 * 1024
LONG = 200


def vmem():
    return pl.BlockSpec(memory_space=pltpu.VMEM)


def hbm():
    return pl.BlockSpec(memory_space=pltpu.HBM)


def call(kernel, out_shape, args, flops, nbytes, scratch=(), specs=None):
    return pl.pallas_call(
        kernel,
        out_shape=out_shape,
        in_specs=specs or [vmem() for _ in args],
        out_specs=jax.tree.map(lambda _: vmem(), out_shape),
        scratch_shapes=list(scratch),
        compiler_params=pltpu.CompilerParams(vmem_limit_bytes=VMEM_LIMIT),
        cost_estimate=pl.CostEstimate(flops=flops, bytes_accessed=nbytes, transcendentals=0),
    )(*args)


def crossed(array, axis, bits):
    return lax.ppermute(array, axis, [(i, i ^ bits) for i in range(lax.axis_size(axis))])


STEPS = (0, 2, 1, 3)


def place(heads):
    index = lax.axis_index("ctx")
    member = lax.rem(index, heads)
    return index // heads, member // 2, lax.rem(member, 2)


def pack_heads(heads, queries_ref, keys_values_ref, starts_ref, *refs):
    *outs, held_ref, start_sem, sem = refs
    rows = queries_ref.shape[0]
    _, pair, _ = place(heads)
    first = pltpu.make_async_copy(starts_ref, held_ref, start_sem)
    first.start()
    copies = []
    for step, out in zip(STEPS, outs):
        for head in range(2):
            columns = pl.ds(pl.multiple_of(((pair ^ step) * 2 + head) * HD, HD), HD)
            first_row = head * 3 * rows
            for part, source in enumerate((queries_ref, keys_values_ref)):
                lines = pl.ds(first_row + part * rows, source.shape[0])
                copies.append(
                    pltpu.make_async_copy(
                        source.at[:, columns], out.at[lines], sem.at[step, 2 * head + part]
                    )
                )
    for copy in copies:
        copy.start()
    first.wait()
    starts = held_ref[...]
    high = (starts // DIGIT).astype(jnp.float32)
    low = (starts % DIGIT).astype(jnp.float32)
    line = lax.broadcasted_iota(jnp.int32, (NOTE_ROWS, rows), 0)
    note = jnp.where(line == 0, high, jnp.where(line == 1, low, 0.0)).astype(jnp.bfloat16)
    for out in outs:
        out[6 * rows :] = note
    for copy in copies:
        copy.wait()


def split(matrix):
    high = matrix.astype(jnp.bfloat16)
    low = (matrix - high.astype(jnp.float32)).astype(jnp.bfloat16)
    return jnp.concatenate([high, low], axis=1)


def pack_hyena(hyena_ref, filters_ref, product_ref, own_ref, far_ref, near_ref, taps_ref, sem):
    width = own_ref.shape[1]
    panel = lax.axis_index("tp")
    parity = lax.rem(lax.axis_index("ctx"), 2)
    copies = []
    for index, target in enumerate((panel, panel ^ (2 + parity), panel ^ 1)):
        columns = pl.ds(pl.multiple_of(target * width, width), width)
        copies.append(
            pltpu.make_async_copy(filters_ref.at[:, columns], taps_ref.at[index], sem.at[index])
        )
    for copy in copies:
        copy.start()
    product_ref[...] = (hyena_ref[1].astype(jnp.float32) * hyena_ref[2].astype(jnp.float32)).astype(
        jnp.bfloat16
    )
    for copy in copies:
        copy.wait()
    for index, out in enumerate((own_ref, far_ref, near_ref)):
        out[...] = taps_ref[index].astype(jnp.bfloat16)


def columns_of(ref, rows, index):
    return ref[rows, index * 2 * HD : (index + 1) * 2 * HD]


def sort_heads(heads, *refs):
    count = heads // 2
    near_ref, far_ref = refs[count : count + 2]
    query_ref, side_ref = refs[-2:]
    rows = (refs[0].shape[0] - NOTE_ROWS) // 6
    _, pair, _ = place(heads)
    for step, ref in zip(STEPS, refs):
        source = pair ^ step
        query_ref[source, rows:, :HD] = ref[6 * rows :]
        for head in range(2):
            columns = slice(head * HD, (head + 1) * HD)
            first = head * 3 * rows
            query_ref[source, :rows, columns] = ref[first : first + rows]
            for part in range(2):
                line = first + (part + 1) * rows
                side_ref[2 * source + part, :, columns] = ref[line : line + rows]
    height, width = far_ref.shape
    parts = width // (2 * HD)
    for part in range(parts):
        line = slice(part * height, (part + 1) * height)
        side_ref[heads, line] = columns_of(far_ref, slice(None), part)
        side_ref[heads + 1, line] = columns_of(near_ref, slice(None), part)


UNIT = 2


def key_set(ref, blocks, head, origin, parity, causal):
    columns = slice(head * HD, (head + 1) * HD)
    rows = ref.shape[1]
    key = jnp.concatenate([ref[2 * block, :, columns] for block in range(blocks)], axis=0)
    value = jnp.concatenate([ref[2 * block + 1, :, columns] for block in range(blocks)], axis=0)
    return key, value, [(2 * block + parity) * rows + origin for block in range(blocks)], causal


def masked_scores(sets, query, start, own, begin):
    held = [[] for _ in range(UNIT)]
    for key, _, firsts, causal in sets:
        scores = lax.dot_general(
            key, query, (((1,), (1,)), ((), ())), preferred_element_type=jnp.float32
        )
        rows = key.shape[0] // len(firsts)
        line = lax.broadcasted_iota(jnp.int32, (rows, rows), 0)
        for block, first in enumerate(firsts):
            for index in range(UNIT):
                if causal and block > begin + index:
                    held[index].append(None)
                    continue
                lanes = slice(index * rows, (index + 1) * rows)
                allowed = line >= start[:, lanes] - first
                if causal and block == begin + index:
                    allowed &= line <= own[:, lanes] - first
                part = scores[block * rows : (block + 1) * rows, lanes]
                held[index].append(jnp.where(allowed, part, MASKED))
    return held


def highest(held):
    tops = [functools.reduce(jnp.maximum, [x for x in parts if x is not None]) for parts in held]
    return jnp.concatenate([jnp.max(top, axis=0, keepdims=True) for top in tops], axis=1)


def weigh(held, top):
    totals, rounded = [], []
    for index, parts in enumerate(held):
        rows = next(x for x in parts if x is not None).shape[1]
        here = top[:, index * rows : (index + 1) * rows]
        weights = [None if x is None else jnp.exp2((x - here) * FACTOR) for x in parts]
        total = functools.reduce(jnp.add, [x for x in weights if x is not None])
        totals.append(jnp.sum(total, axis=0, keepdims=True))
        rounded.append(
            [
                jnp.zeros((rows, rows), jnp.bfloat16) if x is None else x.astype(jnp.bfloat16)
                for x in weights
            ]
        )
    lines = [jnp.concatenate(line, axis=1) for line in zip(*rounded)]
    return jnp.concatenate(totals, axis=1), jnp.concatenate(lines, axis=0)


def mix(sets, rounded):
    return dot(jnp.concatenate([one[1] for one in sets], axis=0).T, rounded)


def unit_rows(heads, query_ref, begin):
    rows = query_ref.shape[1] - NOTE_ROWS
    group, _, parity = place(heads)
    starts = []
    for block in range(begin, begin + UNIT):
        note = query_ref[block, rows:, :HD].astype(jnp.float32)
        starts.append(note[0:1] * float(DIGIT) + note[1:2])
    start = jnp.concatenate(starts, axis=1).astype(jnp.int32) - group * (heads * rows)
    line = lax.broadcasted_iota(jnp.int32, (1, UNIT * rows), 1)
    own = line // rows * rows + line + (2 * begin + parity) * rows
    return start, own


def unit_queries(query_ref, head, begin):
    rows = query_ref.shape[1] - NOTE_ROWS
    blocks = range(begin, begin + UNIT)
    columns = slice(head * HD, (head + 1) * HD)
    return jnp.concatenate([query_ref[block, :rows, columns] for block in blocks], axis=0)


FACTOR = math.log2(math.e) / math.sqrt(HD)


def attend_first(heads, query_ref, key_value_ref, top_ref, total_ref, mixed_ref):
    _, _, parity = place(heads)
    for unit in range(heads // 2 // UNIT):
        begin = unit * UNIT
        start, own = unit_rows(heads, query_ref, begin)
        sets = [[key_set(key_value_ref, begin + UNIT, head, 0, parity, True)] for head in range(2)]
        held = [
            masked_scores(sets[head], unit_queries(query_ref, head, begin), start, own, begin)
            for head in range(2)
        ]
        tops = [highest(each) for each in held]
        weights = [weigh(each, top) for each, top in zip(held, tops)]
        for head, (total, rounded) in enumerate(weights):
            top_ref[head, unit] = tops[head]
            total_ref[head, unit] = total
            mixed_ref[head, unit] = mix(sets[head], rounded)


def attend_second(heads, mine, *refs):
    count = heads // 2
    query_ref, top_ref, total_ref, mixed_ref, other_ref, *more = refs[: -UNIT - 1]
    outs, held_ref = refs[-UNIT - 1 : -1], refs[-1]
    more = more[: len(more) // 2 * 2]
    rows = query_ref.shape[1] - NOTE_ROWS
    _, pair, parity = place(heads)
    here = pair // UNIT

    def one_unit(unit):
        begin = unit * UNIT
        start, own = unit_rows(heads, query_ref, begin)
        sets, held, tops = [], [], []
        for head in range(2):
            sets.append([key_set(other_ref, begin + UNIT, head, 0, 1 - parity, True)])
            for ref, side in zip(more, (parity, 1 - parity)):
                sets[head].append(key_set(ref, count, head, -heads * rows, side, False))
            query = unit_queries(query_ref, head, begin)
            held.append(masked_scores(sets[head], query, start, own, begin))
        for head in range(2):
            tops.append(jnp.maximum(top_ref[head, unit], highest(held[head])))
        weights = [weigh(each, top) for each, top in zip(held, tops)]
        notes = jnp.zeros((NOTE_ROWS, UNIT * rows), jnp.float32)
        for head, (total, rounded) in enumerate(weights):
            top = tops[head]
            scale = jnp.exp2((top_ref[head, unit] - top) * FACTOR)
            total = total_ref[head, unit] * scale + total
            mixed = mixed_ref[head, unit] * scale + mix(sets[head], rounded)
            mixed = (mixed * (1.0 / total)).astype(jnp.bfloat16).T
            logs = top * (1.0 / math.sqrt(HD)) + jnp.log(total)
            high = logs.astype(jnp.bfloat16).astype(jnp.float32)
            middle = (logs - high).astype(jnp.bfloat16).astype(jnp.float32)
            low = logs - high - middle
            line = lax.broadcasted_iota(jnp.int32, (NOTE_ROWS, UNIT * rows), 0) - 3 * head
            for index, part in enumerate((high, middle, low)):
                notes = jnp.where(line == index, part, notes)
            for index in range(UNIT):
                held_ref[index, head * rows : (head + 1) * rows] = mixed[
                    index * rows : (index + 1) * rows
                ]
        for index in range(UNIT):
            held_ref[index, 2 * rows :] = notes[:, index * rows : (index + 1) * rows].astype(
                jnp.bfloat16
            )

    for unit in range(count // UNIT):

        @pl.when((here == unit) if mine else (here != unit))
        def _():
            one_unit(unit)

    for step, out in enumerate(outs):
        out[...] = held_ref[lax.rem(pair, UNIT) ^ step]


def unpack_heads(heads, steps, *refs):
    *sources, out_ref, logs_ref = refs
    rows = out_ref.shape[0]
    _, pair, _ = place(heads)
    for step, source in zip(steps, sources):
        owner = pair ^ step
        note = source[2 * rows :].astype(jnp.float32)
        for head in range(2):
            columns = pl.ds(pl.multiple_of((owner * 2 + head) * HD, HD), HD)
            out_ref[:, columns] = source[head * rows : (head + 1) * rows]
            parts = [note[3 * head + index : 3 * head + index + 1] for index in range(3)]
            logs_ref[pl.ds(owner * 2 + head, 1), :] = parts[0] + parts[1] + parts[2]


def dot(left, right):
    return jnp.dot(left, right, preferred_element_type=jnp.float32)


def twice(array):
    return jnp.concatenate([array, array], axis=0)


def document_starts(starts_ref, rows):
    return jnp.maximum(starts_ref[...] - lax.axis_index("ctx") * rows, -rows)


def filtered(spectrum, filter_ref, back_ref):
    half = spectrum.shape[0] // 2
    even, odd = spectrum[:half], spectrum[half:]
    tap_even, tap_odd = filter_ref[:half], filter_ref[half:]
    real = (even * tap_even - odd * tap_odd).astype(jnp.bfloat16)
    imag = (even * tap_odd + odd * tap_even).astype(jnp.bfloat16)
    return dot(back_ref[...], jnp.concatenate([real, imag], axis=0))


def convolve(
    heads, other_ref, mine_ref, before_ref, own_taps_ref, starts_ref, product_ref, gate_ref, skip_ref,
    ahead_ref, wide_back_ref, out_ref, taps_ref, filter_ref, sum_ref, early_ref, late_ref, back_ref,
):
    rows = product_ref.shape[0]
    early_ref[...] = split(ahead_ref[:, :rows])
    late_ref[...] = split(ahead_ref[:, rows:])
    back_ref[...] = wide_back_ref[...].astype(jnp.bfloat16)
    height, width = own_taps_ref.shape
    panel = lax.axis_index("tp")
    even = lax.rem(lax.axis_index("ctx"), 2) == 0
    everything = slice(None)

    def store(step, part, value):
        line = pl.ds(pl.multiple_of((panel ^ step) * height, height), height)
        taps_ref[line, part * 2 * HD : (part + 1) * 2 * HD] = value

    parts = width // (2 * HD)
    for part in range(parts):
        line = slice(part * height, (part + 1) * height)
        mine_far, other_far = mine_ref[heads, line], other_ref[heads, line]
        store(0, part, columns_of(own_taps_ref, everything, part))
        store(1, part, jnp.where(even, mine_ref[heads + 1, line], other_ref[heads + 1, line]))
        store(2, part, jnp.where(even, mine_far, other_far))
        store(3, part, jnp.where(even, other_far, mine_far))
    filter_ref[...] = dot(early_ref[...], twice(taps_ref[...]))
    starts = document_starts(starts_ref, rows)
    line = lax.broadcasted_iota(jnp.int32, (rows, 1), 0)
    zero = jnp.zeros((), jnp.bfloat16)

    begin = jnp.min(starts)
    past = jnp.where(line - rows >= begin, before_ref[...], zero)
    here = jnp.where(line >= begin, product_ref[...], zero)
    spectrum = dot(early_ref[...], twice(past)) + dot(late_ref[...], twice(here))
    sum_ref[...] = filtered(spectrum, filter_ref, back_ref)

    def one_document(begin):
        here = jnp.where(line >= begin, product_ref[...], zero)
        result = filtered(dot(late_ref[...], twice(here)), filter_ref, back_ref)
        sum_ref[...] = jnp.where(line >= begin, result, sum_ref[...])
        return jnp.min(jnp.where(starts > begin, starts, rows))

    second = jnp.min(jnp.where(starts > begin, starts, rows))
    lax.while_loop(lambda begin: begin < rows, one_document, second)
    out_ref[...] = (
        gate_ref[0].astype(jnp.float32)
        * (skip_ref[...] * product_ref[...].astype(jnp.float32) + sum_ref[...])
    ).astype(jnp.bfloat16)


def twiddles(rows):
    window = 2 * rows
    order = np.arange(rows)[:, None] * 2 + 1
    angle = np.pi * ((order * np.arange(window)[None, :]) % (2 * window)) / window
    ahead = np.concatenate([np.cos(angle), -np.sin(angle)], axis=0)
    back = ahead.T[rows:] / rows
    return jnp.asarray(ahead, jnp.float32), jnp.asarray(back, jnp.float32)


def taps_pairs(peers, panels):
    assert panels == 4
    near, far = [], []
    for peer in range(peers):
        for panel in range(panels):
            here = peer * panels + panel
            far.append((here, peer * panels + (panel ^ (2 + peer % 2))))
            if peer % 2 == 0:
                near.append((here, peer * panels + (panel ^ 1)))
    return near, far


def local(hyena_inputs, filters, skip_bias, queries, keys_values, doc_start):
    rows = queries.shape[0]
    channels = hyena_inputs.shape[2]
    heads = queries.shape[1] // HD
    count = heads // 2
    peers = lax.axis_size("ctx")
    bf16, f32 = jnp.bfloat16, jnp.float32
    shape = jax.ShapeDtypeStruct
    starts = doc_start.reshape(1, rows)

    height = filters.shape[0]

    def pinned(*arrays):
        return [pltpu.with_memory_space_constraint(x, pltpu.HBM) for x in arrays]

    packed = call(
        functools.partial(pack_heads, heads),
        (shape((6 * rows + NOTE_ROWS, HD), bf16),) * count,
        pinned(queries, keys_values.reshape(2 * rows, heads * HD), starts),
        0,
        4 * queries.size * 3,
        scratch=(
            pltpu.VMEM((1, rows), jnp.int32),
            pltpu.SemaphoreType.DMA,
            pltpu.SemaphoreType.DMA((count, 4)),
        ),
        specs=[hbm()] * 3,
    )
    assert count == len(STEPS)
    arrived = [packed[0]] + [crossed(packed[i], "ctx", 2 * STEPS[i]) for i in range(1, count)]
    product, own_taps, far_taps, near_taps = call(
        pack_hyena,
        (shape((rows, channels), bf16),) + (shape((height, channels), bf16),) * 3,
        (hyena_inputs, *pinned(filters)),
        0,
        4 * queries.size * 3,
        scratch=(pltpu.VMEM((3, height, channels), f32), pltpu.SemaphoreType.DMA((3,))),
        specs=[vmem(), hbm()],
    )
    axes = ("ctx", "tp")
    near_pairs, far_pairs = taps_pairs(peers, lax.axis_size("tp"))
    near_taps = lax.ppermute(near_taps, axes, near_pairs)
    far_taps = lax.ppermute(far_taps, axes, far_pairs)
    before = lax.ppermute(product, "ctx", [(i, i + 1) for i in range(peers - 1)])
    query, key_value = call(
        functools.partial(sort_heads, heads),
        (
            shape((count, rows + NOTE_ROWS, 2 * HD), bf16),
            shape((heads + 2, rows, 2 * HD), bf16),
        ),
        (*arrived, near_taps, far_taps),
        0,
        4 * queries.size * 3,
    )
    other = crossed(key_value, "ctx", 1)
    units = count // UNIT
    partial = call(
        functools.partial(attend_first, heads),
        (
            shape((2, units, 1, UNIT * rows), f32),
            shape((2, units, 1, UNIT * rows), f32),
            shape((2, units, HD, UNIT * rows), f32),
        ),
        (query, key_value),
        LONG * (heads * rows) ** 2 * HD,
        4 * queries.size * 4,
    )
    operands = [query, *partial, other]
    if peers > heads:
        pairs = [(i, i + heads) for i in range(peers - heads)]
        operands += [lax.ppermute(each, "ctx", pairs) for each in (key_value, other)]
    assert count == 2 * UNIT
    message = shape((2 * rows + NOTE_ROWS, HD), bf16)

    def second(mine, *more):
        return call(
            functools.partial(attend_second, heads, mine),
            (message,) * UNIT,
            (*operands, *more),
            (heads * rows) ** 2 * HD,
            4 * queries.size * 4,
            scratch=(pltpu.VMEM((UNIT, 2 * rows + NOTE_ROWS, HD), bf16),),
        )

    theirs = second(False)
    own = second(True, theirs[0])
    returned = [own[0], crossed(theirs[0], "ctx", 4), crossed(theirs[1], "ctx", 6)]
    returned.append(crossed(own[1], "ctx", 2))
    hyena_out = call(
        functools.partial(convolve, heads),
        shape((rows, channels), bf16),
        (
            other, key_value, before, own_taps, starts, product, hyena_inputs,
            skip_bias.reshape(1, channels), *twiddles(rows),
        ),
        2 * 4 * 256 * 256 * channels,
        4 * queries.size * 4,
        scratch=(
            pltpu.VMEM((FLEN, channels), bf16),
            pltpu.VMEM((2 * rows, channels), f32),
            pltpu.VMEM((rows, channels), f32),
            pltpu.VMEM((2 * rows, 2 * rows), bf16),
            pltpu.VMEM((2 * rows, 2 * rows), bf16),
            pltpu.VMEM((rows, 2 * rows), bf16),
        ),
    )
    attention_out, log_totals = call(
        functools.partial(unpack_heads, heads, (0, 2, 3, 1)),
        (shape((rows, heads * HD), bf16), shape((heads, rows), f32)),
        returned,
        0,
        4 * queries.size,
    )
    return (hyena_out, attention_out, log_totals)


def solution(mesh):
    in_specs = (
        P(None, "ctx", "tp"),
        P("tp", None),
        P("tp"),
        P("ctx", "tp"),
        P(None, "ctx", "tp"),
        P("ctx"),
    )
    out_specs = (P("ctx", "tp"), P("ctx", "tp"), P("tp", "ctx"))
    return jax.shard_map(local, mesh=mesh, in_specs=in_specs, out_specs=out_specs, check_vma=False)
```

```python
import functools
import math

import jax
import jax.numpy as jnp
import numpy as np
from jax import lax
from jax.experimental import pallas as pl
from jax.experimental.pallas import tpu as pltpu
from jax.sharding import PartitionSpec as P

HD = 128
FLEN = 128
DIGIT = 256
NOTE_ROWS = 16
MASKED = -1e30
VMEM_LIMIT = 16 * 1024 * 1024
LONG = 200


def vmem():
    return pl.BlockSpec(memory_space=pltpu.VMEM)


def hbm():
    return pl.BlockSpec(memory_space=pltpu.HBM)


def call(kernel, out_shape, args, flops, nbytes, scratch=(), specs=None):
    return pl.pallas_call(
        kernel,
        out_shape=out_shape,
        in_specs=specs or [vmem() for _ in args],
        out_specs=jax.tree.map(lambda _: vmem(), out_shape),
        scratch_shapes=list(scratch),
        compiler_params=pltpu.CompilerParams(vmem_limit_bytes=VMEM_LIMIT),
        cost_estimate=pl.CostEstimate(flops=flops, bytes_accessed=nbytes, transcendentals=0),
    )(*args)


def crossed(array, axis, bits):
    return lax.ppermute(array, axis, [(i, i ^ bits) for i in range(lax.axis_size(axis))])


STEPS = (0, 2, 1, 3)


def place(heads):
    index = lax.axis_index("ctx")
    member = lax.rem(index, heads)
    return index // heads, member // 2, lax.rem(member, 2)


def pack_heads(heads, queries_ref, keys_values_ref, starts_ref, *refs):
    *outs, held_ref, start_sem, sem = refs
    rows = queries_ref.shape[0]
    _, pair, _ = place(heads)
    first = pltpu.make_async_copy(starts_ref, held_ref, start_sem)
    first.start()
    copies = []
    for step, out in zip(STEPS, outs):
        for head in range(2):
            columns = pl.ds(pl.multiple_of(((pair ^ step) * 2 + head) * HD, HD), HD)
            first_row = head * 3 * rows
            for part, source in enumerate((queries_ref, keys_values_ref)):
                lines = pl.ds(first_row + part * rows, source.shape[0])
                copies.append(
                    pltpu.make_async_copy(
                        source.at[:, columns], out.at[lines], sem.at[step, 2 * head + part]
                    )
                )
    for copy in copies:
        copy.start()
    first.wait()
    starts = held_ref[...]
    high = (starts // DIGIT).astype(jnp.float32)
    low = (starts % DIGIT).astype(jnp.float32)
    line = lax.broadcasted_iota(jnp.int32, (NOTE_ROWS, rows), 0)
    note = jnp.where(line == 0, high, jnp.where(line == 1, low, 0.0)).astype(jnp.bfloat16)
    for out in outs:
        out[6 * rows :] = note
    for copy in copies:
        copy.wait()


def split(matrix):
    high = matrix.astype(jnp.bfloat16)
    low = (matrix - high.astype(jnp.float32)).astype(jnp.bfloat16)
    return jnp.concatenate([high, low], axis=1)


def pack_hyena(hyena_ref, filters_ref, product_ref, own_ref, far_ref, near_ref, taps_ref, sem):
    width = own_ref.shape[1]
    panel = lax.axis_index("tp")
    parity = lax.rem(lax.axis_index("ctx"), 2)
    copies = []
    for index, target in enumerate((panel, panel ^ (3 - parity), panel ^ 1)):
        columns = pl.ds(pl.multiple_of(target * width, width), width)
        copies.append(
            pltpu.make_async_copy(filters_ref.at[:, columns], taps_ref.at[index], sem.at[index])
        )
    for copy in copies:
        copy.start()
    product_ref[...] = (hyena_ref[1].astype(jnp.float32) * hyena_ref[2].astype(jnp.float32)).astype(
        jnp.bfloat16
    )
    for copy in copies:
        copy.wait()
    for index, out in enumerate((own_ref, far_ref, near_ref)):
        out[...] = taps_ref[index].astype(jnp.bfloat16)


def columns_of(ref, rows, index):
    return ref[rows, index * 2 * HD : (index + 1) * 2 * HD]


def sort_heads(heads, *refs):
    count = heads // 2
    near_ref, far_ref = refs[count : count + 2]
    query_ref, side_ref = refs[-2:]
    rows = (refs[0].shape[0] - NOTE_ROWS) // 6
    _, pair, _ = place(heads)
    for step, ref in zip(STEPS, refs):
        source = pair ^ step
        query_ref[source, rows:, :HD] = ref[6 * rows :]
        for head in range(2):
            columns = slice(head * HD, (head + 1) * HD)
            first = head * 3 * rows
            query_ref[source, :rows, columns] = ref[first : first + rows]
            for part in range(2):
                line = first + (part + 1) * rows
                side_ref[2 * source + part, :, columns] = ref[line : line + rows]
    height, width = far_ref.shape
    parts = width // (2 * HD)
    for part in range(parts):
        line = slice(part * height, (part + 1) * height)
        side_ref[heads, line] = columns_of(far_ref, slice(None), part)
        side_ref[heads + 1, line] = columns_of(near_ref, slice(None), part)


UNIT = 2


def key_set(ref, blocks, head, origin, parity, causal):
    columns = slice(head * HD, (head + 1) * HD)
    rows = ref.shape[1]
    key = jnp.concatenate([ref[2 * block, :, columns] for block in range(blocks)], axis=0)
    value = jnp.concatenate([ref[2 * block + 1, :, columns] for block in range(blocks)], axis=0)
    return key, value, [(2 * block + parity) * rows + origin for block in range(blocks)], causal


def masked_scores(sets, query, start, own, begin):
    held = [[] for _ in range(UNIT)]
    for key, _, firsts, causal in sets:
        scores = lax.dot_general(
            key, query, (((1,), (1,)), ((), ())), preferred_element_type=jnp.float32
        )
        rows = key.shape[0] // len(firsts)
        line = lax.broadcasted_iota(jnp.int32, (rows, rows), 0)
        for block, first in enumerate(firsts):
            for index in range(UNIT):
                if causal and block > begin + index:
                    held[index].append(None)
                    continue
                lanes = slice(index * rows, (index + 1) * rows)
                allowed = line >= start[:, lanes] - first
                if causal and block == begin + index:
                    allowed &= line <= own[:, lanes] - first
                part = scores[block * rows : (block + 1) * rows, lanes]
                held[index].append(jnp.where(allowed, part, MASKED))
    return held


def highest(held):
    tops = [functools.reduce(jnp.maximum, [x for x in parts if x is not None]) for parts in held]
    return jnp.concatenate([jnp.max(top, axis=0, keepdims=True) for top in tops], axis=1)


def weigh(held, top):
    totals, rounded = [], []
    for index, parts in enumerate(held):
        rows = next(x for x in parts if x is not None).shape[1]
        here = top[:, index * rows : (index + 1) * rows]
        weights = [None if x is None else jnp.exp2((x - here) * FACTOR) for x in parts]
        total = functools.reduce(jnp.add, [x for x in weights if x is not None])
        totals.append(jnp.sum(total, axis=0, keepdims=True))
        rounded.append(
            [
                jnp.zeros((rows, rows), jnp.bfloat16) if x is None else x.astype(jnp.bfloat16)
                for x in weights
            ]
        )
    lines = [jnp.concatenate(line, axis=1) for line in zip(*rounded)]
    return jnp.concatenate(totals, axis=1), jnp.concatenate(lines, axis=0)


def mix(sets, rounded):
    return dot(jnp.concatenate([one[1] for one in sets], axis=0).T, rounded)


def unit_rows(heads, query_ref, begin):
    rows = query_ref.shape[1] - NOTE_ROWS
    group, _, parity = place(heads)
    starts = []
    for block in range(begin, begin + UNIT):
        note = query_ref[block, rows:, :HD].astype(jnp.float32)
        starts.append(note[0:1] * float(DIGIT) + note[1:2])
    start = jnp.concatenate(starts, axis=1).astype(jnp.int32) - group * (heads * rows)
    line = lax.broadcasted_iota(jnp.int32, (1, UNIT * rows), 1)
    own = line // rows * rows + line + (2 * begin + parity) * rows
    return start, own


def unit_queries(query_ref, head, begin):
    rows = query_ref.shape[1] - NOTE_ROWS
    blocks = range(begin, begin + UNIT)
    columns = slice(head * HD, (head + 1) * HD)
    return jnp.concatenate([query_ref[block, :rows, columns] for block in blocks], axis=0)


FACTOR = math.log2(math.e) / math.sqrt(HD)


def attend_first(heads, query_ref, key_value_ref, top_ref, total_ref, mixed_ref):
    _, _, parity = place(heads)
    for unit in range(heads // 2 // UNIT):
        begin = unit * UNIT
        start, own = unit_rows(heads, query_ref, begin)
        sets = [[key_set(key_value_ref, begin + UNIT, head, 0, parity, True)] for head in range(2)]
        held = [
            masked_scores(sets[head], unit_queries(query_ref, head, begin), start, own, begin)
            for head in range(2)
        ]
        tops = [highest(each) for each in held]
        weights = [weigh(each, top) for each, top in zip(held, tops)]
        for head, (total, rounded) in enumerate(weights):
            top_ref[head, unit] = tops[head]
            total_ref[head, unit] = total
            mixed_ref[head, unit] = mix(sets[head], rounded)


def attend_second(heads, mine, *refs):
    count = heads // 2
    query_ref, top_ref, total_ref, mixed_ref, other_ref, *more = refs[: -UNIT - 1]
    outs, held_ref = refs[-UNIT - 1 : -1], refs[-1]
    more = more[: len(more) // 2 * 2]
    rows = query_ref.shape[1] - NOTE_ROWS
    _, pair, parity = place(heads)
    here = pair // UNIT

    def one_unit(unit):
        begin = unit * UNIT
        start, own = unit_rows(heads, query_ref, begin)
        sets, held, tops = [], [], []
        for head in range(2):
            sets.append([key_set(other_ref, begin + UNIT, head, 0, 1 - parity, True)])
            for ref, side in zip(more, (parity, 1 - parity)):
                sets[head].append(key_set(ref, count, head, -heads * rows, side, False))
            query = unit_queries(query_ref, head, begin)
            held.append(masked_scores(sets[head], query, start, own, begin))
        for head in range(2):
            tops.append(jnp.maximum(top_ref[head, unit], highest(held[head])))
        weights = [weigh(each, top) for each, top in zip(held, tops)]
        notes = jnp.zeros((NOTE_ROWS, UNIT * rows), jnp.float32)
        for head, (total, rounded) in enumerate(weights):
            top = tops[head]
            scale = jnp.exp2((top_ref[head, unit] - top) * FACTOR)
            total = total_ref[head, unit] * scale + total
            mixed = mixed_ref[head, unit] * scale + mix(sets[head], rounded)
            mixed = (mixed * (1.0 / total)).astype(jnp.bfloat16).T
            logs = top * (1.0 / math.sqrt(HD)) + jnp.log(total)
            high = logs.astype(jnp.bfloat16).astype(jnp.float32)
            middle = (logs - high).astype(jnp.bfloat16).astype(jnp.float32)
            low = logs - high - middle
            line = lax.broadcasted_iota(jnp.int32, (NOTE_ROWS, UNIT * rows), 0) - 3 * head
            for index, part in enumerate((high, middle, low)):
                notes = jnp.where(line == index, part, notes)
            for index in range(UNIT):
                held_ref[index, head * rows : (head + 1) * rows] = mixed[
                    index * rows : (index + 1) * rows
                ]
        for index in range(UNIT):
            held_ref[index, 2 * rows :] = notes[:, index * rows : (index + 1) * rows].astype(
                jnp.bfloat16
            )

    for unit in range(count // UNIT):

        @pl.when((here == unit) if mine else (here != unit))
        def _():
            one_unit(unit)

    for step, out in enumerate(outs):
        out[...] = held_ref[lax.rem(pair, UNIT) ^ step]


def unpack_heads(heads, steps, *refs):
    *sources, out_ref, logs_ref = refs
    rows = out_ref.shape[0]
    _, pair, _ = place(heads)
    for step, source in zip(steps, sources):
        owner = pair ^ step
        note = source[2 * rows :].astype(jnp.float32)
        for head in range(2):
            columns = pl.ds(pl.multiple_of((owner * 2 + head) * HD, HD), HD)
            out_ref[:, columns] = source[head * rows : (head + 1) * rows]
            parts = [note[3 * head + index : 3 * head + index + 1] for index in range(3)]
            logs_ref[pl.ds(owner * 2 + head, 1), :] = parts[0] + parts[1] + parts[2]


def dot(left, right):
    return jnp.dot(left, right, preferred_element_type=jnp.float32)


def twice(array):
    return jnp.concatenate([array, array], axis=0)


def document_starts(starts_ref, rows):
    return jnp.maximum(starts_ref[...] - lax.axis_index("ctx") * rows, -rows)


def filtered(spectrum, filter_ref, back_ref):
    half = spectrum.shape[0] // 2
    even, odd = spectrum[:half], spectrum[half:]
    tap_even, tap_odd = filter_ref[:half], filter_ref[half:]
    real = (even * tap_even - odd * tap_odd).astype(jnp.bfloat16)
    imag = (even * tap_odd + odd * tap_even).astype(jnp.bfloat16)
    return dot(back_ref[...], jnp.concatenate([real, imag], axis=0))


def convolve(
    heads, other_ref, mine_ref, before_ref, own_taps_ref, starts_ref, product_ref, gate_ref, skip_ref,
    ahead_ref, wide_back_ref, out_ref, taps_ref, filter_ref, sum_ref, early_ref, late_ref, back_ref,
):
    rows = product_ref.shape[0]
    early_ref[...] = split(ahead_ref[:, :rows])
    late_ref[...] = split(ahead_ref[:, rows:])
    back_ref[...] = wide_back_ref[...].astype(jnp.bfloat16)
    height, width = own_taps_ref.shape
    panel = lax.axis_index("tp")
    even = lax.rem(lax.axis_index("ctx"), 2) == 0
    everything = slice(None)

    def store(step, part, value):
        line = pl.ds(pl.multiple_of((panel ^ step) * height, height), height)
        taps_ref[line, part * 2 * HD : (part + 1) * 2 * HD] = value

    parts = width // (2 * HD)
    for part in range(parts):
        line = slice(part * height, (part + 1) * height)
        mine_far, other_far = mine_ref[heads, line], other_ref[heads, line]
        store(0, part, columns_of(own_taps_ref, everything, part))
        store(1, part, jnp.where(even, other_ref[heads + 1, line], mine_ref[heads + 1, line]))
        store(2, part, jnp.where(even, other_far, mine_far))
        store(3, part, jnp.where(even, mine_far, other_far))
    filter_ref[...] = dot(early_ref[...], twice(taps_ref[...]))
    starts = document_starts(starts_ref, rows)
    line = lax.broadcasted_iota(jnp.int32, (rows, 1), 0)
    zero = jnp.zeros((), jnp.bfloat16)

    begin = jnp.min(starts)
    past = jnp.where(line - rows >= begin, before_ref[...], zero)
    here = jnp.where(line >= begin, product_ref[...], zero)
    spectrum = dot(early_ref[...], twice(past)) + dot(late_ref[...], twice(here))
    sum_ref[...] = filtered(spectrum, filter_ref, back_ref)

    def one_document(begin):
        here = jnp.where(line >= begin, product_ref[...], zero)
        result = filtered(dot(late_ref[...], twice(here)), filter_ref, back_ref)
        sum_ref[...] = jnp.where(line >= begin, result, sum_ref[...])
        return jnp.min(jnp.where(starts > begin, starts, rows))

    second = jnp.min(jnp.where(starts > begin, starts, rows))
    lax.while_loop(lambda begin: begin < rows, one_document, second)
    out_ref[...] = (
        gate_ref[0].astype(jnp.float32)
        * (skip_ref[...] * product_ref[...].astype(jnp.float32) + sum_ref[...])
    ).astype(jnp.bfloat16)


def twiddles(rows):
    window = 2 * rows
    order = np.arange(rows)[:, None] * 2 + 1
    angle = np.pi * ((order * np.arange(window)[None, :]) % (2 * window)) / window
    ahead = np.concatenate([np.cos(angle), -np.sin(angle)], axis=0)
    back = ahead.T[rows:] / rows
    return jnp.asarray(ahead, jnp.float32), jnp.asarray(back, jnp.float32)


def taps_pairs(peers, panels):
    assert panels == 4
    near, far = [], []
    for peer in range(peers):
        for panel in range(panels):
            here = peer * panels + panel
            far.append((here, peer * panels + (panel ^ (3 - peer % 2))))
            if peer % 2 == 1:
                near.append((here, peer * panels + (panel ^ 1)))
    return near, far


def local(hyena_inputs, filters, skip_bias, queries, keys_values, doc_start):
    rows = queries.shape[0]
    channels = hyena_inputs.shape[2]
    heads = queries.shape[1] // HD
    count = heads // 2
    peers = lax.axis_size("ctx")
    bf16, f32 = jnp.bfloat16, jnp.float32
    shape = jax.ShapeDtypeStruct
    starts = doc_start.reshape(1, rows)

    height = filters.shape[0]

    def pinned(*arrays):
        return [pltpu.with_memory_space_constraint(x, pltpu.HBM) for x in arrays]

    *packed, near_starts = call(
        functools.partial(pack_heads, heads),
        (shape((6 * rows + NOTE_ROWS, HD), bf16),) * count + (shape((1, rows), jnp.int32),),
        pinned(queries, keys_values.reshape(2 * rows, heads * HD), starts),
        0,
        4 * queries.size * 3,
        scratch=(pltpu.SemaphoreType.DMA, pltpu.SemaphoreType.DMA((count, 4))),
        specs=[hbm()] * 3,
    )
    assert count == len(STEPS)
    arrived = [packed[0]] + [crossed(packed[i], "ctx", 2 * STEPS[i]) for i in range(1, count)]
    product, own_taps, far_taps, near_taps = call(
        pack_hyena,
        (shape((rows, channels), bf16),) + (shape((height, channels), bf16),) * 3,
        (hyena_inputs, *pinned(filters)),
        0,
        4 * queries.size * 3,
        scratch=(pltpu.VMEM((3, height, channels), f32), pltpu.SemaphoreType.DMA((3,))),
        specs=[vmem(), hbm()],
    )
    axes = ("ctx", "tp")
    near_pairs, far_pairs = taps_pairs(peers, lax.axis_size("tp"))
    near_taps = lax.ppermute(near_taps, axes, near_pairs)
    far_taps = lax.ppermute(far_taps, axes, far_pairs)
    before = lax.ppermute(product, "ctx", [(i, i + 1) for i in range(peers - 1)])
    query, key_value = call(
        functools.partial(sort_heads, heads),
        (
            shape((count, rows + NOTE_ROWS, 2 * HD), bf16),
            shape((heads + 2, rows, 2 * HD), bf16),
        ),
        (*arrived, near_taps, far_taps),
        0,
        4 * queries.size * 3,
    )
    other = crossed(key_value, "ctx", 1)
    units = count // UNIT
    partial = call(
        functools.partial(attend_first, heads),
        (
            shape((2, units, 1, UNIT * rows), f32),
            shape((2, units, 1, UNIT * rows), f32),
            shape((2, units, HD, UNIT * rows), f32),
        ),
        (query, key_value),
        LONG * (heads * rows) ** 2 * HD,
        4 * queries.size * 4,
    )
    operands = [query, *partial, other]
    if peers > heads:
        pairs = [(i, i + heads) for i in range(peers - heads)]
        operands += [lax.ppermute(each, "ctx", pairs) for each in (key_value, other)]
    assert count == 2 * UNIT
    message = shape((2 * rows + NOTE_ROWS, HD), bf16)

    def second(mine, *more):
        return call(
            functools.partial(attend_second, heads, mine),
            (message,) * UNIT,
            (*operands, *more),
            (heads * rows) ** 2 * HD,
            4 * queries.size * 4,
            scratch=(pltpu.VMEM((UNIT, 2 * rows + NOTE_ROWS, HD), bf16),),
        )

    theirs = second(False)
    own = second(True, theirs[0])
    returned = [own[0], crossed(theirs[0], "ctx", 4), crossed(theirs[1], "ctx", 6)]
    returned.append(crossed(own[1], "ctx", 2))
    hyena_out = call(
        functools.partial(convolve, heads),
        shape((rows, channels), bf16),
        (
            other, key_value, before, own_taps, near_starts, product, hyena_inputs,
            skip_bias.reshape(1, channels), *twiddles(rows),
        ),
        2 * 4 * 256 * 256 * channels,
        4 * queries.size * 4,
        scratch=(
            pltpu.VMEM((FLEN, channels), bf16),
            pltpu.VMEM((2 * rows, channels), f32),
            pltpu.VMEM((rows, channels), f32),
            pltpu.VMEM((2 * rows, 2 * rows), bf16),
            pltpu.VMEM((2 * rows, 2 * rows), bf16),
            pltpu.VMEM((rows, 2 * rows), bf16),
        ),
    )
    attention_out, log_totals = call(
        functools.partial(unpack_heads, heads, (0, 2, 3, 1)),
        (shape((rows, heads * HD), bf16), shape((heads, rows), f32)),
        returned,
        0,
        4 * queries.size,
    )
    return (hyena_out, attention_out, log_totals)


def solution(mesh):
    in_specs = (
        P(None, "ctx", "tp"),
        P("tp", None),
        P("tp"),
        P("ctx", "tp"),
        P(None, "ctx", "tp"),
        P("ctx"),
    )
    out_specs = (P("ctx", "tp"), P("ctx", "tp"), P("tp", "ctx"))
    return jax.shard_map(local, mesh=mesh, in_specs=in_specs, out_specs=out_specs, check_vma=False)
```

```python
import functools
import math

import jax
import jax.numpy as jnp
import numpy as np
from jax import lax
from jax.experimental import pallas as pl
from jax.experimental.pallas import tpu as pltpu
from jax.sharding import PartitionSpec as P

HD = 128
FLEN = 128
DIGIT = 256
NOTE_ROWS = 16
MASKED = -1e30
VMEM_LIMIT = 16 * 1024 * 1024
LONG = 200


def vmem():
    return pl.BlockSpec(memory_space=pltpu.VMEM)


def hbm():
    return pl.BlockSpec(memory_space=pltpu.HBM)


def call(kernel, out_shape, args, flops, nbytes, scratch=(), specs=None):
    return pl.pallas_call(
        kernel,
        out_shape=out_shape,
        in_specs=specs or [vmem() for _ in args],
        out_specs=jax.tree.map(lambda _: vmem(), out_shape),
        scratch_shapes=list(scratch),
        compiler_params=pltpu.CompilerParams(vmem_limit_bytes=VMEM_LIMIT),
        cost_estimate=pl.CostEstimate(flops=flops, bytes_accessed=nbytes, transcendentals=0),
    )(*args)


def crossed(array, axis, bits):
    return lax.ppermute(array, axis, [(i, i ^ bits) for i in range(lax.axis_size(axis))])


STEPS = (0, 2, 1, 3)


def place(heads):
    index = lax.axis_index("ctx")
    member = lax.rem(index, heads)
    return index // heads, member // 2, lax.rem(member, 2)


def pack_heads(heads, queries_ref, keys_values_ref, starts_ref, *refs):
    *outs, held_ref, start_sem, sem = refs
    rows = queries_ref.shape[0]
    _, pair, _ = place(heads)
    first = pltpu.make_async_copy(starts_ref, held_ref, start_sem)
    first.start()
    copies = []
    for step, out in zip(STEPS, outs):
        for head in range(2):
            columns = pl.ds(pl.multiple_of(((pair ^ step) * 2 + head) * HD, HD), HD)
            first_row = head * 3 * rows
            for part, source in enumerate((queries_ref, keys_values_ref)):
                lines = pl.ds(first_row + part * rows, source.shape[0])
                copies.append(
                    pltpu.make_async_copy(
                        source.at[:, columns], out.at[lines], sem.at[step, 2 * head + part]
                    )
                )
    for copy in copies:
        copy.start()
    first.wait()
    starts = held_ref[...]
    high = (starts // DIGIT).astype(jnp.float32)
    low = (starts % DIGIT).astype(jnp.float32)
    line = lax.broadcasted_iota(jnp.int32, (NOTE_ROWS, rows), 0)
    note = jnp.where(line == 0, high, jnp.where(line == 1, low, 0.0)).astype(jnp.bfloat16)
    for out in outs:
        out[6 * rows :] = note
    for copy in copies:
        copy.wait()


def split(matrix):
    high = matrix.astype(jnp.bfloat16)
    low = (matrix - high.astype(jnp.float32)).astype(jnp.bfloat16)
    return jnp.concatenate([high, low], axis=1)


def pack_hyena(hyena_ref, filters_ref, product_ref, own_ref, far_ref, near_ref, taps_ref, sem):
    width = own_ref.shape[1]
    panel = lax.axis_index("tp")
    parity = lax.rem(lax.axis_index("ctx"), 2)
    copies = []
    for index, target in enumerate((panel, panel ^ (3 - parity), panel ^ 1)):
        columns = pl.ds(pl.multiple_of(target * width, width), width)
        copies.append(
            pltpu.make_async_copy(filters_ref.at[:, columns], taps_ref.at[index], sem.at[index])
        )
    for copy in copies:
        copy.start()
    product_ref[...] = (hyena_ref[1].astype(jnp.float32) * hyena_ref[2].astype(jnp.float32)).astype(
        jnp.bfloat16
    )
    for copy in copies:
        copy.wait()
    for index, out in enumerate((own_ref, far_ref, near_ref)):
        out[...] = taps_ref[index].astype(jnp.bfloat16)


def columns_of(ref, rows, index):
    return ref[rows, index * 2 * HD : (index + 1) * 2 * HD]


def sort_heads(heads, *refs):
    count = heads // 2
    near_ref, far_ref = refs[count : count + 2]
    query_ref, side_ref = refs[-2:]
    rows = (refs[0].shape[0] - NOTE_ROWS) // 6
    _, pair, _ = place(heads)
    for step, ref in zip(STEPS, refs):
        source = pair ^ step
        query_ref[source, rows:, :HD] = ref[6 * rows :]
        for head in range(2):
            columns = slice(head * HD, (head + 1) * HD)
            first = head * 3 * rows
            query_ref[source, :rows, columns] = ref[first : first + rows]
            for part in range(2):
                line = first + (part + 1) * rows
                side_ref[2 * source + part, :, columns] = ref[line : line + rows]
    height, width = far_ref.shape
    parts = width // (2 * HD)
    for part in range(parts):
        line = slice(part * height, (part + 1) * height)
        side_ref[heads, line] = columns_of(far_ref, slice(None), part)
        side_ref[heads + 1, line] = columns_of(near_ref, slice(None), part)


UNIT = 2


def key_set(ref, blocks, head, origin, parity, causal):
    columns = slice(head * HD, (head + 1) * HD)
    rows = ref.shape[1]
    key = jnp.concatenate([ref[2 * block, :, columns] for block in range(blocks)], axis=0)
    value = jnp.concatenate([ref[2 * block + 1, :, columns] for block in range(blocks)], axis=0)
    return key, value, [(2 * block + parity) * rows + origin for block in range(blocks)], causal


def masked_scores(sets, query, start, own, begin):
    held = [[] for _ in range(UNIT)]
    for key, _, firsts, causal in sets:
        scores = lax.dot_general(
            key, query, (((1,), (1,)), ((), ())), preferred_element_type=jnp.float32
        )
        rows = key.shape[0] // len(firsts)
        line = lax.broadcasted_iota(jnp.int32, (rows, rows), 0)
        for block, first in enumerate(firsts):
            for index in range(UNIT):
                if causal and block > begin + index:
                    held[index].append(None)
                    continue
                lanes = slice(index * rows, (index + 1) * rows)
                allowed = line >= start[:, lanes] - first
                if causal and block == begin + index:
                    allowed &= line <= own[:, lanes] - first
                part = scores[block * rows : (block + 1) * rows, lanes]
                held[index].append(jnp.where(allowed, part, MASKED))
    return held


def highest(held):
    tops = [functools.reduce(jnp.maximum, [x for x in parts if x is not None]) for parts in held]
    return jnp.concatenate([jnp.max(top, axis=0, keepdims=True) for top in tops], axis=1)


def weigh(held, top):
    totals, rounded = [], []
    for index, parts in enumerate(held):
        rows = next(x for x in parts if x is not None).shape[1]
        here = top[:, index * rows : (index + 1) * rows]
        weights = [None if x is None else jnp.exp2((x - here) * FACTOR) for x in parts]
        total = functools.reduce(jnp.add, [x for x in weights if x is not None])
        totals.append(jnp.sum(total, axis=0, keepdims=True))
        rounded.append(
            [
                jnp.zeros((rows, rows), jnp.bfloat16) if x is None else x.astype(jnp.bfloat16)
                for x in weights
            ]
        )
    lines = [jnp.concatenate(line, axis=1) for line in zip(*rounded)]
    return jnp.concatenate(totals, axis=1), jnp.concatenate(lines, axis=0)


def mix(sets, rounded):
    return dot(jnp.concatenate([one[1] for one in sets], axis=0).T, rounded)


def unit_rows(heads, query_ref, begin):
    rows = query_ref.shape[1] - NOTE_ROWS
    group, _, parity = place(heads)
    starts = []
    for block in range(begin, begin + UNIT):
        note = query_ref[block, rows:, :HD].astype(jnp.float32)
        starts.append(note[0:1] * float(DIGIT) + note[1:2])
    start = jnp.concatenate(starts, axis=1).astype(jnp.int32) - group * (heads * rows)
    line = lax.broadcasted_iota(jnp.int32, (1, UNIT * rows), 1)
    own = line // rows * rows + line + (2 * begin + parity) * rows
    return start, own


def unit_queries(query_ref, head, begin):
    rows = query_ref.shape[1] - NOTE_ROWS
    blocks = range(begin, begin + UNIT)
    columns = slice(head * HD, (head + 1) * HD)
    return jnp.concatenate([query_ref[block, :rows, columns] for block in blocks], axis=0)


FACTOR = math.log2(math.e) / math.sqrt(HD)


def attend_first(heads, query_ref, key_value_ref, top_ref, total_ref, mixed_ref):
    _, _, parity = place(heads)
    for unit in range(heads // 2 // UNIT):
        begin = unit * UNIT
        start, own = unit_rows(heads, query_ref, begin)
        sets = [[key_set(key_value_ref, begin + UNIT, head, 0, parity, True)] for head in range(2)]
        held = [
            masked_scores(sets[head], unit_queries(query_ref, head, begin), start, own, begin)
            for head in range(2)
        ]
        tops = [highest(each) for each in held]
        weights = [weigh(each, top) for each, top in zip(held, tops)]
        for head, (total, rounded) in enumerate(weights):
            top_ref[head, unit] = tops[head]
            total_ref[head, unit] = total
            mixed_ref[head, unit] = mix(sets[head], rounded)


def attend_second(heads, *refs):
    count = heads // 2
    query_ref, top_ref, total_ref, mixed_ref, other_ref, *more = refs[: -count - 1]
    outs, held_ref = refs[-count - 1 : -1], refs[-1]
    rows = query_ref.shape[1] - NOTE_ROWS
    _, pair, parity = place(heads)

    def one_unit(unit):
        begin = unit * UNIT
        start, own = unit_rows(heads, query_ref, begin)
        sets, held, tops = [], [], []
        for head in range(2):
            sets.append([key_set(other_ref, begin + UNIT, head, 0, 1 - parity, True)])
            for ref, side in zip(more, (parity, 1 - parity)):
                sets[head].append(key_set(ref, count, head, -heads * rows, side, False))
            query = unit_queries(query_ref, head, begin)
            held.append(masked_scores(sets[head], query, start, own, begin))
        for head in range(2):
            tops.append(jnp.maximum(top_ref[head, unit], highest(held[head])))
        weights = [weigh(each, top) for each, top in zip(held, tops)]
        notes = jnp.zeros((NOTE_ROWS, UNIT * rows), jnp.float32)
        for head, (total, rounded) in enumerate(weights):
            top = tops[head]
            scale = jnp.exp2((top_ref[head, unit] - top) * FACTOR)
            total = total_ref[head, unit] * scale + total
            mixed = mixed_ref[head, unit] * scale + mix(sets[head], rounded)
            mixed = (mixed * (1.0 / total)).astype(jnp.bfloat16).T
            logs = top * (1.0 / math.sqrt(HD)) + jnp.log(total)
            high = logs.astype(jnp.bfloat16).astype(jnp.float32)
            middle = (logs - high).astype(jnp.bfloat16).astype(jnp.float32)
            low = logs - high - middle
            line = lax.broadcasted_iota(jnp.int32, (NOTE_ROWS, UNIT * rows), 0) - 3 * head
            for index, part in enumerate((high, middle, low)):
                notes = jnp.where(line == index, part, notes)
            for index in range(UNIT):
                held_ref[begin + index, head * rows : (head + 1) * rows] = mixed[
                    index * rows : (index + 1) * rows
                ]
        for index in range(UNIT):
            held_ref[begin + index, 2 * rows :] = notes[:, index * rows : (index + 1) * rows].astype(
                jnp.bfloat16
            )

    for unit in range(count // UNIT):
        one_unit(unit)
    for step, out in enumerate(outs):
        out[...] = held_ref[pair ^ step]


def unpack_heads(heads, steps, *refs):
    *sources, out_ref, logs_ref = refs
    rows = out_ref.shape[0]
    _, pair, _ = place(heads)
    for step, source in zip(steps, sources):
        owner = pair ^ step
        note = source[2 * rows :].astype(jnp.float32)
        for head in range(2):
            columns = pl.ds(pl.multiple_of((owner * 2 + head) * HD, HD), HD)
            out_ref[:, columns] = source[head * rows : (head + 1) * rows]
            parts = [note[3 * head + index : 3 * head + index + 1] for index in range(3)]
            logs_ref[pl.ds(owner * 2 + head, 1), :] = parts[0] + parts[1] + parts[2]


def dot(left, right):
    return jnp.dot(left, right, preferred_element_type=jnp.float32)


def twice(array):
    return jnp.concatenate([array, array], axis=0)


def document_starts(starts_ref, rows):
    return jnp.maximum(starts_ref[...] - lax.axis_index("ctx") * rows, -rows)


def filtered(spectrum, filter_ref, back_ref):
    half = spectrum.shape[0] // 2
    even, odd = spectrum[:half], spectrum[half:]
    tap_even, tap_odd = filter_ref[:half], filter_ref[half:]
    real = (even * tap_even - odd * tap_odd).astype(jnp.bfloat16)
    imag = (even * tap_odd + odd * tap_even).astype(jnp.bfloat16)
    return dot(back_ref[...], jnp.concatenate([real, imag], axis=0))


def convolve(
    heads, other_ref, mine_ref, before_ref, own_taps_ref, starts_ref, product_ref, gate_ref, skip_ref,
    ahead_ref, wide_back_ref, out_ref, taps_ref, filter_ref, sum_ref, early_ref, late_ref, back_ref,
):
    rows = product_ref.shape[0]
    early_ref[...] = split(ahead_ref[:, :rows])
    late_ref[...] = split(ahead_ref[:, rows:])
    back_ref[...] = wide_back_ref[...].astype(jnp.bfloat16)
    height, width = own_taps_ref.shape
    panel = lax.axis_index("tp")
    even = lax.rem(lax.axis_index("ctx"), 2) == 0
    everything = slice(None)

    def store(step, part, value):
        line = pl.ds(pl.multiple_of((panel ^ step) * height, height), height)
        taps_ref[line, part * 2 * HD : (part + 1) * 2 * HD] = value

    parts = width // (2 * HD)
    for part in range(parts):
        line = slice(part * height, (part + 1) * height)
        mine_far, other_far = mine_ref[heads, line], other_ref[heads, line]
        store(0, part, columns_of(own_taps_ref, everything, part))
        store(1, part, jnp.where(even, other_ref[heads + 1, line], mine_ref[heads + 1, line]))
        store(2, part, jnp.where(even, other_far, mine_far))
        store(3, part, jnp.where(even, mine_far, other_far))
    filter_ref[...] = dot(early_ref[...], twice(taps_ref[...]))
    starts = document_starts(starts_ref, rows)
    line = lax.broadcasted_iota(jnp.int32, (rows, 1), 0)
    zero = jnp.zeros((), jnp.bfloat16)

    begin = jnp.min(starts)
    past = jnp.where(line - rows >= begin, before_ref[...], zero)
    here = jnp.where(line >= begin, product_ref[...], zero)
    spectrum = dot(early_ref[...], twice(past)) + dot(late_ref[...], twice(here))
    sum_ref[...] = filtered(spectrum, filter_ref, back_ref)

    def one_document(begin):
        here = jnp.where(line >= begin, product_ref[...], zero)
        result = filtered(dot(late_ref[...], twice(here)), filter_ref, back_ref)
        sum_ref[...] = jnp.where(line >= begin, result, sum_ref[...])
        return jnp.min(jnp.where(starts > begin, starts, rows))

    second = jnp.min(jnp.where(starts > begin, starts, rows))
    lax.while_loop(lambda begin: begin < rows, one_document, second)
    out_ref[...] = (
        gate_ref[0].astype(jnp.float32)
        * (skip_ref[...] * product_ref[...].astype(jnp.float32) + sum_ref[...])
    ).astype(jnp.bfloat16)


def twiddles(rows):
    window = 2 * rows
    order = np.arange(rows)[:, None] * 2 + 1
    angle = np.pi * ((order * np.arange(window)[None, :]) % (2 * window)) / window
    ahead = np.concatenate([np.cos(angle), -np.sin(angle)], axis=0)
    back = ahead.T[rows:] / rows
    return jnp.asarray(ahead, jnp.float32), jnp.asarray(back, jnp.float32)


def taps_pairs(peers, panels):
    assert panels == 4
    near, far = [], []
    for peer in range(peers):
        for panel in range(panels):
            here = peer * panels + panel
            far.append((here, peer * panels + (panel ^ (3 - peer % 2))))
            if peer % 2 == 1:
                near.append((here, peer * panels + (panel ^ 1)))
    return near, far


def local(hyena_inputs, filters, skip_bias, queries, keys_values, doc_start):
    rows = queries.shape[0]
    channels = hyena_inputs.shape[2]
    heads = queries.shape[1] // HD
    count = heads // 2
    peers = lax.axis_size("ctx")
    bf16, f32 = jnp.bfloat16, jnp.float32
    shape = jax.ShapeDtypeStruct
    starts = doc_start.reshape(1, rows)

    height = filters.shape[0]

    def pinned(*arrays):
        return [pltpu.with_memory_space_constraint(x, pltpu.HBM) for x in arrays]

    *packed, near_starts = call(
        functools.partial(pack_heads, heads),
        (shape((6 * rows + NOTE_ROWS, HD), bf16),) * count + (shape((1, rows), jnp.int32),),
        pinned(queries, keys_values.reshape(2 * rows, heads * HD), starts),
        0,
        4 * queries.size * 3,
        scratch=(pltpu.SemaphoreType.DMA, pltpu.SemaphoreType.DMA((count, 4))),
        specs=[hbm()] * 3,
    )
    assert count == len(STEPS)
    arrived = [packed[0]] + [crossed(packed[i], "ctx", 2 * STEPS[i]) for i in range(1, count)]
    product, own_taps, far_taps, near_taps = call(
        pack_hyena,
        (shape((rows, channels), bf16),) + (shape((height, channels), bf16),) * 3,
        (hyena_inputs, *pinned(filters)),
        0,
        4 * queries.size * 3,
        scratch=(pltpu.VMEM((3, height, channels), f32), pltpu.SemaphoreType.DMA((3,))),
        specs=[vmem(), hbm()],
    )
    axes = ("ctx", "tp")
    near_pairs, far_pairs = taps_pairs(peers, lax.axis_size("tp"))
    near_taps = lax.ppermute(near_taps, axes, near_pairs)
    far_taps = lax.ppermute(far_taps, axes, far_pairs)
    before = lax.ppermute(product, "ctx", [(i, i + 1) for i in range(peers - 1)])
    query, key_value = call(
        functools.partial(sort_heads, heads),
        (
            shape((count, rows + NOTE_ROWS, 2 * HD), bf16),
            shape((heads + 2, rows, 2 * HD), bf16),
        ),
        (*arrived, near_taps, far_taps),
        0,
        4 * queries.size * 3,
    )
    other = crossed(key_value, "ctx", 1)
    units = count // UNIT
    partial = call(
        functools.partial(attend_first, heads),
        (
            shape((2, units, 1, UNIT * rows), f32),
            shape((2, units, 1, UNIT * rows), f32),
            shape((2, units, HD, UNIT * rows), f32),
        ),
        (query, key_value),
        LONG * (heads * rows) ** 2 * HD,
        4 * queries.size * 4,
    )
    operands = [query, *partial, other]
    if peers > heads:
        pairs = [(i, i + heads) for i in range(peers - heads)]
        operands += [lax.ppermute(each, "ctx", pairs) for each in (key_value, other)]
    assert count == 2 * UNIT
    message = shape((2 * rows + NOTE_ROWS, HD), bf16)

    mixed = call(
        functools.partial(attend_second, heads),
        (message,) * count,
        operands,
        2 * (heads * rows) ** 2 * HD,
        4 * queries.size * 4,
        scratch=(pltpu.VMEM((count, 2 * rows + NOTE_ROWS, HD), bf16),),
    )
    returned = [mixed[0]] + [crossed(mixed[step], "ctx", 2 * step) for step in (3, 2, 1)]
    hyena_out = call(
        functools.partial(convolve, heads),
        shape((rows, channels), bf16),
        (
            other, key_value, before, own_taps, near_starts, product, hyena_inputs,
            skip_bias.reshape(1, channels), *twiddles(rows),
        ),
        2 * 4 * 256 * 256 * channels,
        4 * queries.size * 4,
        scratch=(
            pltpu.VMEM((FLEN, channels), bf16),
            pltpu.VMEM((2 * rows, channels), f32),
            pltpu.VMEM((rows, channels), f32),
            pltpu.VMEM((2 * rows, 2 * rows), bf16),
            pltpu.VMEM((2 * rows, 2 * rows), bf16),
            pltpu.VMEM((rows, 2 * rows), bf16),
        ),
    )
    attention_out, log_totals = call(
        functools.partial(unpack_heads, heads, (0, 3, 2, 1)),
        (shape((rows, heads * HD), bf16), shape((heads, rows), f32)),
        returned,
        0,
        4 * queries.size,
    )
    return (hyena_out, attention_out, log_totals)


def solution(mesh):
    in_specs = (
        P(None, "ctx", "tp"),
        P("tp", None),
        P("tp"),
        P("ctx", "tp"),
        P(None, "ctx", "tp"),
        P("ctx"),
    )
    out_specs = (P("ctx", "tp"), P("ctx", "tp"), P("tp", "ctx"))
    return jax.shard_map(local, mesh=mesh, in_specs=in_specs, out_specs=out_specs, check_vma=False)
```

```python
import functools
import math

import jax
import jax.numpy as jnp
import numpy as np
from jax import lax
from jax.experimental import pallas as pl
from jax.experimental.pallas import tpu as pltpu
from jax.sharding import PartitionSpec as P

HD = 128
FLEN = 128
DIGIT = 256
NOTE_ROWS = 16
MASKED = -1e30
VMEM_LIMIT = 16 * 1024 * 1024
LONG = 200


def vmem():
    return pl.BlockSpec(memory_space=pltpu.VMEM)


def hbm():
    return pl.BlockSpec(memory_space=pltpu.HBM)


def call(kernel, out_shape, args, flops, nbytes, scratch=(), specs=None):
    return pl.pallas_call(
        kernel,
        out_shape=out_shape,
        in_specs=specs or [vmem() for _ in args],
        out_specs=jax.tree.map(lambda _: vmem(), out_shape),
        scratch_shapes=list(scratch),
        compiler_params=pltpu.CompilerParams(vmem_limit_bytes=VMEM_LIMIT),
        cost_estimate=pl.CostEstimate(flops=flops, bytes_accessed=nbytes, transcendentals=0),
    )(*args)


def crossed(array, axis, bits):
    return lax.ppermute(array, axis, [(i, i ^ bits) for i in range(lax.axis_size(axis))])


STEPS = (0, 2, 1, 3)


def place(heads):
    index = lax.axis_index("ctx")
    member = lax.rem(index, heads)
    return index // heads, member // 2, lax.rem(member, 2)


def pack_heads(heads, queries_ref, keys_values_ref, starts_ref, *refs):
    *outs, held_ref, start_sem, sem = refs
    rows = queries_ref.shape[0]
    _, pair, _ = place(heads)
    first = pltpu.make_async_copy(starts_ref, held_ref, start_sem)
    first.start()
    copies = []
    for step, out in zip(STEPS, outs):
        for head in range(2):
            columns = pl.ds(pl.multiple_of(((pair ^ step) * 2 + head) * HD, HD), HD)
            first_row = head * 3 * rows
            for part, source in enumerate((queries_ref, keys_values_ref)):
                lines = pl.ds(first_row + part * rows, source.shape[0])
                copies.append(
                    pltpu.make_async_copy(
                        source.at[:, columns], out.at[lines], sem.at[step, 2 * head + part]
                    )
                )
    for copy in copies:
        copy.start()
    first.wait()
    starts = held_ref[...]
    high = (starts // DIGIT).astype(jnp.float32)
    low = (starts % DIGIT).astype(jnp.float32)
    line = lax.broadcasted_iota(jnp.int32, (NOTE_ROWS, rows), 0)
    note = jnp.where(line == 0, high, jnp.where(line == 1, low, 0.0)).astype(jnp.bfloat16)
    for out in outs:
        out[6 * rows :] = note
    for copy in copies:
        copy.wait()


def split(matrix):
    high = matrix.astype(jnp.bfloat16)
    low = (matrix - high.astype(jnp.float32)).astype(jnp.bfloat16)
    return jnp.concatenate([high, low], axis=1)


def pack_hyena(hyena_ref, filters_ref, product_ref, own_ref, far_ref, near_ref, taps_ref, sem):
    width = own_ref.shape[1]
    panel = lax.axis_index("tp")
    parity = lax.rem(lax.axis_index("ctx"), 2)
    copies = []
    for index, target in enumerate((panel, panel ^ (3 - parity), panel ^ 1)):
        columns = pl.ds(pl.multiple_of(target * width, width), width)
        copies.append(
            pltpu.make_async_copy(filters_ref.at[:, columns], taps_ref.at[index], sem.at[index])
        )
    for copy in copies:
        copy.start()
    product_ref[...] = (hyena_ref[1].astype(jnp.float32) * hyena_ref[2].astype(jnp.float32)).astype(
        jnp.bfloat16
    )
    for copy in copies:
        copy.wait()
    for index, out in enumerate((own_ref, far_ref, near_ref)):
        out[...] = taps_ref[index].astype(jnp.bfloat16)


def columns_of(ref, rows, index):
    return ref[rows, index * 2 * HD : (index + 1) * 2 * HD]


def sort_heads(heads, *refs):
    count = heads // 2
    near_ref, far_ref = refs[count : count + 2]
    query_ref, side_ref = refs[-2:]
    rows = (refs[0].shape[0] - NOTE_ROWS) // 6
    _, pair, _ = place(heads)
    for step, ref in zip(STEPS, refs):
        source = pair ^ step
        query_ref[source, rows:, :HD] = ref[6 * rows :]
        for head in range(2):
            columns = slice(head * HD, (head + 1) * HD)
            first = head * 3 * rows
            query_ref[source, :rows, columns] = ref[first : first + rows]
            for part in range(2):
                line = first + (part + 1) * rows
                side_ref[2 * source + part, :, columns] = ref[line : line + rows]
    height, width = far_ref.shape
    parts = width // (2 * HD)
    for part in range(parts):
        line = slice(part * height, (part + 1) * height)
        side_ref[heads, line] = columns_of(far_ref, slice(None), part)
        side_ref[heads + 1, line] = columns_of(near_ref, slice(None), part)


UNIT = 2


def key_set(ref, blocks, head, origin, parity, causal):
    columns = slice(head * HD, (head + 1) * HD)
    rows = ref.shape[1]
    key = jnp.concatenate([ref[2 * block, :, columns] for block in range(blocks)], axis=0)
    value = jnp.concatenate([ref[2 * block + 1, :, columns] for block in range(blocks)], axis=0)
    return key, value, [(2 * block + parity) * rows + origin for block in range(blocks)], causal


def masked_scores(sets, query, start, own, begin):
    held = [[] for _ in range(UNIT)]
    for key, _, firsts, causal in sets:
        scores = lax.dot_general(
            key, query, (((1,), (1,)), ((), ())), preferred_element_type=jnp.float32
        )
        rows = key.shape[0] // len(firsts)
        line = lax.broadcasted_iota(jnp.int32, (rows, rows), 0)
        for block, first in enumerate(firsts):
            for index in range(UNIT):
                if causal and block > begin + index:
                    held[index].append(None)
                    continue
                lanes = slice(index * rows, (index + 1) * rows)
                allowed = line >= start[:, lanes] - first
                if causal and block == begin + index:
                    allowed &= line <= own[:, lanes] - first
                part = scores[block * rows : (block + 1) * rows, lanes]
                held[index].append(jnp.where(allowed, part, MASKED))
    return held


def highest(held):
    tops = [functools.reduce(jnp.maximum, [x for x in parts if x is not None]) for parts in held]
    return jnp.concatenate([jnp.max(top, axis=0, keepdims=True) for top in tops], axis=1)


def weigh(held, top):
    totals, rounded = [], []
    for index, parts in enumerate(held):
        rows = next(x for x in parts if x is not None).shape[1]
        here = top[:, index * rows : (index + 1) * rows]
        weights = [None if x is None else jnp.exp2((x - here) * FACTOR) for x in parts]
        total = functools.reduce(jnp.add, [x for x in weights if x is not None])
        totals.append(jnp.sum(total, axis=0, keepdims=True))
        rounded.append(
            [
                jnp.zeros((rows, rows), jnp.bfloat16) if x is None else x.astype(jnp.bfloat16)
                for x in weights
            ]
        )
    lines = [jnp.concatenate(line, axis=1) for line in zip(*rounded)]
    return jnp.concatenate(totals, axis=1), jnp.concatenate(lines, axis=0)


def mix(sets, rounded):
    return dot(jnp.concatenate([one[1] for one in sets], axis=0).T, rounded)


def unit_rows(heads, query_ref, begin):
    rows = query_ref.shape[1] - NOTE_ROWS
    group, _, parity = place(heads)
    starts = []
    for block in range(begin, begin + UNIT):
        note = query_ref[block, rows:, :HD].astype(jnp.float32)
        starts.append(note[0:1] * float(DIGIT) + note[1:2])
    start = jnp.concatenate(starts, axis=1).astype(jnp.int32) - group * (heads * rows)
    line = lax.broadcasted_iota(jnp.int32, (1, UNIT * rows), 1)
    own = line // rows * rows + line + (2 * begin + parity) * rows
    return start, own


def unit_queries(query_ref, head, begin):
    rows = query_ref.shape[1] - NOTE_ROWS
    blocks = range(begin, begin + UNIT)
    columns = slice(head * HD, (head + 1) * HD)
    return jnp.concatenate([query_ref[block, :rows, columns] for block in blocks], axis=0)


FACTOR = math.log2(math.e) / math.sqrt(HD)


def attend_first(heads, query_ref, key_value_ref, top_ref, total_ref, mixed_ref):
    _, _, parity = place(heads)
    for unit in range(heads // 2 // UNIT):
        begin = unit * UNIT
        start, own = unit_rows(heads, query_ref, begin)
        sets = [[key_set(key_value_ref, begin + UNIT, head, 0, parity, True)] for head in range(2)]
        held = [
            masked_scores(sets[head], unit_queries(query_ref, head, begin), start, own, begin)
            for head in range(2)
        ]
        tops = [highest(each) for each in held]
        weights = [weigh(each, top) for each, top in zip(held, tops)]
        for head, (total, rounded) in enumerate(weights):
            top_ref[head, unit] = tops[head]
            total_ref[head, unit] = total
            mixed_ref[head, unit] = mix(sets[head], rounded)


def attend_second(heads, *refs):
    count = heads // 2
    query_ref, top_ref, total_ref, mixed_ref, other_ref, *more = refs[: -count - 1]
    outs, held_ref = refs[-count - 1 : -1], refs[-1]
    rows = query_ref.shape[1] - NOTE_ROWS
    _, pair, parity = place(heads)

    def one_unit(unit):
        begin = unit * UNIT
        start, own = unit_rows(heads, query_ref, begin)
        sets, held, tops = [], [], []
        for head in range(2):
            sets.append([key_set(other_ref, begin + UNIT, head, 0, 1 - parity, True)])
            for ref, side in zip(more, (parity, 1 - parity)):
                sets[head].append(key_set(ref, count, head, -heads * rows, side, False))
            query = unit_queries(query_ref, head, begin)
            held.append(masked_scores(sets[head], query, start, own, begin))
        for head in range(2):
            tops.append(jnp.maximum(top_ref[head, unit], highest(held[head])))
        weights = [weigh(each, top) for each, top in zip(held, tops)]
        notes = jnp.zeros((NOTE_ROWS, UNIT * rows), jnp.float32)
        for head, (total, rounded) in enumerate(weights):
            top = tops[head]
            scale = jnp.exp2((top_ref[head, unit] - top) * FACTOR)
            total = total_ref[head, unit] * scale + total
            mixed = mixed_ref[head, unit] * scale + mix(sets[head], rounded)
            mixed = (mixed * (1.0 / total)).astype(jnp.bfloat16).T
            logs = top * (1.0 / math.sqrt(HD)) + jnp.log(total)
            high = logs.astype(jnp.bfloat16).astype(jnp.float32)
            middle = (logs - high).astype(jnp.bfloat16).astype(jnp.float32)
            low = logs - high - middle
            line = lax.broadcasted_iota(jnp.int32, (NOTE_ROWS, UNIT * rows), 0) - 3 * head
            for index, part in enumerate((high, middle, low)):
                notes = jnp.where(line == index, part, notes)
            for index in range(UNIT):
                held_ref[begin + index, head * rows : (head + 1) * rows] = mixed[
                    index * rows : (index + 1) * rows
                ]
        for index in range(UNIT):
            held_ref[begin + index, 2 * rows :] = notes[:, index * rows : (index + 1) * rows].astype(
                jnp.bfloat16
            )

    for unit in range(count // UNIT):
        one_unit(unit)
    for step, out in enumerate(outs):
        out[...] = held_ref[pair ^ step]


def unpack_heads(heads, steps, *refs):
    *sources, out_ref, logs_ref = refs
    rows = out_ref.shape[0]
    _, pair, _ = place(heads)
    for step, source in zip(steps, sources):
        owner = pair ^ step
        note = source[2 * rows :].astype(jnp.float32)
        for head in range(2):
            columns = pl.ds(pl.multiple_of((owner * 2 + head) * HD, HD), HD)
            out_ref[:, columns] = source[head * rows : (head + 1) * rows]
            parts = [note[3 * head + index : 3 * head + index + 1] for index in range(3)]
            logs_ref[pl.ds(owner * 2 + head, 1), :] = parts[0] + parts[1] + parts[2]


def dot(left, right):
    return jnp.dot(left, right, preferred_element_type=jnp.float32)


def twice(array):
    return jnp.concatenate([array, array], axis=0)


def document_starts(starts_ref, rows):
    return jnp.maximum(starts_ref[...] - lax.axis_index("ctx") * rows, -rows)


def filtered(spectrum, filter_ref, back_ref):
    half = spectrum.shape[0] // 2
    even, odd = spectrum[:half], spectrum[half:]
    tap_even, tap_odd = filter_ref[:half], filter_ref[half:]
    real = (even * tap_even - odd * tap_odd).astype(jnp.bfloat16)
    imag = (even * tap_odd + odd * tap_even).astype(jnp.bfloat16)
    return dot(back_ref[...], jnp.concatenate([real, imag], axis=0))


def convolve(
    heads, other_ref, mine_ref, before_ref, own_taps_ref, starts_ref, product_ref, gate_ref, skip_ref,
    ahead_ref, wide_back_ref, out_ref, taps_ref, filter_ref, sum_ref, early_ref, late_ref, back_ref,
):
    rows = product_ref.shape[0]
    early_ref[...] = split(ahead_ref[:, :rows])
    late_ref[...] = split(ahead_ref[:, rows:])
    back_ref[...] = wide_back_ref[...].astype(jnp.bfloat16)
    height, width = own_taps_ref.shape
    panel = lax.axis_index("tp")
    even = lax.rem(lax.axis_index("ctx"), 2) == 0
    everything = slice(None)

    def store(step, part, value):
        line = pl.ds(pl.multiple_of((panel ^ step) * height, height), height)
        taps_ref[line, part * 2 * HD : (part + 1) * 2 * HD] = value

    parts = width // (2 * HD)
    for part in range(parts):
        line = slice(part * height, (part + 1) * height)
        mine_far, other_far = mine_ref[heads, line], other_ref[heads, line]
        store(0, part, columns_of(own_taps_ref, everything, part))
        store(1, part, jnp.where(even, other_ref[heads + 1, line], mine_ref[heads + 1, line]))
        store(2, part, jnp.where(even, other_far, mine_far))
        store(3, part, jnp.where(even, mine_far, other_far))
    filter_ref[...] = dot(early_ref[...], twice(taps_ref[...]))
    starts = document_starts(starts_ref, rows)
    line = lax.broadcasted_iota(jnp.int32, (rows, 1), 0)
    zero = jnp.zeros((), jnp.bfloat16)

    begin = jnp.min(starts)
    past = jnp.where(line - rows >= begin, before_ref[...], zero)
    here = jnp.where(line >= begin, product_ref[...], zero)
    spectrum = dot(early_ref[...], twice(past)) + dot(late_ref[...], twice(here))
    sum_ref[...] = filtered(spectrum, filter_ref, back_ref)

    def one_document(begin):
        here = jnp.where(line >= begin, product_ref[...], zero)
        result = filtered(dot(late_ref[...], twice(here)), filter_ref, back_ref)
        sum_ref[...] = jnp.where(line >= begin, result, sum_ref[...])
        return jnp.min(jnp.where(starts > begin, starts, rows))

    second = jnp.min(jnp.where(starts > begin, starts, rows))
    lax.while_loop(lambda begin: begin < rows, one_document, second)
    out_ref[...] = (
        gate_ref[0].astype(jnp.float32)
        * (skip_ref[...] * product_ref[...].astype(jnp.float32) + sum_ref[...])
    ).astype(jnp.bfloat16)


def twiddles(rows):
    window = 2 * rows
    order = np.arange(rows)[:, None] * 2 + 1
    angle = np.pi * ((order * np.arange(window)[None, :]) % (2 * window)) / window
    ahead = np.concatenate([np.cos(angle), -np.sin(angle)], axis=0)
    back = ahead.T[rows:] / rows
    return jnp.asarray(ahead, jnp.float32), jnp.asarray(back, jnp.float32)


def taps_pairs(peers, panels):
    assert panels == 4
    near, far = [], []
    for peer in range(peers):
        for panel in range(panels):
            here = peer * panels + panel
            far.append((here, peer * panels + (panel ^ (3 - peer % 2))))
            if peer % 2 == 1:
                near.append((here, peer * panels + (panel ^ 1)))
    return near, far


def local(hyena_inputs, filters, skip_bias, queries, keys_values, doc_start):
    rows = queries.shape[0]
    channels = hyena_inputs.shape[2]
    heads = queries.shape[1] // HD
    count = heads // 2
    peers = lax.axis_size("ctx")
    bf16, f32 = jnp.bfloat16, jnp.float32
    shape = jax.ShapeDtypeStruct
    starts = doc_start.reshape(1, rows)

    height = filters.shape[0]

    def pinned(*arrays):
        return [pltpu.with_memory_space_constraint(x, pltpu.HBM) for x in arrays]

    *packed, near_starts = call(
        functools.partial(pack_heads, heads),
        (shape((6 * rows + NOTE_ROWS, HD), bf16),) * count + (shape((1, rows), jnp.int32),),
        pinned(queries, keys_values.reshape(2 * rows, heads * HD), starts),
        0,
        4 * queries.size * 3,
        scratch=(pltpu.SemaphoreType.DMA, pltpu.SemaphoreType.DMA((count, 4))),
        specs=[hbm()] * 3,
    )
    assert count == len(STEPS)
    arrived = [packed[0]] + [crossed(packed[i], "ctx", 2 * STEPS[i]) for i in range(1, count)]
    product, own_taps, far_taps, near_taps = call(
        pack_hyena,
        (shape((rows, channels), bf16),) + (shape((height, channels), bf16),) * 3,
        (hyena_inputs, *pinned(filters)),
        0,
        4 * queries.size * 3,
        scratch=(pltpu.VMEM((3, height, channels), f32), pltpu.SemaphoreType.DMA((3,))),
        specs=[vmem(), hbm()],
    )
    axes = ("ctx", "tp")
    near_pairs, far_pairs = taps_pairs(peers, lax.axis_size("tp"))
    near_taps = lax.ppermute(near_taps, axes, near_pairs)
    far_taps = lax.ppermute(far_taps, axes, far_pairs)
    before = lax.ppermute(product, "ctx", [(i, i + 1) for i in range(peers - 1)])
    query, key_value = call(
        functools.partial(sort_heads, heads),
        (
            shape((count, rows + NOTE_ROWS, 2 * HD), bf16),
            shape((heads + 2, rows, 2 * HD), bf16),
        ),
        (*arrived, near_taps, far_taps),
        0,
        4 * queries.size * 3,
    )
    other = crossed(key_value, "ctx", 1)
    units = count // UNIT
    partial = call(
        functools.partial(attend_first, heads),
        (
            shape((2, units, 1, UNIT * rows), f32),
            shape((2, units, 1, UNIT * rows), f32),
            shape((2, units, HD, UNIT * rows), f32),
        ),
        (query, key_value),
        LONG * (heads * rows) ** 2 * HD,
        4 * queries.size * 4,
    )
    operands = [query, *partial, other]
    if peers > heads:
        pairs = [(i, i + heads) for i in range(peers - heads)]
        operands += [lax.ppermute(each, "ctx", pairs) for each in (key_value, other)]
    assert count == 2 * UNIT
    message = shape((2 * rows + NOTE_ROWS, HD), bf16)

    mixed = call(
        functools.partial(attend_second, heads),
        (message,) * count,
        operands,
        2 * (heads * rows) ** 2 * HD,
        4 * queries.size * 4,
        scratch=(pltpu.VMEM((count, 2 * rows + NOTE_ROWS, HD), bf16),),
    )
    returned = [mixed[0]] + [crossed(mixed[step], "ctx", 2 * step) for step in (3, 1, 2)]
    hyena_out = call(
        functools.partial(convolve, heads),
        shape((rows, channels), bf16),
        (
            other, key_value, before, own_taps, near_starts, product, hyena_inputs,
            skip_bias.reshape(1, channels), *twiddles(rows),
        ),
        2 * 4 * 256 * 256 * channels,
        4 * queries.size * 4,
        scratch=(
            pltpu.VMEM((FLEN, channels), bf16),
            pltpu.VMEM((2 * rows, channels), f32),
            pltpu.VMEM((rows, channels), f32),
            pltpu.VMEM((2 * rows, 2 * rows), bf16),
            pltpu.VMEM((2 * rows, 2 * rows), bf16),
            pltpu.VMEM((rows, 2 * rows), bf16),
        ),
    )
    attention_out, log_totals = call(
        functools.partial(unpack_heads, heads, (0, 3, 1, 2)),
        (shape((rows, heads * HD), bf16), shape((heads, rows), f32)),
        returned,
        0,
        4 * queries.size,
    )
    return (hyena_out, attention_out, log_totals)


def solution(mesh):
    in_specs = (
        P(None, "ctx", "tp"),
        P("tp", None),
        P("tp"),
        P("ctx", "tp"),
        P(None, "ctx", "tp"),
        P("ctx"),
    )
    out_specs = (P("ctx", "tp"), P("ctx", "tp"), P("tp", "ctx"))
    return jax.shard_map(local, mesh=mesh, in_specs=in_specs, out_specs=out_specs, check_vma=False)
```
